128 devices in a mesh: psg: 8 (over y_lo, x), head: 16 (over y_hi, z, core).
Axes of the slice: x: 4, y: 4 (y_hi: 2, y_lo: 2; y = y_hi * 2 + y_lo), z: 4, core: 2. Of those that a mesh axis runs over, the one named last changes fastest.
Arguments:
- queries: bfloat16 [256, 4096], P(None, 'head'), may hold values from -16 to 16
- memory: bfloat16 [8192, 4096], P('psg', 'head'), may hold values from -6 to 6
- lengths: int32 [32], P('psg'), may hold values from 32 to 256
- owner: int32 [32], P('psg'), may hold values from 0 to 1, as said below
- w_key: bfloat16 [4096, 4096], P(None, 'head'), may hold values from -0.09375 to 0.09375
- w_value: bfloat16 [4096, 4096], P(None, 'head'), may hold values from -0.09375 to 0.09375
- grad_context: bfloat16 [256, 4096], P(None, 'head'), may hold values from -6 to 6
Outputs:
- grad_queries: bfloat16 [256, 4096], P(None, 'head')
- grad_memory: bfloat16 [8192, 4096], P('psg', 'head')
- grad_wk: float32 [4096, 4096], P('psg', 'head')
- grad_wv: float32 [4096, 4096], P('psg', 'head')
The draws below stay inside these ranges and needn't reach their ends.
Inputs may be any that keep to these rules, and one draw needn't show every extreme that they name: `owner`: each question owns exactly 16 passages.
All inputs are finite; a program needn't handle non-finite values.
Results may differ from the reference program's by a relative error of at most 0.022.
The reference program's roundings to bfloat16 on the way count: a program that leaves them out, or rounds other values in their place, can miss the bound.
Values may be sent and summed in bfloat16 or wider, within the bound.
A program may use at most 128 MiB of HBM per device.

```python
import jax
import jax.numpy as jnp
from jax import lax

D = 4096
HEADS = 64
HEAD_DIM = 64
LEN = 256
TQ = 128
QUESTIONS = 2
INNER = 4096
PASSAGES = 32
N_HEAD = 16


def draw_owner(key, part):
    key = jax.random.fold_in(key, 11)
    order = jax.random.permutation(key, jnp.arange(PASSAGES, dtype=jnp.int32))
    return (order % QUESTIONS).astype(jnp.int32)


def draw_queries(key, part):
    key = jax.random.fold_in(key, 23)
    first = jax.random.fold_in(key, 0)
    base = jnp.clip(jax.random.normal(first, (QUESTIONS * TQ, INNER), jnp.float32), -8.0, 8.0)
    return (0.25 * base).astype(jnp.bfloat16)


def place_ends(drawn, rng, least, high):
    extent = drawn.shape
    spot = [jax.random.randint(jax.random.fold_in(rng, axis), (), 0, extent[axis]) for axis in range(len(extent))]
    drawn = drawn.at[tuple(spot)].set(least)
    longest = extent.index(max(extent))
    spot[longest] = (spot[longest] + 1) % extent[longest]
    return drawn.at[tuple(spot)].set(high)


def level_of(own_key, extent, cuts, least, largest):
    def one(dim, shards_of):
        heights = jax.random.uniform(jax.random.fold_in(jax.random.fold_in(own_key, 6), dim), (shards_of,), jnp.float32, least / len(cuts), largest / len(cuts))
        return jnp.repeat(jnp.exp(heights), extent[dim] // shards_of).reshape((-1,) + (1,) * (len(extent) - dim - 1))

    factor_of = one(*cuts[0])
    for cut in cuts[1:]:
        factor_of = factor_of * one(*cut)
    return factor_of


def gaussian(own_key, dims, width, reach, shards=(), held_as=jnp.bfloat16):
    result = width * jax.random.normal(own_key, dims, jnp.float32)
    if shards:
        result = result * level_of(own_key, dims, shards, -0.22, 0.18)
    return jnp.clip(result, -reach, reach).astype(held_as)


def setup_inputs(seed: int = 0) -> dict:
    key_list = jax.random.split(jax.random.key(seed), 8)
    return {
        "queries": draw_queries(jax.random.fold_in(key_list[7], 71), 0),
        "memory": gaussian(key_list[1], (PASSAGES * LEN, D), 1.0, 6.0, ((0, 8), (1, 16))),
        "lengths": place_ends(jax.random.randint(key_list[2], (PASSAGES,), LEN // 8, LEN + 1), jax.random.fold_in(key_list[2], 1), LEN // 8, LEN).astype(jnp.int32),
        "owner": draw_owner(jax.random.fold_in(key_list[7], 71), 0),
        "w_key": gaussian(key_list[4], (D, INNER), D ** -0.5, 0.09375, ((1, 16),)),
        "w_value": gaussian(key_list[5], (D, INNER), D ** -0.5, 0.09375, ((1, 16),)),
        "grad_context": gaussian(key_list[6], (QUESTIONS * TQ, INNER), 1.0, 6.0, ((1, 16),)),
    }


negative_fill = -1e30


def reference(queries, memory, lengths, owner, w_key, w_value, grad_context):
    keys = jnp.dot(memory, w_key, preferred_element_type=jnp.float32).astype(jnp.bfloat16)
    values = jnp.dot(memory, w_value, preferred_element_type=jnp.float32).astype(jnp.bfloat16)
    row_count = PASSAGES * LEN
    key_grid = keys.astype(jnp.float32).reshape(row_count, HEADS, HEAD_DIM)
    value_grid = values.astype(jnp.float32).reshape(row_count, HEADS, HEAD_DIM)
    index = jnp.arange(row_count, dtype=jnp.int32)
    passage = index // LEN
    position = index % LEN
    alive = position < lengths[passage]
    query_grid = queries.astype(jnp.float32).reshape(QUESTIONS, TQ, HEADS, HEAD_DIM)
    context_grid = grad_context.astype(jnp.float32).reshape(QUESTIONS, TQ, HEADS, HEAD_DIM)
    key_total = jnp.zeros((row_count, HEADS, HEAD_DIM), jnp.float32)
    value_total = jnp.zeros((row_count, HEADS, HEAD_DIM), jnp.float32)
    query_parts = []
    for question in range(QUESTIONS):
        usable = alive & (owner[passage] == question)
        scores = jnp.einsum("thd,jhd->htj", query_grid[question], key_grid)
        masked = jnp.where(usable[None, None, :], scores, negative_fill)
        top_score = jnp.max(masked, axis=-1)
        shifted = jnp.where(usable[None, None, :], jnp.exp(masked - top_score[..., None]), 0.0)
        softmax_mass = jnp.sum(shifted, axis=-1)
        grad_probs = jnp.einsum("thd,jhd->htj", context_grid[question], value_grid)
        row_shift = jnp.sum(shifted * grad_probs, axis=-1) / softmax_mass
        probs = shifted / softmax_mass[..., None]
        probs_bf = lax.optimization_barrier(probs.astype(jnp.bfloat16)).astype(jnp.float32)
        grad_scores = lax.optimization_barrier((probs * (grad_probs - row_shift[..., None])).astype(jnp.bfloat16)).astype(jnp.float32)
        query_parts.append(jnp.einsum("htj,jhd->thd", grad_scores, key_grid))
        key_total = key_total + jnp.einsum("htj,thd->jhd", grad_scores, query_grid[question])
        value_total = value_total + jnp.einsum("htj,thd->jhd", probs_bf, context_grid[question])
    grad_queries = jnp.stack(query_parts).reshape(QUESTIONS * TQ, INNER).astype(jnp.bfloat16)
    grad_keys = key_total.reshape(row_count, INNER).astype(jnp.bfloat16)
    grad_values = value_total.reshape(row_count, INNER).astype(jnp.bfloat16)
    grad_wk = jnp.dot(memory.T, grad_keys, preferred_element_type=jnp.float32)
    grad_wv = jnp.dot(memory.T, grad_values, preferred_element_type=jnp.float32)
    group_width = INNER // N_HEAD
    memory_total = jnp.zeros((row_count, D), jnp.float32)
    for group in range(N_HEAD):
        low = group * group_width
        high = low + group_width
        part_sum = jnp.dot(grad_keys[:, low:high], w_key[:, low:high].T, preferred_element_type=jnp.float32) + jnp.dot(grad_values[:, low:high], w_value[:, low:high].T, preferred_element_type=jnp.float32)
        memory_total = memory_total + lax.optimization_barrier(part_sum.astype(jnp.bfloat16)).astype(jnp.float32)
    grad_memory = memory_total.astype(jnp.bfloat16)
    return (grad_queries, grad_memory, grad_wk, grad_wv)
```

```python
import jax
import jax.numpy as jnp
from jax import lax
from jax.experimental import pallas as pl
from jax.experimental.pallas import tpu as pltpu
from jax.sharding import PartitionSpec as P

HEAD_DIM = 64
LEN = 256
TQ = 128
HEADS_HERE = 4
PASSAGES_HERE = 4
B = 256
PAIRS = HEADS_HERE * TQ
MESH = pl.DeviceIdType.MESH
FILL = -1e30
F32 = jnp.float32
BF16 = jnp.bfloat16

PLACES = ((0, 0), (0, 1), (0, 3), (1, 0), (0, 2), (1, 2), (1, 1), (1, 3))
SLOT = {place: slot for slot, place in enumerate(PLACES)}


def is_equal(a, k):
    return 1 - ((a - k) * (a - k) + 48) // 49


def slot_of(dy, dz):
    code = dy * 4 + dz
    total = 0
    for (py, pz), slot in SLOT.items():
        total = total + slot * is_equal(code, py * 4 + pz)
    return total


def nt(a, b):
    return lax.dot_general(a, b, (((1,), (1,)), ((), ())), preferred_element_type=F32)


def nn(a, b):
    return jnp.dot(a, b, preferred_element_type=F32)


class Scatter:
    def __init__(self, send, recv, ysend, yrecv, ssem, rsem, yssem, yrsem, following, before, partner):
        self.send, self.recv, self.ysend, self.yrecv = send, recv, ysend, yrecv
        self.ssem, self.rsem, self.yssem, self.yrsem = ssem, rsem, yssem, yrsem
        self.following, self.before, self.partner = following, before, partner

    def half(self, ref, index, way):
        return ref.at[index, pl.ds(way * B, B)]

    def copy(self, index, way):
        return pltpu.make_async_remote_copy(
            src_ref=self.half(self.send, index, way),
            dst_ref=self.half(self.recv, index, way),
            send_sem=self.ssem.at[index, way],
            recv_sem=self.rsem.at[index, way],
            device_id=self.before if way else self.following,
            device_id_type=MESH,
        )

    def ycopy(self, u):
        return pltpu.make_async_remote_copy(
            src_ref=self.ysend.at[u],
            dst_ref=self.yrecv.at[u],
            send_sem=self.yssem.at[u],
            recv_sem=self.yrsem.at[u],
            device_id=self.partner,
            device_id_type=MESH,
        )

    def arrived(self, index, way):
        return self.recv[index, way * B : (way + 1) * B, :].astype(F32)

    def item(self, kind, dy, u, own, store):
        first = (dy * 2 + u) * 3
        if kind == "D":
            for way in (0, 1):
                self.copy(first + 1, way).wait_recv()
                self.copy(first + 2, way).wait_recv()
            if dy == 0:
                self.ycopy(u).wait_recv()
            for way in (0, 1):
                value = own(0, way * 2 + u, way)
                value = value + self.arrived(first + 2, way) + self.arrived(first + 1, 1 - way)
                if dy == 1:
                    self.ysend[u, way * B : (way + 1) * B, :] = value.astype(BF16)
                else:
                    value = value + self.yrecv[u, way * B : (way + 1) * B, :].astype(F32)
                    store(way * 2 + u, value)
            if dy == 1:
                self.ycopy(u).start()
            return
        index = first + "ABC".index(kind)
        for way in (0, 1):
            dz, r = chunk_of(kind, u, way)
            if kind == "C":
                self.copy(first, way).wait_recv()
            value = own(dz, r, way)
            if kind == "C":
                value = value + self.arrived(first, way)
            self.send[index, way * B : (way + 1) * B, :] = value.astype(BF16)
            self.copy(index, way).start()

    def finish(self):
        for index in range(12):
            for way in (0, 1):
                self.copy(index, way).wait_send()
        for u in (0, 1):
            self.ycopy(u).wait_send()


def chunk_of(kind, u, way):
    if kind == "A":
        return 2, way * 2 + u
    if kind == "B":
        return (3, u) if way else (1, 2 + u)
    if kind == "C":
        return (3, 2 + u) if way else (1, u)
    return 0, way * 2 + u


ITEMS = (
    ("A", 1, 0), ("B", 1, 0), ("A", 1, 1), ("C", 1, 0), ("B", 1, 1), ("C", 1, 1),
    ("A", 0, 0), ("B", 0, 0), ("D", 1, 0), ("A", 0, 1), ("C", 0, 0), ("D", 1, 1),
    ("B", 0, 1), ("C", 0, 1), ("D", 0, 0), ("D", 0, 1),
)


def kernel(
    len_ref, own_ref, q_ref, c_ref, mem_ref, wk_ref, wv_ref,
    gq_out, gm_out, gwk_out, gwv_out,
    fm, w, qa, ca, qat, cat, acc, kt, e_ref, gp_ref, stat, sl, sall, g, gt, gs,
    sib_send, sib_recv, m_send, m_recv, my_send, my_recv, w_send, w_recv, wy_send, wy_recv,
    gq_acc, gq_recv, gq_own, gq_full,
    mem_sem, w_sem, ag_ssem, ag_rsem, st_ssem, st_rsem, sib_ssem, sib_rsem,
    m_ssem, m_rsem, my_ssem, my_rsem, w_ssem, w_rsem, wy_ssem, wy_rsem,
    q1_ssem, q1_rsem, q2_ssem, q2_rsem,
):
    p, h = lax.axis_index("psg"), lax.axis_index("head")
    yl, x = p // 4, p % 4
    yh, z, core = h // 8, (h // 2) % 4, h % 2

    def head_at(dy, dz, dc=0):
        return ((yh + dy) % 2) * 8 + ((z + dz) % 4) * 2 + (core + dc) % 2

    def psg_at(dy, dx):
        return ((yl + dy) % 2) * 4 + (x + dx) % 4

    def on_head(dy, dz, dc=0):
        return (p, head_at(dy, dz, dc))

    def on_psg(dy, dx):
        return (psg_at(dy, dx), h)

    up, down, across, sibling = on_head(0, 1), on_head(0, 3), on_head(1, 0), on_head(0, 0, 1)
    peers = [(k // 4, k % 4) for k in range(1, 8)]

    mem_copy = pltpu.make_async_copy(mem_ref, fm.at[:, pl.ds(0, B)], mem_sem)
    mem_copy.start()
    w_copies = []
    for slot, (dy, dz) in enumerate(PLACES):
        for dc in (0, 1):
            rows = pl.ds(pl.multiple_of(head_at(dy, dz, dc) * B, B), B)
            into = pl.ds((slot * 2 + dc) * B, B)
            for part, ref in enumerate((wk_ref, wv_ref)):
                w_copies.append(
                    pltpu.make_async_copy(
                        ref.at[rows, :],
                        w.at[into, pl.ds(part * B, B)],
                        w_sem.at[(slot * 2 + dc) * 2 + part],
                    )
                )
                w_copies[-1].start()

    barrier = pltpu.get_barrier_semaphore()
    partners = [up, down, across, sibling] + [on_psg(*peer) for peer in peers]
    for device in partners:
        pl.semaphore_signal(barrier, inc=1, device_id=device, device_id_type=MESH)
    pl.semaphore_wait(barrier, len(partners))
    mem_copy.wait()

    def block(slot, dc, r):
        return fm.at[pl.ds(r * B, B), pl.ds((slot * 2 + dc) * B, B)]

    def gather_copy(source, target, r, number, device):
        return pltpu.make_async_remote_copy(
            src_ref=block(source[0], source[1], r),
            dst_ref=block(target[0], target[1], r),
            send_sem=ag_ssem.at[number, r],
            recv_sem=ag_rsem.at[target[0] * 2 + target[1], r],
            device_id=device,
            device_id_type=MESH,
        )

    def gathered(slot, dc, r):
        gather_copy((slot, dc), (slot, dc), r, 0, sibling).wait_recv()

    def to_sibling(slot, r):
        gather_copy((slot, 0), (slot, 1), r, 4 + slot, sibling).start()

    for r in range(PASSAGES_HERE):
        gather_copy((0, 0), (SLOT[0, 3], 0), r, 0, up).start()
        gather_copy((0, 0), (SLOT[0, 1], 0), r, 1, down).start()
        gather_copy((0, 0), (SLOT[1, 0], 0), r, 2, across).start()
        to_sibling(0, r)

    lane = lax.broadcasted_iota(jnp.int32, (TQ, B), 1) // HEAD_DIM
    row = lax.broadcasted_iota(jnp.int32, (B, TQ), 0) // HEAD_DIM
    for source, plain, turned in ((q_ref, qa, qat), (c_ref, ca, cat)):
        for question in range(2):
            mine = source[question * TQ : (question + 1) * TQ, :].astype(F32)
            mine_t = mine.T
            for head in range(HEADS_HERE):
                at = slice(head * TQ, (head + 1) * TQ)
                plain[question, at, :] = jnp.where(lane == head, mine, 0.0).astype(BF16)
                turned[question, :, at] = jnp.where(row == head, mine_t, 0.0).astype(BF16)

    for copy in w_copies[:16]:
        copy.wait()

    def rows_of(r):
        return pl.ds(pl.multiple_of(r * B, B), B)

    def first_part(r, carry):
        gathered(SLOT[0, 3], 0, r)

        @pl.when(r < 2)
        def _():
            gather_copy((SLOT[0, 3], 0), (SLOT[0, 2], 0), r, 3, up).start()

        to_sibling(SLOT[0, 3], r)
        gathered(SLOT[0, 1], 0, r)

        @pl.when(r >= 2)
        def _():
            gather_copy((SLOT[0, 1], 0), (SLOT[0, 2], 0), r, 3, down).start()

        to_sibling(SLOT[0, 1], r)
        gathered(SLOT[1, 0], 0, r)
        gather_copy((SLOT[1, 0], 0), (SLOT[1, 3], 0), r, 12, up).start()
        gather_copy((SLOT[1, 0], 0), (SLOT[1, 1], 0), r, 13, down).start()
        to_sibling(SLOT[1, 0], r)
        for slot in range(4):
            gathered(slot, 1, r)
        acc[rows_of(r), :] = nn(fm[rows_of(r), 0 : 8 * B], w[0 : 8 * B, :])
        return carry

    lax.fori_loop(0, PASSAGES_HERE, first_part, 0)

    for r in (0, 2, 1, 3):
        gathered(SLOT[0, 2], 0, r)
        gather_copy((SLOT[0, 2], 0), (SLOT[1, 2], 0), r, 14, across).start()
        to_sibling(SLOT[0, 2], r)

    for copy in w_copies[16:]:
        copy.wait()

    def second_part(r, carry):
        gathered(SLOT[1, 2], 0, r)
        to_sibling(SLOT[1, 2], r)
        gathered(SLOT[0, 2], 1, r)
        gathered(SLOT[1, 2], 1, r)
        acc[rows_of(r), :] += nn(fm[rows_of(r), 8 * B : 12 * B], w[8 * B : 12 * B, :])
        for slot in (SLOT[1, 1], SLOT[1, 3]):
            gathered(slot, 0, r)
            to_sibling(slot, r)
        for slot in (SLOT[1, 1], SLOT[1, 3]):
            gathered(slot, 1, r)
        both = acc[rows_of(r), :] + nn(fm[rows_of(r), 12 * B :], w[12 * B :, :])
        keys, values = both[:, :B], both[:, B:].astype(BF16)
        kt[r] = keys.T.astype(BF16)
        keys = keys.astype(BF16)
        question = own_ref[r]
        scores = nt(keys, qa[question])
        flows = nt(values, ca[question])
        alive = lax.broadcasted_iota(jnp.int32, (LEN, PAIRS), 0) < len_ref[r]
        masked = jnp.where(alive, scores, FILL)
        top = jnp.max(masked, axis=0, keepdims=True)
        shifted = jnp.where(alive, jnp.exp(masked - top), 0.0)
        e_ref[r] = shifted
        gp_ref[r] = flows
        stat[r, 0:1, :] = top
        stat[r, 1:2, :] = jnp.sum(shifted, axis=0, keepdims=True)
        stat[r, 2:3, :] = jnp.sum(shifted * flows, axis=0, keepdims=True)
        return carry

    lax.fori_loop(0, PASSAGES_HERE, second_part, 0)

    picks = []
    for r in range(PASSAGES_HERE):
        second = own_ref[r].astype(F32)
        picks.append((1.0 - second, second))
    for question in range(2):
        tops = [
            stat[r, 0:1, :] * picks[r][question] + FILL * (1.0 - picks[r][question])
            for r in range(PASSAGES_HERE)
        ]
        top = jnp.maximum(jnp.maximum(tops[0], tops[1]), jnp.maximum(tops[2], tops[3]))
        mass = jnp.zeros((1, PAIRS), F32)
        flow = jnp.zeros((1, PAIRS), F32)
        for r in range(PASSAGES_HERE):
            scale = jnp.exp(tops[r] - top) * picks[r][question]
            mass += stat[r, 1:2, :] * scale
            flow += stat[r, 2:3, :] * scale
        sl[question : question + 1, :] = top
        sl[2 + question : 3 + question, :] = mass
        sl[4 + question : 5 + question, :] = flow
    sl[6:8, :] = jnp.zeros((2, PAIRS), F32)

    def seen_by(dy, dx):
        return dy * 4 + (4 - dx) % 4

    def stat_copy(dy, dx):
        there = seen_by(dy, dx)
        return pltpu.make_async_remote_copy(
            src_ref=sl,
            dst_ref=sall.at[there],
            send_sem=st_ssem.at[dy * 4 + dx],
            recv_sem=st_rsem.at[there],
            device_id=on_psg(dy, dx),
            device_id_type=MESH,
        )

    for peer in peers:
        stat_copy(*peer).start()
    for peer in peers:
        stat_copy(*peer).wait_recv()
    sall[0] = sl[...]
    totals = []
    for question in range(2):
        tops = [sall[k, question : question + 1, :] for k in range(8)]
        top = tops[0]
        for other in tops[1:]:
            top = jnp.maximum(top, other)
        mass = jnp.zeros((1, PAIRS), F32)
        flow = jnp.zeros((1, PAIRS), F32)
        for k in range(8):
            scale = jnp.exp(tops[k] - top)
            mass += sall[k, 2 + question : 3 + question, :] * scale
            flow += sall[k, 4 + question : 5 + question, :] * scale
        totals.append((top, 1.0 / mass, flow / mass))
    for r in range(PASSAGES_HERE):
        top, inverse, shift = (
            totals[0][k] * picks[r][0] + totals[1][k] * picks[r][1] for k in range(3)
        )
        stat[r, 3:4, :] = jnp.exp(stat[r, 0:1, :] - top) * inverse
        stat[r, 4:5, :] = shift

    def gradients(r, carry):
        question = own_ref[r]
        probs = e_ref[r] * stat[r, 3:4, :]
        grad = (probs * (gp_ref[r] - stat[r, 4:5, :])).astype(BF16)
        probs = probs.astype(BF16)
        gs[r] = grad
        g[rows_of(r), 0:B] = nn(grad, qa[question]).astype(BF16)
        g[rows_of(r), B : 2 * B] = nn(probs, ca[question]).astype(BF16)
        gt[0:B, rows_of(r)] = nt(qat[question], grad).astype(BF16)
        gt[B : 2 * B, rows_of(r)] = nt(cat[question], probs).astype(BF16)
        return carry

    lax.fori_loop(0, PASSAGES_HERE, gradients, 0)

    over_head = Scatter(
        m_send, m_recv, my_send, my_recv, m_ssem, m_rsem, my_ssem, my_rsem, up, down, across
    )
    over_psg = Scatter(
        w_send, w_recv, wy_send, wy_recv, w_ssem, w_rsem, wy_ssem, wy_rsem,
        on_psg(0, 1), on_psg(0, 3), on_psg(1, 0),
    )

    def part(slot, dc, r):
        at = (slot * 2 + dc) * B
        return nt(g[r * B : (r + 1) * B, :], w[at : at + B, :]).astype(BF16)

    def sibling_copy(number):
        return pltpu.make_async_remote_copy(
            src_ref=sib_send.at[number],
            dst_ref=sib_recv.at[number],
            send_sem=sib_ssem.at[number],
            recv_sem=sib_rsem.at[number],
            device_id=sibling,
            device_id_type=MESH,
        )

    def sibling_item(number):
        kind, dy, u = ITEMS[number]
        for way in (0, 1):
            dz, r = chunk_of(kind, u, way)
            sib_send[number, way * B : (way + 1) * B, :] = part(SLOT[dy, dz], 1, r)
        sibling_copy(number).start()

    def head_item(number):
        kind, dy, u = ITEMS[number]
        sibling_copy(number).wait_recv()

        def own(dz, r, way):
            other = sib_recv[number, way * B : (way + 1) * B, :].astype(F32)
            return part(SLOT[dy, dz], 0, r).astype(F32) + other

        def store(r, value):
            gm_out[r * B : (r + 1) * B, :] = value.astype(BF16)

        over_head.item(kind, dy, u, own, store)

    def psg_item(number):
        kind, dy, u = ITEMS[number]

        def own(dx, r, way):
            kv, half = r // 2, r % 2
            slot = slot_of((yl + dy + 2 - yh) % 2, (x + dx + 4 - z) % 4)
            column = (slot * 2 + (half + 2 - core) % 2) * B
            return nn(gt[kv * B : (kv + 1) * B, :], fm[:, pl.ds(pl.multiple_of(column, B), B)])

        def store(r, value):
            out = gwk_out if r // 2 == 0 else gwv_out
            half = r % 2
            out[half * B : (half + 1) * B, :] = value.T

        over_psg.item(kind, dy, u, own, store)

    piece = 2 * B // 8

    def q1_copy(dy, dx):
        there = seen_by(dy, dx)
        start = pl.multiple_of(psg_at(dy, dx) * piece, piece)
        return pltpu.make_async_remote_copy(
            src_ref=gq_acc.at[pl.ds(start, piece)],
            dst_ref=gq_recv.at[there],
            send_sem=q1_ssem.at[dy * 4 + dx],
            recv_sem=q1_rsem.at[there],
            device_id=on_psg(dy, dx),
            device_id_type=MESH,
        )

    def q2_copy(dy, dx):
        return pltpu.make_async_remote_copy(
            src_ref=gq_own,
            dst_ref=gq_full.at[p],
            send_sem=q2_ssem.at[dy * 4 + dx],
            recv_sem=q2_rsem.at[seen_by(dy, dx)],
            device_id=on_psg(dy, dx),
            device_id_type=MESH,
        )

    def q2_wait(dy, dx):
        pltpu.make_async_remote_copy(
            src_ref=gq_own,
            dst_ref=gq_full.at[psg_at(dy, dx)],
            send_sem=q2_ssem.at[dy * 4 + dx],
            recv_sem=q2_rsem.at[dy * 4 + dx],
            device_id=on_psg(dy, dx),
            device_id_type=MESH,
        ).wait_recv()

    def query_terms():
        gq_acc[...] = jnp.zeros((2 * B, TQ), F32)
        for r in range(PASSAGES_HERE):
            term = nn(kt[r], gs[r])
            for head in range(HEADS_HERE):
                at = slice(head * HEAD_DIM, (head + 1) * HEAD_DIM)
                mine = term[at, head * TQ : (head + 1) * TQ]
                gq_acc[at, :] += mine * picks[r][0]
                after = slice(B + head * HEAD_DIM, B + (head + 1) * HEAD_DIM)
                gq_acc[after, :] += mine * picks[r][1]
        for peer in peers:
            q1_copy(*peer).start()

    def query_sums():
        total = gq_acc[pl.ds(pl.multiple_of(p * piece, piece), piece), :]
        for dy, dx in peers:
            there = dy * 4 + dx
            pltpu.make_async_remote_copy(
                src_ref=gq_recv.at[there],
                dst_ref=gq_recv.at[there],
                send_sem=q1_ssem.at[there],
                recv_sem=q1_rsem.at[there],
                device_id=on_psg(dy, dx),
                device_id_type=MESH,
            ).wait_recv()
            total = total + gq_recv[there]
        gq_own[...] = total.astype(BF16)
        for peer in peers:
            q2_copy(*peer).start()
        gq_full[p] = gq_own[...]

    sibling_item(0)
    for number in range(len(ITEMS)):
        psg_item(number)
        if number + 1 < len(ITEMS):
            sibling_item(number + 1)
        head_item(number)
        if number == 2:
            query_terms()
        if number == 8:
            query_sums()

    for peer in peers:
        q2_wait(*peer)
    for question in range(2):
        turned = jnp.concatenate([gq_full[question * 4 + k] for k in range(4)], axis=0)
        gq_out[question * TQ : (question + 1) * TQ, :] = turned.astype(F32).T.astype(BF16)

    def gather_sent(r, carry):
        for number in range(15):
            gather_copy((0, 0), (0, 0), r, number, sibling).wait_send()
        return carry

    lax.fori_loop(0, PASSAGES_HERE, gather_sent, 0)
    for peer in peers:
        stat_copy(*peer).wait_send()
        q1_copy(*peer).wait_send()
        q2_copy(*peer).wait_send()
    for number in range(len(ITEMS)):
        sibling_copy(number).wait_send()
    over_head.finish()
    over_psg.finish()


def on_device(queries, memory, lengths, owner, w_key, w_value, grad_context):
    rows, width = memory.shape[0], w_key.shape[0]
    vmem = pl.BlockSpec(memory_space=pltpu.VMEM)
    smem = pl.BlockSpec(memory_space=pltpu.SMEM)
    anywhere = pl.BlockSpec(memory_space=pl.ANY)
    dma = pltpu.SemaphoreType.DMA
    half = 2 * B
    outs = pl.pallas_call(
        kernel,
        out_shape=(
            jax.ShapeDtypeStruct((2 * TQ, B), BF16),
            jax.ShapeDtypeStruct((rows, B), BF16),
            jax.ShapeDtypeStruct((half, B), F32),
            jax.ShapeDtypeStruct((half, B), F32),
        ),
        in_specs=[smem, smem, vmem, vmem, anywhere, anywhere, anywhere],
        out_specs=[vmem] * 4,
        scratch_shapes=[
            pltpu.VMEM((rows, width), BF16),
            pltpu.VMEM((width, 2 * B), BF16),
            pltpu.VMEM((2, PAIRS, B), BF16),
            pltpu.VMEM((2, PAIRS, B), BF16),
            pltpu.VMEM((2, B, PAIRS), BF16),
            pltpu.VMEM((2, B, PAIRS), BF16),
            pltpu.VMEM((rows, 2 * B), F32),
            pltpu.VMEM((PASSAGES_HERE, B, B), BF16),
            pltpu.VMEM((PASSAGES_HERE, LEN, PAIRS), F32),
            pltpu.VMEM((PASSAGES_HERE, LEN, PAIRS), F32),
            pltpu.VMEM((PASSAGES_HERE, 8, PAIRS), F32),
            pltpu.VMEM((8, PAIRS), F32),
            pltpu.VMEM((8, 8, PAIRS), F32),
            pltpu.VMEM((rows, 2 * B), BF16),
            pltpu.VMEM((2 * B, rows), BF16),
            pltpu.VMEM((PASSAGES_HERE, LEN, PAIRS), BF16),
            pltpu.VMEM((16, half, B), BF16),
            pltpu.VMEM((16, half, B), BF16),
            pltpu.VMEM((12, half, B), BF16),
            pltpu.VMEM((12, half, B), BF16),
            pltpu.VMEM((2, half, B), BF16),
            pltpu.VMEM((2, half, B), BF16),
            pltpu.VMEM((12, half, B), BF16),
            pltpu.VMEM((12, half, B), BF16),
            pltpu.VMEM((2, half, B), BF16),
            pltpu.VMEM((2, half, B), BF16),
            pltpu.VMEM((2 * B, TQ), F32),
            pltpu.VMEM((8, 2 * B // 8, TQ), F32),
            pltpu.VMEM((2 * B // 8, TQ), BF16),
            pltpu.VMEM((8, 2 * B // 8, TQ), BF16),
            dma, dma((32,)), dma((15, 4)), dma((16, 4)),
            dma((8,)), dma((8,)),
            dma((16,)), dma((16,)),
            dma((12, 2)), dma((12, 2)), dma((2,)), dma((2,)),
            dma((12, 2)), dma((12, 2)), dma((2,)), dma((2,)),
            dma((8,)), dma((8,)), dma((8,)), dma((8,)),
        ],
        compiler_params=pltpu.CompilerParams(
            collective_id=0, has_side_effects=True, vmem_limit_bytes=60 * 2**20
        ),
        name="whole",
    )(lengths, owner, queries, grad_context, memory, w_key, w_value)
    return tuple(outs)


def solution(mesh):
    in_specs = (
        P(None, "head"),
        P("psg", "head"),
        P("psg"),
        P("psg"),
        P(None, "head"),
        P(None, "head"),
        P(None, "head"),
    )
    out_specs = (P(None, "head"), P("psg", "head"), P("psg", "head"), P("psg", "head"))
    return jax.shard_map(
        on_device, mesh=mesh, in_specs=in_specs, out_specs=out_specs, check_vma=False
    )
```

```python
import jax
import jax.numpy as jnp
from jax import lax
from jax.experimental import pallas as pl
from jax.experimental.pallas import tpu as pltpu
from jax.sharding import PartitionSpec as P

HEAD_DIM = 64
LEN = 256
TQ = 128
HEADS_HERE = 4
PASSAGES_HERE = 4
B = 256
PAIRS = HEADS_HERE * TQ
MESH = pl.DeviceIdType.MESH
FILL = -1e30
F32 = jnp.float32
BF16 = jnp.bfloat16

PLACES = ((0, 0), (0, 1), (0, 3), (1, 0), (0, 2), (1, 2), (1, 1), (1, 3))
SLOT = {place: slot for slot, place in enumerate(PLACES)}


def is_equal(a, k):
    return 1 - ((a - k) * (a - k) + 48) // 49


def slot_of(dy, dz):
    code = dy * 4 + dz
    total = 0
    for (py, pz), slot in SLOT.items():
        total = total + slot * is_equal(code, py * 4 + pz)
    return total


def nt(a, b):
    return lax.dot_general(a, b, (((1,), (1,)), ((), ())), preferred_element_type=F32)


def nn(a, b):
    return jnp.dot(a, b, preferred_element_type=F32)


class Scatter:
    def __init__(self, send, recv, ysend, yrecv, ssem, rsem, yssem, yrsem, following, before, partner):
        self.send, self.recv, self.ysend, self.yrecv = send, recv, ysend, yrecv
        self.ssem, self.rsem, self.yssem, self.yrsem = ssem, rsem, yssem, yrsem
        self.following, self.before, self.partner = following, before, partner

    def half(self, ref, index, way):
        return ref.at[index, pl.ds(way * B, B)]

    def copy(self, index, way):
        return pltpu.make_async_remote_copy(
            src_ref=self.half(self.send, index, way),
            dst_ref=self.half(self.recv, index, way),
            send_sem=self.ssem.at[index, way],
            recv_sem=self.rsem.at[index, way],
            device_id=self.before if way else self.following,
            device_id_type=MESH,
        )

    def ycopy(self, u):
        return pltpu.make_async_remote_copy(
            src_ref=self.ysend.at[u],
            dst_ref=self.yrecv.at[u],
            send_sem=self.yssem.at[u],
            recv_sem=self.yrsem.at[u],
            device_id=self.partner,
            device_id_type=MESH,
        )

    def arrived(self, index, way):
        return self.recv[index, way * B : (way + 1) * B, :].astype(F32)

    def item(self, kind, dy, u, own, store):
        first = (dy * 2 + u) * 3
        if kind == "D":
            for way in (0, 1):
                self.copy(first + 1, way).wait_recv()
                self.copy(first + 2, way).wait_recv()
            if dy == 0:
                self.ycopy(u).wait_recv()
            for way in (0, 1):
                value = own(0, way * 2 + u, way)
                value = value + self.arrived(first + 2, way) + self.arrived(first + 1, 1 - way)
                if dy == 1:
                    self.ysend[u, way * B : (way + 1) * B, :] = value.astype(BF16)
                else:
                    value = value + self.yrecv[u, way * B : (way + 1) * B, :].astype(F32)
                    store(way * 2 + u, value)
            if dy == 1:
                self.ycopy(u).start()
            return
        index = first + "ABC".index(kind)
        for way in (0, 1):
            dz, r = chunk_of(kind, u, way)
            if kind == "C":
                self.copy(first, way).wait_recv()
            value = own(dz, r, way)
            if kind == "C":
                value = value + self.arrived(first, way)
            self.send[index, way * B : (way + 1) * B, :] = value.astype(BF16)
            self.copy(index, way).start()

    def finish(self, indices):
        for index in indices:
            for way in (0, 1):
                self.copy(index, way).wait_send()

    def finish_y(self):
        for u in (0, 1):
            self.ycopy(u).wait_send()


def chunk_of(kind, u, way):
    if kind == "A":
        return 2, way * 2 + u
    if kind == "B":
        return (3, u) if way else (1, 2 + u)
    if kind == "C":
        return (3, 2 + u) if way else (1, u)
    return 0, way * 2 + u


ITEMS = (
    ("A", 1, 0), ("B", 1, 0), ("A", 1, 1), ("C", 1, 0), ("B", 1, 1), ("C", 1, 1),
    ("A", 0, 0), ("B", 0, 0), ("D", 1, 0), ("A", 0, 1), ("C", 0, 0), ("D", 1, 1),
    ("B", 0, 1), ("C", 0, 1), ("D", 0, 0), ("D", 0, 1),
)
LAST = (4, 5)
EARLIER = tuple(index for index in range(12) if index not in LAST)


def kernel(
    len_ref, own_ref, q_in, c_in, mem_ref, wk_ref, wv_ref,
    gq_out, gm_out, gw_out,
    q_ref, c_ref, gm_own, gw_own, fm, w, qa, ca, qat, cat, acc, kt, e_ref, gp_ref, stat, sl, sall, g, gt, gs,
    sib_send, sib_recv, m_send, m_recv, my_send, my_recv, w_send, w_recv, wy_send, wy_recv,
    gq_acc, gq_recv, gq_own, gq_full,
    mem_sem, w_sem, qc_sem, out_sem, ag_ssem, ag_rsem, st_ssem, st_rsem, sib_ssem, sib_rsem,
    m_ssem, m_rsem, my_ssem, my_rsem, w_ssem, w_rsem, wy_ssem, wy_rsem,
    q1_ssem, q1_rsem, q2_ssem, q2_rsem,
):
    p, h = lax.axis_index("psg"), lax.axis_index("head")
    yl, x = p // 4, p % 4
    yh, z, core = h // 8, (h // 2) % 4, h % 2

    def head_at(dy, dz, dc=0):
        return ((yh + dy) % 2) * 8 + ((z + dz) % 4) * 2 + (core + dc) % 2

    def psg_at(dy, dx):
        return ((yl + dy) % 2) * 4 + (x + dx) % 4

    def on_head(dy, dz, dc=0):
        return (p, head_at(dy, dz, dc))

    def on_psg(dy, dx):
        return (psg_at(dy, dx), h)

    up, down, across, sibling = on_head(0, 1), on_head(0, 3), on_head(1, 0), on_head(0, 0, 1)
    peers = [(k // 4, k % 4) for k in range(1, 8)]

    mem_copy = pltpu.make_async_copy(mem_ref, fm.at[:, pl.ds(0, B)], mem_sem)
    mem_copy.start()
    q_copies = [
        pltpu.make_async_copy(q_in, q_ref, qc_sem.at[0]),
        pltpu.make_async_copy(c_in, c_ref, qc_sem.at[1]),
    ]
    for copy in q_copies:
        copy.start()
    barrier = pltpu.get_barrier_semaphore()
    partners = [up, down, across, sibling] + [on_psg(*peer) for peer in peers]
    for device in partners:
        pl.semaphore_signal(barrier, inc=1, device_id=device, device_id_type=MESH)
    pl.semaphore_wait(barrier, len(partners))
    mem_copy.wait()

    def block(slot, dc, r):
        return fm.at[pl.ds(r * B, B), pl.ds((slot * 2 + dc) * B, B)]

    def gather_copy(source, target, r, number, device):
        return pltpu.make_async_remote_copy(
            src_ref=block(source[0], source[1], r),
            dst_ref=block(target[0], target[1], r),
            send_sem=ag_ssem.at[number, r],
            recv_sem=ag_rsem.at[target[0] * 2 + target[1], r],
            device_id=device,
            device_id_type=MESH,
        )

    def gathered(slot, dc, r):
        gather_copy((slot, dc), (slot, dc), r, 0, sibling).wait_recv()

    def to_sibling(slot, r):
        gather_copy((slot, 0), (slot, 1), r, 4 + slot, sibling).start()

    for k in range(PASSAGES_HERE):
        gather_copy((0, 0), (SLOT[0, 3], 0), k, 0, up).start()
        gather_copy((0, 0), (SLOT[0, 1], 0), (k + 2) % 4, 1, down).start()
        gather_copy((0, 0), (SLOT[1, 0], 0), k % 2 * 2 + k // 2, 2, across).start()
    for r in range(PASSAGES_HERE):
        to_sibling(0, r)
    w_copies = []
    for slot, (dy, dz) in enumerate(PLACES):
        for dc in (0, 1):
            rows = pl.ds(pl.multiple_of(head_at(dy, dz, dc) * B, B), B)
            into = pl.ds((slot * 2 + dc) * B, B)
            for part, ref in enumerate((wk_ref, wv_ref)):
                w_copies.append(
                    pltpu.make_async_copy(
                        ref.at[rows, :],
                        w.at[into, pl.ds(part * B, B)],
                        w_sem.at[(slot * 2 + dc) * 2 + part],
                    )
                )
                w_copies[-1].start()

    lane = lax.broadcasted_iota(jnp.int32, (TQ, B), 1) // HEAD_DIM
    row = lax.broadcasted_iota(jnp.int32, (B, TQ), 0) // HEAD_DIM
    for copy in q_copies:
        copy.wait()
    for source, plain, turned in ((q_ref, qa, qat), (c_ref, ca, cat)):
        for question in range(2):
            mine = source[question * TQ : (question + 1) * TQ, :].astype(F32)
            mine_t = mine.T
            for head in range(HEADS_HERE):
                at = slice(head * TQ, (head + 1) * TQ)
                plain[question, at, :] = jnp.where(lane == head, mine, 0.0).astype(BF16)
                turned[question, :, at] = jnp.where(row == head, mine_t, 0.0).astype(BF16)

    def rows_of(r):
        return pl.ds(pl.multiple_of(r * B, B), B)

    for r in (0, 1):
        gathered(SLOT[0, 3], 0, r)
        gather_copy((SLOT[0, 3], 0), (SLOT[0, 2], 0), r, 3, up).start()
        to_sibling(SLOT[0, 3], r)
        gathered(SLOT[0, 1], 0, 2 + r)
        gather_copy((SLOT[0, 1], 0), (SLOT[0, 2], 0), 2 + r, 3, down).start()
        to_sibling(SLOT[0, 1], 2 + r)

    def passage(k):
        return k % 2 * 2 + k // 2

    for k in range(PASSAGES_HERE):
        r = passage(k)
        gathered(SLOT[1, 0], 0, r)
        gather_copy((SLOT[1, 0], 0), (SLOT[1, 3], 0), r, 12, up).start()
        gather_copy((SLOT[1, 0], 0), (SLOT[1, 1], 0), r, 13, down).start()
        to_sibling(SLOT[1, 0], r)
        late = SLOT[0, 1] if r < 2 else SLOT[0, 3]
        gathered(late, 0, r)
        to_sibling(late, r)

    for copy in w_copies[:16]:
        copy.wait()

    def first_part(k, carry):
        r = passage(k)
        for slot in range(4):
            gathered(slot, 1, r)
        acc[rows_of(r), :] = nn(fm[rows_of(r), 0 : 8 * B], w[0 : 8 * B, :])
        return carry

    for pair in (0, 1):
        lax.fori_loop(pair * 2, pair * 2 + 2, first_part, 0)
        for r in (pair, 2 + pair):
            gathered(SLOT[0, 2], 0, r)
            gather_copy((SLOT[0, 2], 0), (SLOT[1, 2], 0), r, 14, across).start()
            to_sibling(SLOT[0, 2], r)

    for copy in w_copies[16:]:
        copy.wait()

    def second_part(k, carry):
        r = passage(k)
        gathered(SLOT[1, 2], 0, r)
        to_sibling(SLOT[1, 2], r)
        gathered(SLOT[0, 2], 1, r)
        gathered(SLOT[1, 2], 1, r)
        acc[rows_of(r), :] += nn(fm[rows_of(r), 8 * B : 12 * B], w[8 * B : 12 * B, :])
        for slot in (SLOT[1, 1], SLOT[1, 3]):
            gathered(slot, 0, r)
            to_sibling(slot, r)
        for slot in (SLOT[1, 1], SLOT[1, 3]):
            gathered(slot, 1, r)
        both = acc[rows_of(r), :] + nn(fm[rows_of(r), 12 * B :], w[12 * B :, :])
        keys, values = both[:, :B], both[:, B:].astype(BF16)
        kt[r] = keys.T.astype(BF16)
        keys = keys.astype(BF16)
        question = own_ref[r]
        scores = nt(keys, qa[question])
        flows = nt(values, ca[question])
        alive = lax.broadcasted_iota(jnp.int32, (LEN, PAIRS), 0) < len_ref[r]
        masked = jnp.where(alive, scores, FILL)
        top = jnp.max(masked, axis=0, keepdims=True)
        shifted = jnp.where(alive, jnp.exp(masked - top), 0.0)
        e_ref[r] = shifted
        gp_ref[r] = flows
        stat[r, 0:1, :] = top
        stat[r, 1:2, :] = jnp.sum(shifted, axis=0, keepdims=True)
        stat[r, 2:3, :] = jnp.sum(shifted * flows, axis=0, keepdims=True)
        return carry

    lax.fori_loop(0, PASSAGES_HERE, second_part, 0)

    picks = []
    for r in range(PASSAGES_HERE):
        second = own_ref[r].astype(F32)
        picks.append((1.0 - second, second))
    for question in range(2):
        tops = [
            stat[r, 0:1, :] * picks[r][question] + FILL * (1.0 - picks[r][question])
            for r in range(PASSAGES_HERE)
        ]
        top = jnp.maximum(jnp.maximum(tops[0], tops[1]), jnp.maximum(tops[2], tops[3]))
        mass = jnp.zeros((1, PAIRS), F32)
        flow = jnp.zeros((1, PAIRS), F32)
        for r in range(PASSAGES_HERE):
            scale = jnp.exp(tops[r] - top) * picks[r][question]
            mass += stat[r, 1:2, :] * scale
            flow += stat[r, 2:3, :] * scale
        sl[question : question + 1, :] = top
        sl[2 + question : 3 + question, :] = mass
        sl[4 + question : 5 + question, :] = flow
    sl[6:8, :] = jnp.zeros((2, PAIRS), F32)

    def seen_by(dy, dx):
        return dy * 4 + (4 - dx) % 4

    def stat_copy(dy, dx):
        there = seen_by(dy, dx)
        return pltpu.make_async_remote_copy(
            src_ref=sl,
            dst_ref=sall.at[there],
            send_sem=st_ssem.at[dy * 4 + dx],
            recv_sem=st_rsem.at[there],
            device_id=on_psg(dy, dx),
            device_id_type=MESH,
        )

    for peer in peers:
        stat_copy(*peer).start()
    for peer in peers:
        stat_copy(*peer).wait_recv()
    sall[0] = sl[...]
    totals = []
    for question in range(2):
        tops = [sall[k, question : question + 1, :] for k in range(8)]
        top = tops[0]
        for other in tops[1:]:
            top = jnp.maximum(top, other)
        mass = jnp.zeros((1, PAIRS), F32)
        flow = jnp.zeros((1, PAIRS), F32)
        for k in range(8):
            scale = jnp.exp(tops[k] - top)
            mass += sall[k, 2 + question : 3 + question, :] * scale
            flow += sall[k, 4 + question : 5 + question, :] * scale
        totals.append((top, 1.0 / mass, flow / mass))
    for r in range(PASSAGES_HERE):
        top, inverse, shift = (
            totals[0][k] * picks[r][0] + totals[1][k] * picks[r][1] for k in range(3)
        )
        stat[r, 3:4, :] = jnp.exp(stat[r, 0:1, :] - top) * inverse
        stat[r, 4:5, :] = shift

    def gradients(k, carry):
        r = passage(k)
        question = own_ref[r]
        probs = e_ref[r] * stat[r, 3:4, :]
        grad = (probs * (gp_ref[r] - stat[r, 4:5, :])).astype(BF16)
        probs = probs.astype(BF16)
        gs[r] = grad
        g[rows_of(r), 0:B] = nn(grad, qa[question]).astype(BF16)
        g[rows_of(r), B : 2 * B] = nn(probs, ca[question]).astype(BF16)
        gt[0:B, rows_of(r)] = nt(qat[question], grad).astype(BF16)
        gt[B : 2 * B, rows_of(r)] = nt(cat[question], probs).astype(BF16)
        return carry

    lax.fori_loop(0, 2, gradients, 0)

    over_head = Scatter(
        m_send, m_recv, my_send, my_recv, m_ssem, m_rsem, my_ssem, my_rsem, up, down, across
    )
    over_psg = Scatter(
        w_send, w_recv, wy_send, wy_recv, w_ssem, w_rsem, wy_ssem, wy_rsem,
        on_psg(0, 1), on_psg(0, 3), on_psg(1, 0),
    )

    def out_copy(source, target, number):
        return pltpu.make_async_copy(source, target, out_sem.at[number])

    def part(slot, dc, r):
        at = (slot * 2 + dc) * B
        return nt(g[r * B : (r + 1) * B, :], w[at : at + B, :]).astype(BF16)

    def sibling_copy(number):
        return pltpu.make_async_remote_copy(
            src_ref=sib_send.at[number],
            dst_ref=sib_recv.at[number],
            send_sem=sib_ssem.at[number],
            recv_sem=sib_rsem.at[number],
            device_id=sibling,
            device_id_type=MESH,
        )

    def sibling_item(number):
        kind, dy, u = ITEMS[number]
        for way in (0, 1):
            dz, r = chunk_of(kind, u, way)
            sib_send[number, way * B : (way + 1) * B, :] = part(SLOT[dy, dz], 1, r)
        sibling_copy(number).start()

    def head_item(number):
        kind, dy, u = ITEMS[number]
        sibling_copy(number).wait_recv()

        def own(dz, r, way):
            other = sib_recv[number, way * B : (way + 1) * B, :].astype(F32)
            return part(SLOT[dy, dz], 0, r).astype(F32) + other

        def store(r, value):
            gm_own[r * B : (r + 1) * B, :] = value.astype(BF16)
            out_copy(gm_own.at[pl.ds(r * B, B)], gm_out.at[pl.ds(r * B, B)], r).start()

        over_head.item(kind, dy, u, own, store)

    def psg_item(number):
        kind, dy, u = ITEMS[number]

        def own(dx, r, way):
            kv, half = r // 2, r % 2
            slot = slot_of((yl + dy + 2 - yh) % 2, (x + dx + 4 - z) % 4)
            column = (slot * 2 + (half + 2 - core) % 2) * B
            return nn(gt[kv * B : (kv + 1) * B, :], fm[:, pl.ds(pl.multiple_of(column, B), B)])

        def store(r, value):
            gw_own[r] = value
            out_copy(gw_own.at[r], gw_out.at[r], 4 + r).start()

        over_psg.item(kind, dy, u, own, store)

    piece = 2 * B // 8

    def q1_copy(dy, dx):
        there = seen_by(dy, dx)
        start = pl.multiple_of(psg_at(dy, dx) * piece, piece)
        return pltpu.make_async_remote_copy(
            src_ref=gq_acc.at[pl.ds(start, piece)],
            dst_ref=gq_recv.at[there],
            send_sem=q1_ssem.at[dy * 4 + dx],
            recv_sem=q1_rsem.at[there],
            device_id=on_psg(dy, dx),
            device_id_type=MESH,
        )

    def q2_copy(dy, dx):
        return pltpu.make_async_remote_copy(
            src_ref=gq_own,
            dst_ref=gq_full.at[p],
            send_sem=q2_ssem.at[dy * 4 + dx],
            recv_sem=q2_rsem.at[seen_by(dy, dx)],
            device_id=on_psg(dy, dx),
            device_id_type=MESH,
        )

    def q2_wait(dy, dx):
        pltpu.make_async_remote_copy(
            src_ref=gq_own,
            dst_ref=gq_full.at[psg_at(dy, dx)],
            send_sem=q2_ssem.at[dy * 4 + dx],
            recv_sem=q2_rsem.at[dy * 4 + dx],
            device_id=on_psg(dy, dx),
            device_id_type=MESH,
        ).wait_recv()

    def query_terms():
        gq_acc[...] = jnp.zeros((2 * B, TQ), F32)
        for r in range(PASSAGES_HERE):
            term = nn(kt[r], gs[r])
            for head in range(HEADS_HERE):
                at = slice(head * HEAD_DIM, (head + 1) * HEAD_DIM)
                mine = term[at, head * TQ : (head + 1) * TQ]
                gq_acc[at, :] += mine * picks[r][0]
                after = slice(B + head * HEAD_DIM, B + (head + 1) * HEAD_DIM)
                gq_acc[after, :] += mine * picks[r][1]
        for peer in peers:
            q1_copy(*peer).start()

    def query_sums():
        total = gq_acc[pl.ds(pl.multiple_of(p * piece, piece), piece), :]
        for dy, dx in peers:
            there = dy * 4 + dx
            pltpu.make_async_remote_copy(
                src_ref=gq_recv.at[there],
                dst_ref=gq_recv.at[there],
                send_sem=q1_ssem.at[there],
                recv_sem=q1_rsem.at[there],
                device_id=on_psg(dy, dx),
                device_id_type=MESH,
            ).wait_recv()
            total = total + gq_recv[there]
        gq_own[...] = total.astype(BF16)
        for peer in peers:
            q2_copy(*peer).start()
        gq_full[p] = gq_own[...]

    def query_end():
        for peer in peers:
            q2_wait(*peer)
        out_copy(gq_full, gq_out, 8).start()

    def gather_sent(r, carry):
        for number in range(15):
            gather_copy((0, 0), (0, 0), r, number, sibling).wait_send()
        return carry

    def sent():
        lax.fori_loop(0, PASSAGES_HERE, gather_sent, 0)
        for peer in peers:
            stat_copy(*peer).wait_send()
            q1_copy(*peer).wait_send()
            q2_copy(*peer).wait_send()
        for number in range(len(ITEMS) - 1):
            sibling_copy(number).wait_send()

    sibling_item(0)
    lax.fori_loop(2, 4, gradients, 0)
    for number in range(len(ITEMS)):
        if number == 14:
            query_end()
            sent()
            over_head.finish(EARLIER)
            over_psg.finish(EARLIER)
        psg_item(number)
        if number + 1 < len(ITEMS):
            sibling_item(number + 1)
        head_item(number)
        if number == 2:
            query_terms()
        if number == 8:
            query_sums()

    sibling_copy(len(ITEMS) - 1).wait_send()
    over_head.finish(LAST)
    over_psg.finish(LAST)
    over_head.finish_y()
    over_psg.finish_y()
    for r in range(PASSAGES_HERE):
        out_copy(gm_own.at[pl.ds(r * B, B)], gm_out.at[pl.ds(r * B, B)], r).wait()
        out_copy(gw_own.at[r], gw_out.at[r], 4 + r).wait()
    out_copy(gq_full, gq_out, 8).wait()


def epilogue(gq_in, gm_in, gw_in, gq_out, gm_out, gwk_out, gwv_out):
    gm_out[...] = gm_in[...]
    for r in range(4):
        out = gwk_out if r < 2 else gwv_out
        half = r % 2
        out[half * B : (half + 1) * B, :] = gw_in[r].T
    for question in range(2):
        turned = jnp.concatenate([gq_in[question * 4 + k] for k in range(4)], axis=0)
        gq_out[question * TQ : (question + 1) * TQ, :] = turned.astype(F32).T.astype(BF16)


def on_device(queries, memory, lengths, owner, w_key, w_value, grad_context):
    rows, width = memory.shape[0], w_key.shape[0]
    vmem = pl.BlockSpec(memory_space=pltpu.VMEM)
    smem = pl.BlockSpec(memory_space=pltpu.SMEM)
    anywhere = pl.BlockSpec(memory_space=pl.ANY)
    dma = pltpu.SemaphoreType.DMA
    half = 2 * B
    outs = pl.pallas_call(
        kernel,
        out_shape=(
            jax.ShapeDtypeStruct((8, 2 * B // 8, TQ), BF16),
            jax.ShapeDtypeStruct((rows, B), BF16),
            jax.ShapeDtypeStruct((4, B, B), F32),
        ),
        in_specs=[smem, smem] + [anywhere] * 5,
        out_specs=[anywhere] * 3,
        scratch_shapes=[
            pltpu.VMEM((2 * TQ, B), BF16),
            pltpu.VMEM((2 * TQ, B), BF16),
            pltpu.VMEM((rows, B), BF16),
            pltpu.VMEM((4, B, B), F32),
            pltpu.VMEM((rows, width), BF16),
            pltpu.VMEM((width, 2 * B), BF16),
            pltpu.VMEM((2, PAIRS, B), BF16),
            pltpu.VMEM((2, PAIRS, B), BF16),
            pltpu.VMEM((2, B, PAIRS), BF16),
            pltpu.VMEM((2, B, PAIRS), BF16),
            pltpu.VMEM((rows, 2 * B), F32),
            pltpu.VMEM((PASSAGES_HERE, B, B), BF16),
            pltpu.VMEM((PASSAGES_HERE, LEN, PAIRS), F32),
            pltpu.VMEM((PASSAGES_HERE, LEN, PAIRS), F32),
            pltpu.VMEM((PASSAGES_HERE, 8, PAIRS), F32),
            pltpu.VMEM((8, PAIRS), F32),
            pltpu.VMEM((8, 8, PAIRS), F32),
            pltpu.VMEM((rows, 2 * B), BF16),
            pltpu.VMEM((2 * B, rows), BF16),
            pltpu.VMEM((PASSAGES_HERE, LEN, PAIRS), BF16),
            pltpu.VMEM((16, half, B), BF16),
            pltpu.VMEM((16, half, B), BF16),
            pltpu.VMEM((12, half, B), BF16),
            pltpu.VMEM((12, half, B), BF16),
            pltpu.VMEM((2, half, B), BF16),
            pltpu.VMEM((2, half, B), BF16),
            pltpu.VMEM((12, half, B), BF16),
            pltpu.VMEM((12, half, B), BF16),
            pltpu.VMEM((2, half, B), BF16),
            pltpu.VMEM((2, half, B), BF16),
            pltpu.VMEM((2 * B, TQ), F32),
            pltpu.VMEM((8, 2 * B // 8, TQ), F32),
            pltpu.VMEM((2 * B // 8, TQ), BF16),
            pltpu.VMEM((8, 2 * B // 8, TQ), BF16),
            dma, dma((32,)), dma((2,)), dma((9,)),
            dma((15, 4)), dma((16, 4)),
            dma((8,)), dma((8,)),
            dma((16,)), dma((16,)),
            dma((12, 2)), dma((12, 2)), dma((2,)), dma((2,)),
            dma((12, 2)), dma((12, 2)), dma((2,)), dma((2,)),
            dma((8,)), dma((8,)), dma((8,)), dma((8,)),
        ],
        compiler_params=pltpu.CompilerParams(
            collective_id=0, has_side_effects=True, vmem_limit_bytes=60 * 2**20
        ),
        name="whole",
    )(lengths, owner, queries, grad_context, memory, w_key, w_value)
    gq, gm, gwk, gwv = pl.pallas_call(
        epilogue,
        out_shape=(
            jax.ShapeDtypeStruct((2 * TQ, B), BF16),
            jax.ShapeDtypeStruct((rows, B), BF16),
            jax.ShapeDtypeStruct((half, B), F32),
            jax.ShapeDtypeStruct((half, B), F32),
        ),
        in_specs=[vmem] * 3,
        out_specs=[vmem] * 4,
        name="turn",
    )(*outs)
    return gq, gm, gwk, gwv


def solution(mesh):
    in_specs = (
        P(None, "head"),
        P("psg", "head"),
        P("psg"),
        P("psg"),
        P(None, "head"),
        P(None, "head"),
        P(None, "head"),
    )
    out_specs = (P(None, "head"), P("psg", "head"), P("psg", "head"), P("psg", "head"))
    return jax.shard_map(
        on_device, mesh=mesh, in_specs=in_specs, out_specs=out_specs, check_vma=False
    )
```

```python
import jax
import jax.numpy as jnp
from jax import lax
from jax.experimental import pallas as pl
from jax.experimental.pallas import tpu as pltpu
from jax.sharding import PartitionSpec as P

HEAD_DIM = 64
LEN = 256
TQ = 128
HEADS_HERE = 4
PASSAGES_HERE = 4
B = 256
PAIRS = HEADS_HERE * TQ
MESH = pl.DeviceIdType.MESH
FILL = -1e30
F32 = jnp.float32
BF16 = jnp.bfloat16

PLACES = ((0, 0), (0, 1), (0, 3), (1, 0), (0, 2), (1, 2), (1, 1), (1, 3))
SLOT = {place: slot for slot, place in enumerate(PLACES)}


def is_equal(a, k):
    return 1 - ((a - k) * (a - k) + 48) // 49


def slot_of(dy, dz):
    code = dy * 4 + dz
    total = 0
    for (py, pz), slot in SLOT.items():
        total = total + slot * is_equal(code, py * 4 + pz)
    return total


def nt(a, b):
    return lax.dot_general(a, b, (((1,), (1,)), ((), ())), preferred_element_type=F32)


def nn(a, b):
    return jnp.dot(a, b, preferred_element_type=F32)


class Scatter:
    def __init__(self, send, recv, ysend, yrecv, ssem, rsem, yssem, yrsem, following, before, partner):
        self.send, self.recv, self.ysend, self.yrecv = send, recv, ysend, yrecv
        self.ssem, self.rsem, self.yssem, self.yrsem = ssem, rsem, yssem, yrsem
        self.following, self.before, self.partner = following, before, partner

    def half(self, ref, index, way):
        return ref.at[index, pl.ds(way * B, B)]

    def copy(self, index, way):
        return pltpu.make_async_remote_copy(
            src_ref=self.half(self.send, index, way),
            dst_ref=self.half(self.recv, index, way),
            send_sem=self.ssem.at[index, way],
            recv_sem=self.rsem.at[index, way],
            device_id=self.before if way else self.following,
            device_id_type=MESH,
        )

    def ycopy(self, u):
        return pltpu.make_async_remote_copy(
            src_ref=self.ysend.at[u],
            dst_ref=self.yrecv.at[u],
            send_sem=self.yssem.at[u],
            recv_sem=self.yrsem.at[u],
            device_id=self.partner,
            device_id_type=MESH,
        )

    def arrived(self, index, way):
        return self.recv[index, way * B : (way + 1) * B, :].astype(F32)

    def item(self, kind, dy, u, own, store):
        first = (dy * 2 + u) * 3
        if kind == "D":
            mine = [own(0, way * 2 + u, way) for way in (0, 1)]
            for way in (0, 1):
                self.copy(first + 1, way).wait_recv()
                self.copy(first + 2, way).wait_recv()
            if dy == 0:
                self.ycopy(u).wait_recv()
            for way in (0, 1):
                value = mine[way] + self.arrived(first + 2, way) + self.arrived(first + 1, 1 - way)
                if dy == 1:
                    self.ysend[u, way * B : (way + 1) * B, :] = value.astype(BF16)
                else:
                    value = value + self.yrecv[u, way * B : (way + 1) * B, :].astype(F32)
                    store(way * 2 + u, value)
            if dy == 1:
                self.ycopy(u).start()
            return
        index = first + "ABC".index(kind)
        for way in (0, 1):
            dz, r = chunk_of(kind, u, way)
            value = own(dz, r, way)
            if kind == "C":
                self.copy(first, way).wait_recv()
                value = value + self.arrived(first, way)
            self.send[index, way * B : (way + 1) * B, :] = value.astype(BF16)
            self.copy(index, way).start()

    def finish(self, indices):
        for index in indices:
            for way in (0, 1):
                self.copy(index, way).wait_send()

    def finish_y(self):
        for u in (0, 1):
            self.ycopy(u).wait_send()


def chunk_of(kind, u, way):
    if kind == "A":
        return 2, way * 2 + u
    if kind == "B":
        return (3, u) if way else (1, 2 + u)
    if kind == "C":
        return (3, 2 + u) if way else (1, u)
    return 0, way * 2 + u


ITEMS = (
    ("A", 1, 0), ("B", 1, 0), ("C", 1, 0), ("A", 1, 1), ("B", 1, 1), ("D", 1, 0),
    ("C", 1, 1), ("A", 0, 0), ("B", 0, 0), ("D", 1, 1), ("C", 0, 0), ("A", 0, 1),
    ("B", 0, 1), ("C", 0, 1), ("D", 0, 0), ("D", 0, 1),
)
LAST = (4, 5)
EARLIER = tuple(index for index in range(12) if index not in LAST)


def kernel(
    len_ref, own_ref, q_in, c_in, mem_ref, wk_ref, wv_ref,
    gq_out, gm_out, gw_out,
    q_ref, c_ref, gm_own, gw_own, fm, w, qa, ca, qat, cat, acc, kt, e_ref, gp_ref, stat, sl, sall, g, gt, gs,
    sib_send, sib_recv, m_send, m_recv, my_send, my_recv, w_send, w_recv, wy_send, wy_recv,
    gq_acc, gq_recv, gq_own, gq_full,
    mem_sem, w_sem, qc_sem, out_sem, ag_ssem, ag_rsem, st_ssem, st_rsem, sib_ssem, sib_rsem,
    m_ssem, m_rsem, my_ssem, my_rsem, w_ssem, w_rsem, wy_ssem, wy_rsem,
    q1_ssem, q1_rsem, q2_ssem, q2_rsem,
):
    p, h = lax.axis_index("psg"), lax.axis_index("head")
    yl, x = p // 4, p % 4
    yh, z, core = h // 8, (h // 2) % 4, h % 2

    def head_at(dy, dz, dc=0):
        return ((yh + dy) % 2) * 8 + ((z + dz) % 4) * 2 + (core + dc) % 2

    def psg_at(dy, dx):
        return ((yl + dy) % 2) * 4 + (x + dx) % 4

    def on_head(dy, dz, dc=0):
        return (p, head_at(dy, dz, dc))

    def on_psg(dy, dx):
        return (psg_at(dy, dx), h)

    up, down, across, sibling = on_head(0, 1), on_head(0, 3), on_head(1, 0), on_head(0, 0, 1)
    peers = [(k // 4, k % 4) for k in range(1, 8)]

    mem_copy = pltpu.make_async_copy(mem_ref, fm.at[:, pl.ds(0, B)], mem_sem)
    mem_copy.start()
    q_copies = [
        pltpu.make_async_copy(q_in, q_ref, qc_sem.at[0]),
        pltpu.make_async_copy(c_in, c_ref, qc_sem.at[1]),
    ]
    for copy in q_copies:
        copy.start()
    barrier = pltpu.get_barrier_semaphore()
    partners = [up, down, across, sibling] + [on_psg(*peer) for peer in peers]
    for device in partners:
        pl.semaphore_signal(barrier, inc=1, device_id=device, device_id_type=MESH)
    pl.semaphore_wait(barrier, len(partners))
    mem_copy.wait()

    def block(slot, dc, r):
        return fm.at[pl.ds(r * B, B), pl.ds((slot * 2 + dc) * B, B)]

    def gather_copy(source, target, r, number, device):
        return pltpu.make_async_remote_copy(
            src_ref=block(source[0], source[1], r),
            dst_ref=block(target[0], target[1], r),
            send_sem=ag_ssem.at[number, r],
            recv_sem=ag_rsem.at[target[0] * 2 + target[1], r],
            device_id=device,
            device_id_type=MESH,
        )

    def gathered(slot, dc, r):
        gather_copy((slot, dc), (slot, dc), r, 0, sibling).wait_recv()

    def to_sibling(slot, r):
        gather_copy((slot, 0), (slot, 1), r, 4 + slot, sibling).start()

    def own_along(k):
        gather_copy((0, 0), (SLOT[0, 3], 0), k, 0, up).start()
        gather_copy((0, 0), (SLOT[0, 1], 0), (k + 2) % 4, 1, down).start()

    own_along(0)
    own_along(1)
    for k in range(PASSAGES_HERE):
        gather_copy((0, 0), (SLOT[1, 0], 0), k % 2 * 2 + k // 2, 2, across).start()
    for r in range(PASSAGES_HERE):
        to_sibling(0, r)
    w_copies = []
    for slot, (dy, dz) in enumerate(PLACES):
        for dc in (0, 1):
            rows = pl.ds(pl.multiple_of(head_at(dy, dz, dc) * B, B), B)
            into = pl.ds((slot * 2 + dc) * B, B)
            for part, ref in enumerate((wk_ref, wv_ref)):
                w_copies.append(
                    pltpu.make_async_copy(
                        ref.at[rows, :],
                        w.at[into, pl.ds(part * B, B)],
                        w_sem.at[(slot * 2 + dc) * 2 + part],
                    )
                )
                w_copies[-1].start()

    def opposite(r):
        gathered(SLOT[0, 2], 0, r)
        gather_copy((SLOT[0, 2], 0), (SLOT[1, 2], 0), r, 14, across).start()
        to_sibling(SLOT[0, 2], r)

    def partner(r):
        gathered(SLOT[1, 0], 0, r)
        gather_copy((SLOT[1, 0], 0), (SLOT[1, 3], 0), r, 12, up).start()
        gather_copy((SLOT[1, 0], 0), (SLOT[1, 1], 0), r, 13, down).start()
        to_sibling(SLOT[1, 0], r)

    for r in (0, 1):
        gathered(SLOT[0, 3], 0, r)
        gather_copy((SLOT[0, 3], 0), (SLOT[0, 2], 0), r, 3, up).start()
        gathered(SLOT[0, 1], 0, 2 + r)
        gather_copy((SLOT[0, 1], 0), (SLOT[0, 2], 0), 2 + r, 3, down).start()
        own_along(2 + r)
        to_sibling(SLOT[0, 3], r)
        to_sibling(SLOT[0, 1], 2 + r)
    for r in (0, 1):
        partner(r)
        partner(2 + r)
        opposite(r)
        opposite(2 + r)

    lane = lax.broadcasted_iota(jnp.int32, (TQ, B), 1) // HEAD_DIM
    row = lax.broadcasted_iota(jnp.int32, (B, TQ), 0) // HEAD_DIM
    for copy in q_copies:
        copy.wait()
    for source, plain, turned in ((q_ref, qa, qat), (c_ref, ca, cat)):
        for question in range(2):
            mine = source[question * TQ : (question + 1) * TQ, :].astype(F32)
            mine_t = mine.T
            for head in range(HEADS_HERE):
                at = slice(head * TQ, (head + 1) * TQ)
                plain[question, at, :] = jnp.where(lane == head, mine, 0.0).astype(BF16)
                turned[question, :, at] = jnp.where(row == head, mine_t, 0.0).astype(BF16)

    def rows_of(r):
        return pl.ds(pl.multiple_of(r * B, B), B)

    def passage(k):
        return k % 2 * 2 + k // 2

    for r in (0, 1):
        gathered(SLOT[0, 1], 0, r)
        to_sibling(SLOT[0, 1], r)
        gathered(SLOT[0, 3], 0, 2 + r)
        to_sibling(SLOT[0, 3], 2 + r)

    for copy in w_copies[:16]:
        copy.wait()

    def first_part(k, carry):
        r = passage(k)
        for slot in range(4):
            gathered(slot, 1, r)
        acc[rows_of(r), :] = nn(fm[rows_of(r), 0 : 8 * B], w[0 : 8 * B, :])
        return carry

    lax.fori_loop(0, PASSAGES_HERE, first_part, 0)

    for copy in w_copies[16:]:
        copy.wait()

    def second_part(k, carry):
        r = passage(k)
        gathered(SLOT[1, 2], 0, r)
        to_sibling(SLOT[1, 2], r)
        gathered(SLOT[0, 2], 1, r)
        gathered(SLOT[1, 2], 1, r)
        acc[rows_of(r), :] += nn(fm[rows_of(r), 8 * B : 12 * B], w[8 * B : 12 * B, :])
        for slot in (SLOT[1, 1], SLOT[1, 3]):
            gathered(slot, 0, r)
            to_sibling(slot, r)
        for slot in (SLOT[1, 1], SLOT[1, 3]):
            gathered(slot, 1, r)
        both = acc[rows_of(r), :] + nn(fm[rows_of(r), 12 * B :], w[12 * B :, :])
        keys, values = both[:, :B], both[:, B:].astype(BF16)
        kt[r] = keys.T.astype(BF16)
        keys = keys.astype(BF16)
        question = own_ref[r]
        scores = nt(keys, qa[question])
        flows = nt(values, ca[question])
        alive = lax.broadcasted_iota(jnp.int32, (LEN, PAIRS), 0) < len_ref[r]
        masked = jnp.where(alive, scores, FILL)
        top = jnp.max(masked, axis=0, keepdims=True)
        shifted = jnp.where(alive, jnp.exp(masked - top), 0.0)
        e_ref[r] = shifted
        gp_ref[r] = flows
        stat[r, 0:1, :] = top
        stat[r, 1:2, :] = jnp.sum(shifted, axis=0, keepdims=True)
        stat[r, 2:3, :] = jnp.sum(shifted * flows, axis=0, keepdims=True)
        return carry

    lax.fori_loop(0, PASSAGES_HERE, second_part, 0)

    picks = []
    for r in range(PASSAGES_HERE):
        second = own_ref[r].astype(F32)
        picks.append((1.0 - second, second))
    for question in range(2):
        tops = [
            stat[r, 0:1, :] * picks[r][question] + FILL * (1.0 - picks[r][question])
            for r in range(PASSAGES_HERE)
        ]
        top = jnp.maximum(jnp.maximum(tops[0], tops[1]), jnp.maximum(tops[2], tops[3]))
        mass = jnp.zeros((1, PAIRS), F32)
        flow = jnp.zeros((1, PAIRS), F32)
        for r in range(PASSAGES_HERE):
            scale = jnp.exp(tops[r] - top) * picks[r][question]
            mass += stat[r, 1:2, :] * scale
            flow += stat[r, 2:3, :] * scale
        sl[question : question + 1, :] = top
        sl[2 + question : 3 + question, :] = mass
        sl[4 + question : 5 + question, :] = flow
    sl[6:8, :] = jnp.zeros((2, PAIRS), F32)

    def seen_by(dy, dx):
        return dy * 4 + (4 - dx) % 4

    def stat_copy(dy, dx):
        there = seen_by(dy, dx)
        return pltpu.make_async_remote_copy(
            src_ref=sl,
            dst_ref=sall.at[there],
            send_sem=st_ssem.at[dy * 4 + dx],
            recv_sem=st_rsem.at[there],
            device_id=on_psg(dy, dx),
            device_id_type=MESH,
        )

    for peer in peers:
        stat_copy(*peer).start()
    for peer in peers:
        stat_copy(*peer).wait_recv()
    sall[0] = sl[...]
    totals = []
    for question in range(2):
        tops = [sall[k, question : question + 1, :] for k in range(8)]
        top = tops[0]
        for other in tops[1:]:
            top = jnp.maximum(top, other)
        mass = jnp.zeros((1, PAIRS), F32)
        flow = jnp.zeros((1, PAIRS), F32)
        for k in range(8):
            scale = jnp.exp(tops[k] - top)
            mass += sall[k, 2 + question : 3 + question, :] * scale
            flow += sall[k, 4 + question : 5 + question, :] * scale
        totals.append((top, 1.0 / mass, flow / mass))
    for r in range(PASSAGES_HERE):
        top, inverse, shift = (
            totals[0][k] * picks[r][0] + totals[1][k] * picks[r][1] for k in range(3)
        )
        stat[r, 3:4, :] = jnp.exp(stat[r, 0:1, :] - top) * inverse
        stat[r, 4:5, :] = shift

    def gradients(k, carry):
        r = passage(k)
        question = own_ref[r]
        probs = e_ref[r] * stat[r, 3:4, :]
        grad = (probs * (gp_ref[r] - stat[r, 4:5, :])).astype(BF16)
        probs = probs.astype(BF16)
        gs[r] = grad
        g[rows_of(r), 0:B] = nn(grad, qa[question]).astype(BF16)
        g[rows_of(r), B : 2 * B] = nn(probs, ca[question]).astype(BF16)
        gt[0:B, rows_of(r)] = nt(qat[question], grad).astype(BF16)
        gt[B : 2 * B, rows_of(r)] = nt(cat[question], probs).astype(BF16)
        return carry

    lax.fori_loop(0, 2, gradients, 0)

    over_head = Scatter(
        m_send, m_recv, my_send, my_recv, m_ssem, m_rsem, my_ssem, my_rsem, up, down, across
    )
    over_psg = Scatter(
        w_send, w_recv, wy_send, wy_recv, w_ssem, w_rsem, wy_ssem, wy_rsem,
        on_psg(0, 1), on_psg(0, 3), on_psg(1, 0),
    )

    def out_copy(source, target, number):
        return pltpu.make_async_copy(source, target, out_sem.at[number])

    def part(slot, dc, r):
        at = (slot * 2 + dc) * B
        return nt(g[r * B : (r + 1) * B, :], w[at : at + B, :]).astype(BF16)

    def sibling_copy(number):
        return pltpu.make_async_remote_copy(
            src_ref=sib_send.at[number],
            dst_ref=sib_recv.at[number],
            send_sem=sib_ssem.at[number],
            recv_sem=sib_rsem.at[number],
            device_id=sibling,
            device_id_type=MESH,
        )

    def sibling_item(number):
        kind, dy, u = ITEMS[number]
        for way in (0, 1):
            dz, r = chunk_of(kind, u, way)
            sib_send[number, way * B : (way + 1) * B, :] = part(SLOT[dy, dz], 1, r)
        sibling_copy(number).start()

    def head_item(number):
        kind, dy, u = ITEMS[number]
        sibling_copy(number).wait_recv()

        def own(dz, r, way):
            other = sib_recv[number, way * B : (way + 1) * B, :].astype(F32)
            return part(SLOT[dy, dz], 0, r).astype(F32) + other

        def store(r, value):
            gm_own[r * B : (r + 1) * B, :] = value.astype(BF16)
            out_copy(gm_own.at[pl.ds(r * B, B)], gm_out.at[pl.ds(r * B, B)], r).start()

        over_head.item(kind, dy, u, own, store)

    def psg_item(number):
        kind, dy, u = ITEMS[number]

        def own(dx, r, way):
            kv, half = r // 2, r % 2
            slot = slot_of((yl + dy + 2 - yh) % 2, (x + dx + 4 - z) % 4)
            column = (slot * 2 + (half + 2 - core) % 2) * B
            return nn(gt[kv * B : (kv + 1) * B, :], fm[:, pl.ds(pl.multiple_of(column, B), B)])

        def store(r, value):
            gw_own[r] = value
            out_copy(gw_own.at[r], gw_out.at[r], 4 + r).start()

        over_psg.item(kind, dy, u, own, store)

    piece = 2 * B // 8

    def q1_copy(dy, dx):
        there = seen_by(dy, dx)
        start = pl.multiple_of(psg_at(dy, dx) * piece, piece)
        return pltpu.make_async_remote_copy(
            src_ref=gq_acc.at[pl.ds(start, piece)],
            dst_ref=gq_recv.at[there],
            send_sem=q1_ssem.at[dy * 4 + dx],
            recv_sem=q1_rsem.at[there],
            device_id=on_psg(dy, dx),
            device_id_type=MESH,
        )

    def q2_copy(dy, dx):
        return pltpu.make_async_remote_copy(
            src_ref=gq_own,
            dst_ref=gq_full.at[p],
            send_sem=q2_ssem.at[dy * 4 + dx],
            recv_sem=q2_rsem.at[seen_by(dy, dx)],
            device_id=on_psg(dy, dx),
            device_id_type=MESH,
        )

    def q2_wait(dy, dx):
        pltpu.make_async_remote_copy(
            src_ref=gq_own,
            dst_ref=gq_full.at[psg_at(dy, dx)],
            send_sem=q2_ssem.at[dy * 4 + dx],
            recv_sem=q2_rsem.at[dy * 4 + dx],
            device_id=on_psg(dy, dx),
            device_id_type=MESH,
        ).wait_recv()

    def query_terms():
        gq_acc[...] = jnp.zeros((2 * B, TQ), F32)
        for r in range(PASSAGES_HERE):
            term = nn(kt[r], gs[r])
            for head in range(HEADS_HERE):
                at = slice(head * HEAD_DIM, (head + 1) * HEAD_DIM)
                mine = term[at, head * TQ : (head + 1) * TQ]
                gq_acc[at, :] += mine * picks[r][0]
                after = slice(B + head * HEAD_DIM, B + (head + 1) * HEAD_DIM)
                gq_acc[after, :] += mine * picks[r][1]
        for peer in peers:
            q1_copy(*peer).start()

    def query_sums():
        total = gq_acc[pl.ds(pl.multiple_of(p * piece, piece), piece), :]
        for dy, dx in peers:
            there = dy * 4 + dx
            pltpu.make_async_remote_copy(
                src_ref=gq_recv.at[there],
                dst_ref=gq_recv.at[there],
                send_sem=q1_ssem.at[there],
                recv_sem=q1_rsem.at[there],
                device_id=on_psg(dy, dx),
                device_id_type=MESH,
            ).wait_recv()
            total = total + gq_recv[there]
        gq_own[...] = total.astype(BF16)
        for peer in peers:
            q2_copy(*peer).start()
        gq_full[p] = gq_own[...]

    def query_end():
        for peer in peers:
            q2_wait(*peer)
        out_copy(gq_full, gq_out, 8).start()

    def gather_sent(r, carry):
        for number in range(15):
            gather_copy((0, 0), (0, 0), r, number, sibling).wait_send()
        return carry

    def sent():
        lax.fori_loop(0, PASSAGES_HERE, gather_sent, 0)
        for peer in peers:
            stat_copy(*peer).wait_send()
            q1_copy(*peer).wait_send()
            q2_copy(*peer).wait_send()
        for number in range(len(ITEMS) - 1):
            sibling_copy(number).wait_send()

    sibling_item(0)
    lax.fori_loop(2, 4, gradients, 0)
    for number in range(len(ITEMS)):
        if number == 14:
            query_end()
            sent()
            over_head.finish(EARLIER)
            over_psg.finish(EARLIER)
        psg_item(number)
        if number + 1 < len(ITEMS):
            sibling_item(number + 1)
        head_item(number)
        if number == 2:
            query_terms()
        if number == 8:
            query_sums()

    sibling_copy(len(ITEMS) - 1).wait_send()
    over_head.finish(LAST)
    over_psg.finish(LAST)
    over_head.finish_y()
    over_psg.finish_y()
    for r in range(PASSAGES_HERE):
        out_copy(gm_own.at[pl.ds(r * B, B)], gm_out.at[pl.ds(r * B, B)], r).wait()
        out_copy(gw_own.at[r], gw_out.at[r], 4 + r).wait()
    out_copy(gq_full, gq_out, 8).wait()


def epilogue(gq_in, gm_in, gw_in, gq_out, gm_out, gwk_out, gwv_out):
    gm_out[...] = gm_in[...]
    for r in range(4):
        out = gwk_out if r < 2 else gwv_out
        half = r % 2
        out[half * B : (half + 1) * B, :] = gw_in[r].T
    for question in range(2):
        turned = jnp.concatenate([gq_in[question * 4 + k] for k in range(4)], axis=0)
        gq_out[question * TQ : (question + 1) * TQ, :] = turned.astype(F32).T.astype(BF16)


def on_device(queries, memory, lengths, owner, w_key, w_value, grad_context):
    rows, width = memory.shape[0], w_key.shape[0]
    vmem = pl.BlockSpec(memory_space=pltpu.VMEM)
    smem = pl.BlockSpec(memory_space=pltpu.SMEM)
    anywhere = pl.BlockSpec(memory_space=pl.ANY)
    dma = pltpu.SemaphoreType.DMA
    half = 2 * B
    outs = pl.pallas_call(
        kernel,
        out_shape=(
            jax.ShapeDtypeStruct((8, 2 * B // 8, TQ), BF16),
            jax.ShapeDtypeStruct((rows, B), BF16),
            jax.ShapeDtypeStruct((4, B, B), F32),
        ),
        in_specs=[smem, smem] + [anywhere] * 5,
        out_specs=[anywhere] * 3,
        scratch_shapes=[
            pltpu.VMEM((2 * TQ, B), BF16),
            pltpu.VMEM((2 * TQ, B), BF16),
            pltpu.VMEM((rows, B), BF16),
            pltpu.VMEM((4, B, B), F32),
            pltpu.VMEM((rows, width), BF16),
            pltpu.VMEM((width, 2 * B), BF16),
            pltpu.VMEM((2, PAIRS, B), BF16),
            pltpu.VMEM((2, PAIRS, B), BF16),
            pltpu.VMEM((2, B, PAIRS), BF16),
            pltpu.VMEM((2, B, PAIRS), BF16),
            pltpu.VMEM((rows, 2 * B), F32),
            pltpu.VMEM((PASSAGES_HERE, B, B), BF16),
            pltpu.VMEM((PASSAGES_HERE, LEN, PAIRS), F32),
            pltpu.VMEM((PASSAGES_HERE, LEN, PAIRS), F32),
            pltpu.VMEM((PASSAGES_HERE, 8, PAIRS), F32),
            pltpu.VMEM((8, PAIRS), F32),
            pltpu.VMEM((8, 8, PAIRS), F32),
            pltpu.VMEM((rows, 2 * B), BF16),
            pltpu.VMEM((2 * B, rows), BF16),
            pltpu.VMEM((PASSAGES_HERE, LEN, PAIRS), BF16),
            pltpu.VMEM((16, half, B), BF16),
            pltpu.VMEM((16, half, B), BF16),
            pltpu.VMEM((12, half, B), BF16),
            pltpu.VMEM((12, half, B), BF16),
            pltpu.VMEM((2, half, B), BF16),
            pltpu.VMEM((2, half, B), BF16),
            pltpu.VMEM((12, half, B), BF16),
            pltpu.VMEM((12, half, B), BF16),
            pltpu.VMEM((2, half, B), BF16),
            pltpu.VMEM((2, half, B), BF16),
            pltpu.VMEM((2 * B, TQ), F32),
            pltpu.VMEM((8, 2 * B // 8, TQ), F32),
            pltpu.VMEM((2 * B // 8, TQ), BF16),
            pltpu.VMEM((8, 2 * B // 8, TQ), BF16),
            dma, dma((32,)), dma((2,)), dma((9,)),
            dma((15, 4)), dma((16, 4)),
            dma((8,)), dma((8,)),
            dma((16,)), dma((16,)),
            dma((12, 2)), dma((12, 2)), dma((2,)), dma((2,)),
            dma((12, 2)), dma((12, 2)), dma((2,)), dma((2,)),
            dma((8,)), dma((8,)), dma((8,)), dma((8,)),
        ],
        compiler_params=pltpu.CompilerParams(
            collective_id=0, has_side_effects=True, vmem_limit_bytes=60 * 2**20
        ),
        name="whole",
    )(lengths, owner, queries, grad_context, memory, w_key, w_value)
    gq, gm, gwk, gwv = pl.pallas_call(
        epilogue,
        out_shape=(
            jax.ShapeDtypeStruct((2 * TQ, B), BF16),
            jax.ShapeDtypeStruct((rows, B), BF16),
            jax.ShapeDtypeStruct((half, B), F32),
            jax.ShapeDtypeStruct((half, B), F32),
        ),
        in_specs=[vmem] * 3,
        out_specs=[vmem] * 4,
        name="turn",
    )(*outs)
    return gq, gm, gwk, gwv


def solution(mesh):
    in_specs = (
        P(None, "head"),
        P("psg", "head"),
        P("psg"),
        P("psg"),
        P(None, "head"),
        P(None, "head"),
        P(None, "head"),
    )
    out_specs = (P(None, "head"), P("psg", "head"), P("psg", "head"), P("psg", "head"))
    return jax.shard_map(
        on_device, mesh=mesh, in_specs=in_specs, out_specs=out_specs, check_vma=False
    )
```

```python
import jax
import jax.numpy as jnp
from jax import lax
from jax.experimental import pallas as pl
from jax.experimental.pallas import tpu as pltpu
from jax.sharding import PartitionSpec as P

HEAD_DIM = 64
LEN = 256
TQ = 128
HEADS_HERE = 4
PASSAGES_HERE = 4
B = 256
PAIRS = HEADS_HERE * TQ
MESH = pl.DeviceIdType.MESH
FILL = -1e30
F32 = jnp.float32
BF16 = jnp.bfloat16

PLACES = ((0, 0), (0, 1), (0, 3), (1, 0), (0, 2), (1, 2), (1, 1), (1, 3))
SLOT = {place: slot for slot, place in enumerate(PLACES)}


def is_equal(a, k):
    return 1 - ((a - k) * (a - k) + 48) // 49


def slot_of(dy, dz):
    code = dy * 4 + dz
    total = 0
    for (py, pz), slot in SLOT.items():
        total = total + slot * is_equal(code, py * 4 + pz)
    return total


def nt(a, b):
    return lax.dot_general(a, b, (((1,), (1,)), ((), ())), preferred_element_type=F32)


def nn(a, b):
    return jnp.dot(a, b, preferred_element_type=F32)


class Scatter:
    def __init__(self, send, recv, ysend, yrecv, ssem, rsem, yssem, yrsem, following, before, partner):
        self.send, self.recv, self.ysend, self.yrecv = send, recv, ysend, yrecv
        self.ssem, self.rsem, self.yssem, self.yrsem = ssem, rsem, yssem, yrsem
        self.following, self.before, self.partner = following, before, partner

    def half(self, ref, index, way):
        return ref.at[index, pl.ds(way * B, B)]

    def copy(self, index, way):
        return pltpu.make_async_remote_copy(
            src_ref=self.half(self.send, index, way),
            dst_ref=self.half(self.recv, index, way),
            send_sem=self.ssem.at[index, way],
            recv_sem=self.rsem.at[index, way],
            device_id=self.before if way else self.following,
            device_id_type=MESH,
        )

    def ycopy(self, u):
        return pltpu.make_async_remote_copy(
            src_ref=self.ysend.at[u],
            dst_ref=self.yrecv.at[u],
            send_sem=self.yssem.at[u],
            recv_sem=self.yrsem.at[u],
            device_id=self.partner,
            device_id_type=MESH,
        )

    def arrived(self, index, way):
        return self.recv[index, way * B : (way + 1) * B, :].astype(F32)

    def item(self, kind, dy, u, own, store):
        first = (dy * 2 + u) * 3
        if kind == "D":
            mine = [own(0, way * 2 + u, way) for way in (0, 1)]
            for way in (0, 1):
                self.copy(first + 1, way).wait_recv()
                self.copy(first + 2, way).wait_recv()
            if dy == 0:
                self.ycopy(u).wait_recv()
            for way in (0, 1):
                value = mine[way] + self.arrived(first + 2, way) + self.arrived(first + 1, 1 - way)
                if dy == 1:
                    self.ysend[u, way * B : (way + 1) * B, :] = value.astype(BF16)
                else:
                    value = value + self.yrecv[u, way * B : (way + 1) * B, :].astype(F32)
                    store(way * 2 + u, value)
            if dy == 1:
                self.ycopy(u).start()
            return
        index = first + "ABC".index(kind)
        for way in (0, 1):
            dz, r = chunk_of(kind, u, way)
            value = own(dz, r, way)
            if kind == "C":
                self.copy(first, way).wait_recv()
                value = value + self.arrived(first, way)
            self.send[index, way * B : (way + 1) * B, :] = value.astype(BF16)
            self.copy(index, way).start()

    def finish(self, indices):
        for index in indices:
            for way in (0, 1):
                self.copy(index, way).wait_send()

    def finish_y(self):
        for u in (0, 1):
            self.ycopy(u).wait_send()


def chunk_of(kind, u, way):
    if kind == "A":
        return 2, way * 2 + u
    if kind == "B":
        return (3, u) if way else (1, 2 + u)
    if kind == "C":
        return (3, 2 + u) if way else (1, u)
    return 0, way * 2 + u


ITEMS = (
    ("A", 1, 0), ("B", 1, 0), ("C", 1, 0), ("A", 1, 1), ("B", 1, 1), ("D", 1, 0),
    ("C", 1, 1), ("A", 0, 0), ("B", 0, 0), ("D", 1, 1), ("C", 0, 0), ("A", 0, 1),
    ("B", 0, 1), ("C", 0, 1), ("D", 0, 0), ("D", 0, 1),
)
LAST = (4, 5)
EARLIER = tuple(index for index in range(12) if index not in LAST)


def kernel(
    len_ref, own_ref, q_in, c_in, mem_ref, wk_ref, wv_ref,
    gq_out, gm_out, gw_out,
    q_ref, c_ref, gm_own, gw_own, fm, w, qa, ca, qat, cat, acc, kt, e_ref, gp_ref, stat, sl, sall, g, gt, gs,
    sib_send, sib_recv, m_send, m_recv, my_send, my_recv, w_send, w_recv, wy_send, wy_recv,
    gq_acc, gq_send, gq_recv, gq_own, gq_full,
    mem_sem, w_sem, qc_sem, out_sem, ag_ssem, ag_rsem, st_ssem, st_rsem, sib_ssem, sib_rsem,
    m_ssem, m_rsem, my_ssem, my_rsem, w_ssem, w_rsem, wy_ssem, wy_rsem,
    q1_ssem, q1_rsem, q2_ssem, q2_rsem,
):
    p, h = lax.axis_index("psg"), lax.axis_index("head")
    yl, x = p // 4, p % 4
    yh, z, core = h // 8, (h // 2) % 4, h % 2

    def head_at(dy, dz, dc=0):
        return ((yh + dy) % 2) * 8 + ((z + dz) % 4) * 2 + (core + dc) % 2

    def psg_at(dy, dx):
        return ((yl + dy) % 2) * 4 + (x + dx) % 4

    def on_head(dy, dz, dc=0):
        return (p, head_at(dy, dz, dc))

    def on_psg(dy, dx):
        return (psg_at(dy, dx), h)

    up, down, across, sibling = on_head(0, 1), on_head(0, 3), on_head(1, 0), on_head(0, 0, 1)
    peers = [(k // 4, k % 4) for k in range(1, 8)]

    mem_copy = pltpu.make_async_copy(mem_ref, fm.at[:, pl.ds(0, B)], mem_sem)
    mem_copy.start()
    q_copies = [
        pltpu.make_async_copy(q_in, q_ref, qc_sem.at[0]),
        pltpu.make_async_copy(c_in, c_ref, qc_sem.at[1]),
    ]
    for copy in q_copies:
        copy.start()
    barrier = pltpu.get_barrier_semaphore()
    partners = [on_psg(*peer) for peer in reversed(peers)] + [across, up, down, sibling]
    for device in partners:
        pl.semaphore_signal(barrier, inc=1, device_id=device, device_id_type=MESH)
    pl.semaphore_wait(barrier, len(partners))

    def block(slot, dc, r):
        return fm.at[pl.ds(r * B, B), pl.ds((slot * 2 + dc) * B, B)]

    def gather_copy(source, target, r, number, device):
        return pltpu.make_async_remote_copy(
            src_ref=block(source[0], source[1], r),
            dst_ref=block(target[0], target[1], r),
            send_sem=ag_ssem.at[number, r],
            recv_sem=ag_rsem.at[target[0] * 2 + target[1], r],
            device_id=device,
            device_id_type=MESH,
        )

    def gathered(slot, dc, r):
        gather_copy((slot, dc), (slot, dc), r, 0, sibling).wait_recv()

    def to_sibling(slot, r):
        gather_copy((slot, 0), (slot, 1), r, 4 + slot, sibling).start()

    def own_copy(target, r, number, device):
        return pltpu.make_async_remote_copy(
            src_ref=mem_ref.at[pl.ds(r * B, B)],
            dst_ref=block(target, 0, r),
            send_sem=ag_ssem.at[number, r],
            recv_sem=ag_rsem.at[target * 2, r],
            device_id=device,
            device_id_type=MESH,
        )

    def own_along(k):
        own_copy(SLOT[0, 3], k, 0, up).start()
        own_copy(SLOT[0, 1], (k + 2) % 4, 1, down).start()

    own_along(0)
    own_along(1)
    for k in range(PASSAGES_HERE):
        own_copy(SLOT[1, 0], k % 2 * 2 + k // 2, 2, across).start()
    mem_copy.wait()
    for r in range(PASSAGES_HERE):
        to_sibling(0, r)
    w_copies = []
    for slot, (dy, dz) in enumerate(PLACES):
        for dc in (0, 1):
            rows = pl.ds(pl.multiple_of(head_at(dy, dz, dc) * B, B), B)
            into = pl.ds((slot * 2 + dc) * B, B)
            for part, ref in enumerate((wk_ref, wv_ref)):
                w_copies.append(
                    pltpu.make_async_copy(
                        ref.at[rows, :],
                        w.at[into, pl.ds(part * B, B)],
                        w_sem.at[(slot * 2 + dc) * 2 + part],
                    )
                )
                w_copies[-1].start()

    def opposite(r):
        gathered(SLOT[0, 2], 0, r)
        gather_copy((SLOT[0, 2], 0), (SLOT[1, 2], 0), r, 14, across).start()
        to_sibling(SLOT[0, 2], r)

    def partner(r):
        gathered(SLOT[1, 0], 0, r)
        gather_copy((SLOT[1, 0], 0), (SLOT[1, 3], 0), r, 12, up).start()
        gather_copy((SLOT[1, 0], 0), (SLOT[1, 1], 0), r, 13, down).start()
        to_sibling(SLOT[1, 0], r)

    for r in (0, 1):
        gathered(SLOT[0, 3], 0, r)
        gather_copy((SLOT[0, 3], 0), (SLOT[0, 2], 0), r, 3, up).start()
        gathered(SLOT[0, 1], 0, 2 + r)
        gather_copy((SLOT[0, 1], 0), (SLOT[0, 2], 0), 2 + r, 3, down).start()
        own_along(2 + r)
        to_sibling(SLOT[0, 3], r)
        to_sibling(SLOT[0, 1], 2 + r)
    for r in (0, 1):
        partner(r)
        partner(2 + r)
        opposite(r)
        opposite(2 + r)

    lane = lax.broadcasted_iota(jnp.int32, (TQ, B), 1) // HEAD_DIM
    row = lax.broadcasted_iota(jnp.int32, (B, TQ), 0) // HEAD_DIM
    for copy in q_copies:
        copy.wait()
    for source, plain, turned in ((q_ref, qa, qat), (c_ref, ca, cat)):
        for question in range(2):
            mine = source[question * TQ : (question + 1) * TQ, :].astype(F32)
            mine_t = mine.T
            for head in range(HEADS_HERE):
                at = slice(head * TQ, (head + 1) * TQ)
                plain[question, at, :] = jnp.where(lane == head, mine, 0.0).astype(BF16)
                turned[question, :, at] = jnp.where(row == head, mine_t, 0.0).astype(BF16)

    def rows_of(r):
        return pl.ds(pl.multiple_of(r * B, B), B)

    def passage(k):
        return k % 2 * 2 + k // 2

    for r in (0, 1):
        gathered(SLOT[0, 1], 0, r)
        to_sibling(SLOT[0, 1], r)
        gathered(SLOT[0, 3], 0, 2 + r)
        to_sibling(SLOT[0, 3], 2 + r)

    for copy in w_copies[:16]:
        copy.wait()

    def first_part(k, carry):
        r = passage(k)
        for slot in range(4):
            gathered(slot, 1, r)
        acc[rows_of(r), :] = nn(fm[rows_of(r), 0 : 8 * B], w[0 : 8 * B, :])
        return carry

    lax.fori_loop(0, PASSAGES_HERE, first_part, 0)

    for copy in w_copies[16:]:
        copy.wait()

    def second_part(k, carry):
        @pl.when(k < PASSAGES_HERE)
        def _():
            r = passage(k)
            for slot in (SLOT[1, 2], SLOT[1, 1], SLOT[1, 3]):
                gathered(slot, 0, r)
                to_sibling(slot, r)
            gathered(SLOT[0, 2], 1, r)
            gathered(SLOT[1, 2], 1, r)
            acc[rows_of(r), :] += nn(fm[rows_of(r), 8 * B : 12 * B], w[8 * B : 12 * B, :])

        @pl.when(k > 0)
        def _():
            attend(passage(k - 1))

        return carry

    def attend(r):
        for slot in (SLOT[1, 1], SLOT[1, 3]):
            gathered(slot, 1, r)
        both = acc[rows_of(r), :] + nn(fm[rows_of(r), 12 * B :], w[12 * B :, :])
        keys, values = both[:, :B], both[:, B:].astype(BF16)
        kt[r] = keys.T.astype(BF16)
        keys = keys.astype(BF16)
        question = own_ref[r]
        scores = nt(keys, qa[question])
        flows = nt(values, ca[question])
        alive = lax.broadcasted_iota(jnp.int32, (LEN, PAIRS), 0) < len_ref[r]
        masked = jnp.where(alive, scores, FILL)
        top = jnp.max(masked, axis=0, keepdims=True)
        shifted = jnp.where(alive, jnp.exp(masked - top), 0.0)
        e_ref[r] = shifted
        gp_ref[r] = flows
        stat[r, 0:1, :] = top
        stat[r, 1:2, :] = jnp.sum(shifted, axis=0, keepdims=True)
        stat[r, 2:3, :] = jnp.sum(shifted * flows, axis=0, keepdims=True)

    lax.fori_loop(0, PASSAGES_HERE + 1, second_part, 0)

    picks = []
    for r in range(PASSAGES_HERE):
        second = own_ref[r].astype(F32)
        picks.append((1.0 - second, second))
    for question in range(2):
        tops = [
            stat[r, 0:1, :] * picks[r][question] + FILL * (1.0 - picks[r][question])
            for r in range(PASSAGES_HERE)
        ]
        top = jnp.maximum(jnp.maximum(tops[0], tops[1]), jnp.maximum(tops[2], tops[3]))
        mass = jnp.zeros((1, PAIRS), F32)
        flow = jnp.zeros((1, PAIRS), F32)
        for r in range(PASSAGES_HERE):
            scale = jnp.exp(tops[r] - top) * picks[r][question]
            mass += stat[r, 1:2, :] * scale
            flow += stat[r, 2:3, :] * scale
        sl[question : question + 1, :] = top
        sl[2 + question : 3 + question, :] = mass
        sl[4 + question : 5 + question, :] = flow
    sl[6:8, :] = jnp.zeros((2, PAIRS), F32)

    def seen_by(dy, dx):
        return dy * 4 + (4 - dx) % 4

    def stat_copy(dy, dx):
        there = seen_by(dy, dx)
        return pltpu.make_async_remote_copy(
            src_ref=sl,
            dst_ref=sall.at[there],
            send_sem=st_ssem.at[dy * 4 + dx],
            recv_sem=st_rsem.at[there],
            device_id=on_psg(dy, dx),
            device_id_type=MESH,
        )

    for peer in peers:
        stat_copy(*peer).start()
    for peer in peers:
        stat_copy(*peer).wait_recv()
    sall[0] = sl[...]
    totals = []
    for question in range(2):
        tops = [sall[k, question : question + 1, :] for k in range(8)]
        top = tops[0]
        for other in tops[1:]:
            top = jnp.maximum(top, other)
        mass = jnp.zeros((1, PAIRS), F32)
        flow = jnp.zeros((1, PAIRS), F32)
        for k in range(8):
            scale = jnp.exp(tops[k] - top)
            mass += sall[k, 2 + question : 3 + question, :] * scale
            flow += sall[k, 4 + question : 5 + question, :] * scale
        totals.append((top, 1.0 / mass, flow / mass))
    for r in range(PASSAGES_HERE):
        top, inverse, shift = (
            totals[0][k] * picks[r][0] + totals[1][k] * picks[r][1] for k in range(3)
        )
        stat[r, 3:4, :] = jnp.exp(stat[r, 0:1, :] - top) * inverse
        stat[r, 4:5, :] = shift

    def gradients(k, carry):
        r = passage(k)
        question = own_ref[r]
        probs = e_ref[r] * stat[r, 3:4, :]
        grad = (probs * (gp_ref[r] - stat[r, 4:5, :])).astype(BF16)
        probs = probs.astype(BF16)
        gs[r] = grad
        g[rows_of(r), 0:B] = nn(grad, qa[question]).astype(BF16)
        g[rows_of(r), B : 2 * B] = nn(probs, ca[question]).astype(BF16)
        gt[0:B, rows_of(r)] = nt(qat[question], grad).astype(BF16)
        gt[B : 2 * B, rows_of(r)] = nt(cat[question], probs).astype(BF16)
        return carry

    lax.fori_loop(0, 2, gradients, 0)

    over_head = Scatter(
        m_send, m_recv, my_send, my_recv, m_ssem, m_rsem, my_ssem, my_rsem, up, down, across
    )
    over_psg = Scatter(
        w_send, w_recv, wy_send, wy_recv, w_ssem, w_rsem, wy_ssem, wy_rsem,
        on_psg(0, 1), on_psg(0, 3), on_psg(1, 0),
    )

    def out_copy(source, target, number):
        return pltpu.make_async_copy(source, target, out_sem.at[number])

    def part(slot, dc, r):
        at = (slot * 2 + dc) * B
        return nt(g[r * B : (r + 1) * B, :], w[at : at + B, :]).astype(BF16)

    def sibling_copy(number):
        return pltpu.make_async_remote_copy(
            src_ref=sib_send.at[number],
            dst_ref=sib_recv.at[number],
            send_sem=sib_ssem.at[number],
            recv_sem=sib_rsem.at[number],
            device_id=sibling,
            device_id_type=MESH,
        )

    def sibling_item(number):
        kind, dy, u = ITEMS[number]
        for way in (0, 1):
            dz, r = chunk_of(kind, u, way)
            sib_send[number, way * B : (way + 1) * B, :] = part(SLOT[dy, dz], 1, r)
        sibling_copy(number).start()

    def head_item(number):
        kind, dy, u = ITEMS[number]
        sibling_copy(number).wait_recv()

        def own(dz, r, way):
            other = sib_recv[number, way * B : (way + 1) * B, :].astype(F32)
            return part(SLOT[dy, dz], 0, r).astype(F32) + other

        def store(r, value):
            gm_own[r * B : (r + 1) * B, :] = value.astype(BF16)
            out_copy(gm_own.at[pl.ds(r * B, B)], gm_out.at[pl.ds(r * B, B)], r).start()

        over_head.item(kind, dy, u, own, store)

    def psg_item(number):
        kind, dy, u = ITEMS[number]

        def own(dx, r, way):
            kv, half = r // 2, r % 2
            slot = slot_of((yl + dy + 2 - yh) % 2, (x + dx + 4 - z) % 4)
            column = (slot * 2 + (half + 2 - core) % 2) * B
            return nn(gt[kv * B : (kv + 1) * B, :], fm[:, pl.ds(pl.multiple_of(column, B), B)])

        def store(r, value):
            gw_own[r] = value
            out_copy(gw_own.at[r], gw_out.at[r], 4 + r).start()

        over_psg.item(kind, dy, u, own, store)

    piece = 2 * B // 8

    def q1_copy(dy, dx):
        there = seen_by(dy, dx)
        start = pl.multiple_of(psg_at(dy, dx) * piece, piece)
        return pltpu.make_async_remote_copy(
            src_ref=gq_send.at[pl.ds(start, piece)],
            dst_ref=gq_recv.at[there],
            send_sem=q1_ssem.at[dy * 4 + dx],
            recv_sem=q1_rsem.at[there],
            device_id=on_psg(dy, dx),
            device_id_type=MESH,
        )

    def q2_copy(dy, dx):
        return pltpu.make_async_remote_copy(
            src_ref=gq_own,
            dst_ref=gq_full.at[p],
            send_sem=q2_ssem.at[dy * 4 + dx],
            recv_sem=q2_rsem.at[seen_by(dy, dx)],
            device_id=on_psg(dy, dx),
            device_id_type=MESH,
        )

    def q2_wait(dy, dx):
        pltpu.make_async_remote_copy(
            src_ref=gq_own,
            dst_ref=gq_full.at[psg_at(dy, dx)],
            send_sem=q2_ssem.at[dy * 4 + dx],
            recv_sem=q2_rsem.at[dy * 4 + dx],
            device_id=on_psg(dy, dx),
            device_id_type=MESH,
        ).wait_recv()

    def query_terms():
        gq_acc[...] = jnp.zeros((2 * B, TQ), F32)
        for r in range(PASSAGES_HERE):
            term = nn(kt[r], gs[r])
            for head in range(HEADS_HERE):
                at = slice(head * HEAD_DIM, (head + 1) * HEAD_DIM)
                mine = term[at, head * TQ : (head + 1) * TQ]
                gq_acc[at, :] += mine * picks[r][0]
                after = slice(B + head * HEAD_DIM, B + (head + 1) * HEAD_DIM)
                gq_acc[after, :] += mine * picks[r][1]
        gq_send[...] = gq_acc[...].astype(BF16)
        for peer in peers:
            q1_copy(*peer).start()

    def query_sums():
        total = gq_acc[pl.ds(pl.multiple_of(p * piece, piece), piece), :]
        for dy, dx in peers:
            there = dy * 4 + dx
            pltpu.make_async_remote_copy(
                src_ref=gq_recv.at[there],
                dst_ref=gq_recv.at[there],
                send_sem=q1_ssem.at[there],
                recv_sem=q1_rsem.at[there],
                device_id=on_psg(dy, dx),
                device_id_type=MESH,
            ).wait_recv()
            total = total + gq_recv[there].astype(F32)
        gq_own[...] = total.astype(BF16)
        for peer in peers:
            q2_copy(*peer).start()
        gq_full[p] = gq_own[...]

    def query_end():
        for peer in peers:
            q2_wait(*peer)
        out_copy(gq_full, gq_out, 8).start()

    def gather_sent(r, carry):
        for number in range(15):
            gather_copy((0, 0), (0, 0), r, number, sibling).wait_send()
        return carry

    def sent():
        lax.fori_loop(0, PASSAGES_HERE, gather_sent, 0)
        for peer in peers:
            stat_copy(*peer).wait_send()
            q1_copy(*peer).wait_send()
            q2_copy(*peer).wait_send()
        for number in range(len(ITEMS) - 1):
            sibling_copy(number).wait_send()

    sibling_item(0)
    lax.fori_loop(2, 4, gradients, 0)
    for number in range(len(ITEMS)):
        if number == 14:
            query_end()
            sent()
            over_head.finish(EARLIER)
            over_psg.finish(EARLIER)
        psg_item(number)
        if number + 1 < len(ITEMS):
            sibling_item(number + 1)
        head_item(number)
        if number == 2:
            query_terms()
        if number == 8:
            query_sums()

    sibling_copy(len(ITEMS) - 1).wait_send()
    over_head.finish(LAST)
    over_psg.finish(LAST)
    over_head.finish_y()
    over_psg.finish_y()
    for r in range(PASSAGES_HERE):
        out_copy(gm_own.at[pl.ds(r * B, B)], gm_out.at[pl.ds(r * B, B)], r).wait()
        out_copy(gw_own.at[r], gw_out.at[r], 4 + r).wait()
    out_copy(gq_full, gq_out, 8).wait()


def epilogue(gq_in, gm_in, gw_in, gq_out, gm_out, gwk_out, gwv_out):
    gm_out[...] = gm_in[...]
    for r in range(4):
        out = gwk_out if r < 2 else gwv_out
        half = r % 2
        out[half * B : (half + 1) * B, :] = gw_in[r].T
    for question in range(2):
        turned = jnp.concatenate([gq_in[question * 4 + k] for k in range(4)], axis=0)
        gq_out[question * TQ : (question + 1) * TQ, :] = turned.astype(F32).T.astype(BF16)


def on_device(queries, memory, lengths, owner, w_key, w_value, grad_context):
    rows, width = memory.shape[0], w_key.shape[0]
    vmem = pl.BlockSpec(memory_space=pltpu.VMEM)
    smem = pl.BlockSpec(memory_space=pltpu.SMEM)
    anywhere = pl.BlockSpec(memory_space=pl.ANY)
    dma = pltpu.SemaphoreType.DMA
    half = 2 * B
    outs = pl.pallas_call(
        kernel,
        out_shape=(
            jax.ShapeDtypeStruct((8, 2 * B // 8, TQ), BF16),
            jax.ShapeDtypeStruct((rows, B), BF16),
            jax.ShapeDtypeStruct((4, B, B), F32),
        ),
        in_specs=[smem, smem] + [anywhere] * 5,
        out_specs=[anywhere] * 3,
        scratch_shapes=[
            pltpu.VMEM((2 * TQ, B), BF16),
            pltpu.VMEM((2 * TQ, B), BF16),
            pltpu.VMEM((rows, B), BF16),
            pltpu.VMEM((4, B, B), F32),
            pltpu.VMEM((rows, width), BF16),
            pltpu.VMEM((width, 2 * B), BF16),
            pltpu.VMEM((2, PAIRS, B), BF16),
            pltpu.VMEM((2, PAIRS, B), BF16),
            pltpu.VMEM((2, B, PAIRS), BF16),
            pltpu.VMEM((2, B, PAIRS), BF16),
            pltpu.VMEM((rows, 2 * B), F32),
            pltpu.VMEM((PASSAGES_HERE, B, B), BF16),
            pltpu.VMEM((PASSAGES_HERE, LEN, PAIRS), F32),
            pltpu.VMEM((PASSAGES_HERE, LEN, PAIRS), F32),
            pltpu.VMEM((PASSAGES_HERE, 8, PAIRS), F32),
            pltpu.VMEM((8, PAIRS), F32),
            pltpu.VMEM((8, 8, PAIRS), F32),
            pltpu.VMEM((rows, 2 * B), BF16),
            pltpu.VMEM((2 * B, rows), BF16),
            pltpu.VMEM((PASSAGES_HERE, LEN, PAIRS), BF16),
            pltpu.VMEM((16, half, B), BF16),
            pltpu.VMEM((16, half, B), BF16),
            pltpu.VMEM((12, half, B), BF16),
            pltpu.VMEM((12, half, B), BF16),
            pltpu.VMEM((2, half, B), BF16),
            pltpu.VMEM((2, half, B), BF16),
            pltpu.VMEM((12, half, B), BF16),
            pltpu.VMEM((12, half, B), BF16),
            pltpu.VMEM((2, half, B), BF16),
            pltpu.VMEM((2, half, B), BF16),
            pltpu.VMEM((2 * B, TQ), F32),
            pltpu.VMEM((2 * B, TQ), BF16),
            pltpu.VMEM((8, 2 * B // 8, TQ), BF16),
            pltpu.VMEM((2 * B // 8, TQ), BF16),
            pltpu.VMEM((8, 2 * B // 8, TQ), BF16),
            dma, dma((32,)), dma((2,)), dma((9,)),
            dma((15, 4)), dma((16, 4)),
            dma((8,)), dma((8,)),
            dma((16,)), dma((16,)),
            dma((12, 2)), dma((12, 2)), dma((2,)), dma((2,)),
            dma((12, 2)), dma((12, 2)), dma((2,)), dma((2,)),
            dma((8,)), dma((8,)), dma((8,)), dma((8,)),
        ],
        compiler_params=pltpu.CompilerParams(
            collective_id=0, has_side_effects=True, vmem_limit_bytes=60 * 2**20
        ),
        name="whole",
    )(lengths, owner, queries, grad_context, memory, w_key, w_value)
    gq, gm, gwk, gwv = pl.pallas_call(
        epilogue,
        out_shape=(
            jax.ShapeDtypeStruct((2 * TQ, B), BF16),
            jax.ShapeDtypeStruct((rows, B), BF16),
            jax.ShapeDtypeStruct((half, B), F32),
            jax.ShapeDtypeStruct((half, B), F32),
        ),
        in_specs=[vmem] * 3,
        out_specs=[vmem] * 4,
        name="turn",
    )(*outs)
    return gq, gm, gwk, gwv


def solution(mesh):
    in_specs = (
        P(None, "head"),
        P("psg", "head"),
        P("psg"),
        P("psg"),
        P(None, "head"),
        P(None, "head"),
        P(None, "head"),
    )
    out_specs = (P(None, "head"), P("psg", "head"), P("psg", "head"), P("psg", "head"))
    return jax.shard_map(
        on_device, mesh=mesh, in_specs=in_specs, out_specs=out_specs, check_vma=False
    )
```

```python
import jax
import jax.numpy as jnp
from jax import lax
from jax.experimental import pallas as pl
from jax.experimental.pallas import tpu as pltpu
from jax.sharding import PartitionSpec as P

HEAD_DIM = 64
LEN = 256
TQ = 128
HEADS_HERE = 4
PASSAGES_HERE = 4
B = 256
PAIRS = HEADS_HERE * TQ
MESH = pl.DeviceIdType.MESH
FILL = -1e30
F32 = jnp.float32
BF16 = jnp.bfloat16

PLACES = ((0, 0), (0, 1), (0, 3), (1, 0), (0, 2), (1, 2), (1, 1), (1, 3))
SLOT = {place: slot for slot, place in enumerate(PLACES)}


def is_equal(a, k):
    return 1 - ((a - k) * (a - k) + 48) // 49


def slot_of(dy, dz):
    code = dy * 4 + dz
    total = 0
    for (py, pz), slot in SLOT.items():
        total = total + slot * is_equal(code, py * 4 + pz)
    return total


def nt(a, b):
    return lax.dot_general(a, b, (((1,), (1,)), ((), ())), preferred_element_type=F32)


def nn(a, b):
    return jnp.dot(a, b, preferred_element_type=F32)


class Scatter:
    def __init__(self, pair_first, send, recv, ysend, yrecv, ssem, rsem, yssem, yrsem, following, before, partner):
        self.pair_first = pair_first
        self.send, self.recv, self.ysend, self.yrecv = send, recv, ysend, yrecv
        self.ssem, self.rsem, self.yssem, self.yrsem = ssem, rsem, yssem, yrsem
        self.following, self.before, self.partner = following, before, partner

    def half(self, ref, index, way):
        return ref.at[index, pl.ds(way * B, B)]

    def copy(self, index, way):
        return pltpu.make_async_remote_copy(
            src_ref=self.half(self.send, index, way),
            dst_ref=self.half(self.recv, index, way),
            send_sem=self.ssem.at[index, way],
            recv_sem=self.rsem.at[index, way],
            device_id=self.before if way else self.following,
            device_id_type=MESH,
        )

    def first_copy(self):
        return pltpu.make_async_remote_copy(
            src_ref=self.send.at[FIRST],
            dst_ref=self.recv.at[FIRST],
            send_sem=self.ssem.at[FIRST, 0],
            recv_sem=self.rsem.at[FIRST, 0],
            device_id=self.partner,
            device_id_type=MESH,
        )

    def ycopy(self, u):
        return pltpu.make_async_remote_copy(
            src_ref=self.ysend.at[u],
            dst_ref=self.yrecv.at[u],
            send_sem=self.yssem.at[u],
            recv_sem=self.yrsem.at[u],
            device_id=self.partner,
            device_id_type=MESH,
        )

    def arrived(self, index, way):
        return self.recv[index, way * B : (way + 1) * B, :].astype(F32)

    def item(self, kind, dy, u, own, store):
        first = (dy * 2 + u) * 3
        if kind == "D":
            mine = [own(0, way * 2 + u, way) for way in (0, 1)]
            for way in (0, 1):
                self.copy(first + 1, way).wait_recv()
                self.copy(first + 2, way).wait_recv()
            if dy == 0:
                self.ycopy(u).wait_recv()
            for way in (0, 1):
                value = mine[way] + self.arrived(first + 2, way) + self.arrived(first + 1, 1 - way)
                if dy == 1:
                    self.ysend[u, way * B : (way + 1) * B, :] = value.astype(BF16)
                else:
                    value = value + self.yrecv[u, way * B : (way + 1) * B, :].astype(F32)
                    store(way * 2 + u, value)
            if dy == 1:
                self.ycopy(u).start()
            return
        index = first + "ABC".index(kind)
        if self.pair_first and index == FIRST:
            for way in (0, 1):
                dz, r = chunk_of(kind, u, way)
                self.send[index, way * B : (way + 1) * B, :] = own(dz, r, way).astype(BF16)
            self.first_copy().start()
            return
        if self.pair_first and index == 0:
            self.first_copy().wait_recv()
        for way in (0, 1):
            dz, r = chunk_of(kind, u, way)
            value = own(dz, r, way)
            if self.pair_first and index == 0:
                value = value + self.arrived(FIRST, way)
            if kind == "C" and not (self.pair_first and first == FIRST):
                self.copy(first, way).wait_recv()
                value = value + self.arrived(first, way)
            self.send[index, way * B : (way + 1) * B, :] = value.astype(BF16)
            self.copy(index, way).start()

    def finish(self, indices):
        for index in indices:
            if self.pair_first and index == FIRST:
                self.first_copy().wait_send()
                continue
            for way in (0, 1):
                self.copy(index, way).wait_send()

    def finish_y(self):
        for u in (0, 1):
            self.ycopy(u).wait_send()


def chunk_of(kind, u, way):
    if kind == "A":
        return 2, way * 2 + u
    if kind == "B":
        return (3, u) if way else (1, 2 + u)
    if kind == "C":
        return (3, 2 + u) if way else (1, u)
    return 0, way * 2 + u


ITEMS = (
    ("A", 1, 0), ("B", 1, 0), ("C", 1, 0), ("A", 1, 1), ("B", 1, 1), ("D", 1, 0),
    ("C", 1, 1), ("A", 0, 0), ("B", 0, 0), ("D", 1, 1), ("C", 0, 0), ("A", 0, 1),
    ("B", 0, 1), ("C", 0, 1), ("D", 0, 0), ("D", 0, 1),
)
FIRST = 6
LAST = (4, 5)
EARLIER = tuple(index for index in range(12) if index not in LAST)


def kernel(
    len_in, own_in, q_in, c_in, mem_ref, wk_ref, wv_ref,
    gq_out, gm_out, gw_out,
    len_ref, own_ref, q_ref, c_ref, gm_own, gw_own, fm, w, qa, ca, qat, cat, acc, kt, e_ref, gp_ref, stat, sl, sall, g, gt, gs,
    sib_send, sib_recv, m_send, m_recv, my_send, my_recv, w_send, w_recv, wy_send, wy_recv,
    gq_acc, gq_send, gq_recv, gq_own, gq_full,
    mem_sem, w_sem, qc_sem, out_sem, ag_ssem, ag_rsem, st_ssem, st_rsem, sib_ssem, sib_rsem,
    m_ssem, m_rsem, my_ssem, my_rsem, w_ssem, w_rsem, wy_ssem, wy_rsem,
    q1_ssem, q1_rsem, q2_ssem, q2_rsem,
):
    p, h = lax.axis_index("psg"), lax.axis_index("head")
    yl, x = p // 4, p % 4
    yh, z, core = h // 8, (h // 2) % 4, h % 2

    def head_at(dy, dz, dc=0):
        return ((yh + dy) % 2) * 8 + ((z + dz) % 4) * 2 + (core + dc) % 2

    def psg_at(dy, dx):
        return ((yl + dy) % 2) * 4 + (x + dx) % 4

    def on_head(dy, dz, dc=0):
        return (p, head_at(dy, dz, dc))

    def on_psg(dy, dx):
        return (psg_at(dy, dx), h)

    up, down, across, sibling = on_head(0, 1), on_head(0, 3), on_head(1, 0), on_head(0, 0, 1)
    peers = [(k // 4, k % 4) for k in range(1, 8)]

    mem_copy = pltpu.make_async_copy(mem_ref, fm.at[:, pl.ds(0, B)], mem_sem)
    mem_copy.start()
    q_copies = [
        pltpu.make_async_copy(q_in, q_ref, qc_sem.at[0]),
        pltpu.make_async_copy(c_in, c_ref, qc_sem.at[1]),
        pltpu.make_async_copy(len_in, len_ref, qc_sem.at[2]),
        pltpu.make_async_copy(own_in, own_ref, qc_sem.at[3]),
    ]
    for copy in q_copies:
        copy.start()
    barrier = pltpu.get_barrier_semaphore()
    partners = [on_psg(*peer) for peer in reversed(peers)] + [across, up, down, sibling]
    for device in partners:
        pl.semaphore_signal(barrier, inc=1, device_id=device, device_id_type=MESH)
    pl.semaphore_wait(barrier, len(partners))

    def block(slot, dc, r):
        return fm.at[pl.ds(r * B, B), pl.ds((slot * 2 + dc) * B, B)]

    def gather_copy(source, target, r, number, device):
        return pltpu.make_async_remote_copy(
            src_ref=block(source[0], source[1], r),
            dst_ref=block(target[0], target[1], r),
            send_sem=ag_ssem.at[number, r],
            recv_sem=ag_rsem.at[target[0] * 2 + target[1], r],
            device_id=device,
            device_id_type=MESH,
        )

    def gathered(slot, dc, r):
        gather_copy((slot, dc), (slot, dc), r, 0, sibling).wait_recv()

    def to_sibling(slot, r):
        gather_copy((slot, 0), (slot, 1), r, 4 + slot, sibling).start()

    def own_copy(target, r, number, device):
        return pltpu.make_async_remote_copy(
            src_ref=mem_ref.at[pl.ds(r * B, B)],
            dst_ref=block(target, 0, r),
            send_sem=ag_ssem.at[number, r],
            recv_sem=ag_rsem.at[target * 2, r],
            device_id=device,
            device_id_type=MESH,
        )

    def own_along(k):
        own_copy(SLOT[0, 3], k, 0, up).start()
        own_copy(SLOT[0, 1], (k + 2) % 4, 1, down).start()

    own_along(0)
    own_along(1)
    for k in range(PASSAGES_HERE):
        own_copy(SLOT[1, 0], k % 2 * 2 + k // 2, 2, across).start()
    mem_copy.wait()
    for r in range(PASSAGES_HERE):
        to_sibling(0, r)
    w_copies = []
    for slot, (dy, dz) in enumerate(PLACES):
        for dc in (0, 1):
            rows = pl.ds(pl.multiple_of(head_at(dy, dz, dc) * B, B), B)
            into = pl.ds((slot * 2 + dc) * B, B)
            for part, ref in enumerate((wk_ref, wv_ref)):
                w_copies.append(
                    pltpu.make_async_copy(
                        ref.at[rows, :],
                        w.at[into, pl.ds(part * B, B)],
                        w_sem.at[(slot * 2 + dc) * 2 + part],
                    )
                )
                w_copies[-1].start()

    def opposite(r):
        gathered(SLOT[0, 2], 0, r)
        gather_copy((SLOT[0, 2], 0), (SLOT[1, 2], 0), r, 14, across).start()
        to_sibling(SLOT[0, 2], r)

    def partner(r):
        gathered(SLOT[1, 0], 0, r)
        gather_copy((SLOT[1, 0], 0), (SLOT[1, 3], 0), r, 12, up).start()
        gather_copy((SLOT[1, 0], 0), (SLOT[1, 1], 0), r, 13, down).start()
        to_sibling(SLOT[1, 0], r)

    for r in (0, 1):
        gathered(SLOT[0, 3], 0, r)
        gather_copy((SLOT[0, 3], 0), (SLOT[0, 2], 0), r, 3, up).start()
        gathered(SLOT[0, 1], 0, 2 + r)
        gather_copy((SLOT[0, 1], 0), (SLOT[0, 2], 0), 2 + r, 3, down).start()
        own_along(2 + r)
        to_sibling(SLOT[0, 3], r)
        to_sibling(SLOT[0, 1], 2 + r)
    for r in (0, 1):
        partner(r)
        partner(2 + r)
        opposite(r)
        opposite(2 + r)

    lane = lax.broadcasted_iota(jnp.int32, (TQ, B), 1) // HEAD_DIM
    row = lax.broadcasted_iota(jnp.int32, (B, TQ), 0) // HEAD_DIM
    for copy in q_copies:
        copy.wait()
    for source, plain, turned in ((q_ref, qa, qat), (c_ref, ca, cat)):
        for question in range(2):
            mine = source[question * TQ : (question + 1) * TQ, :].astype(F32)
            mine_t = mine.T
            for head in range(HEADS_HERE):
                at = slice(head * TQ, (head + 1) * TQ)
                plain[question, at, :] = jnp.where(lane == head, mine, 0.0).astype(BF16)
                turned[question, :, at] = jnp.where(row == head, mine_t, 0.0).astype(BF16)

    def rows_of(r):
        return pl.ds(pl.multiple_of(r * B, B), B)

    def passage(k):
        return k % 2 * 2 + k // 2

    for r in (0, 1):
        gathered(SLOT[0, 1], 0, r)
        to_sibling(SLOT[0, 1], r)
        gathered(SLOT[0, 3], 0, 2 + r)
        to_sibling(SLOT[0, 3], 2 + r)

    for copy in w_copies[:16]:
        copy.wait()

    def first_part(k, carry):
        r = passage(k)
        for slot in range(4):
            gathered(slot, 1, r)
        acc[rows_of(r), :] = nn(fm[rows_of(r), 0 : 8 * B], w[0 : 8 * B, :])
        return carry

    lax.fori_loop(0, PASSAGES_HERE, first_part, 0)

    for copy in w_copies[16:]:
        copy.wait()

    def second_part(k, carry):
        @pl.when(k < PASSAGES_HERE)
        def _():
            r = passage(k)
            for slot in (SLOT[1, 2], SLOT[1, 1], SLOT[1, 3]):
                gathered(slot, 0, r)
                to_sibling(slot, r)
            gathered(SLOT[0, 2], 1, r)
            gathered(SLOT[1, 2], 1, r)
            acc[rows_of(r), :] += nn(fm[rows_of(r), 8 * B : 12 * B], w[8 * B : 12 * B, :])

        @pl.when(k > 0)
        def _():
            attend(passage(k - 1))

        return carry

    def attend(r):
        for slot in (SLOT[1, 1], SLOT[1, 3]):
            gathered(slot, 1, r)
        both = acc[rows_of(r), :] + nn(fm[rows_of(r), 12 * B :], w[12 * B :, :])
        keys, values = both[:, :B], both[:, B:].astype(BF16)
        kt[r] = keys.T.astype(BF16)
        keys = keys.astype(BF16)
        question = own_ref[r]
        scores = nt(keys, qa[question])
        flows = nt(values, ca[question])
        alive = lax.broadcasted_iota(jnp.int32, (LEN, PAIRS), 0) < len_ref[r]
        masked = jnp.where(alive, scores, FILL)
        top = jnp.max(masked, axis=0, keepdims=True)
        shifted = jnp.where(alive, jnp.exp(masked - top), 0.0)
        e_ref[r] = shifted
        gp_ref[r] = flows
        stat[r, 0:1, :] = top
        stat[r, 1:2, :] = jnp.sum(shifted, axis=0, keepdims=True)
        stat[r, 2:3, :] = jnp.sum(shifted * flows, axis=0, keepdims=True)

    lax.fori_loop(0, PASSAGES_HERE + 1, second_part, 0)

    picks = []
    for r in range(PASSAGES_HERE):
        second = own_ref[r].astype(F32)
        picks.append((1.0 - second, second))
    for question in range(2):
        tops = [
            stat[r, 0:1, :] * picks[r][question] + FILL * (1.0 - picks[r][question])
            for r in range(PASSAGES_HERE)
        ]
        top = jnp.maximum(jnp.maximum(tops[0], tops[1]), jnp.maximum(tops[2], tops[3]))
        mass = jnp.zeros((1, PAIRS), F32)
        flow = jnp.zeros((1, PAIRS), F32)
        for r in range(PASSAGES_HERE):
            scale = jnp.exp(tops[r] - top) * picks[r][question]
            mass += stat[r, 1:2, :] * scale
            flow += stat[r, 2:3, :] * scale
        sl[question : question + 1, :] = top
        sl[2 + question : 3 + question, :] = mass
        sl[4 + question : 5 + question, :] = flow
    sl[6:8, :] = jnp.zeros((2, PAIRS), F32)

    def seen_by(dy, dx):
        return dy * 4 + (4 - dx) % 4

    def stat_copy(dy, dx):
        there = seen_by(dy, dx)
        return pltpu.make_async_remote_copy(
            src_ref=sl,
            dst_ref=sall.at[there],
            send_sem=st_ssem.at[dy * 4 + dx],
            recv_sem=st_rsem.at[there],
            device_id=on_psg(dy, dx),
            device_id_type=MESH,
        )

    for peer in peers:
        stat_copy(*peer).start()
    for peer in peers:
        stat_copy(*peer).wait_recv()
    sall[0] = sl[...]
    totals = []
    for question in range(2):
        tops = [sall[k, question : question + 1, :] for k in range(8)]
        top = tops[0]
        for other in tops[1:]:
            top = jnp.maximum(top, other)
        mass = jnp.zeros((1, PAIRS), F32)
        flow = jnp.zeros((1, PAIRS), F32)
        for k in range(8):
            scale = jnp.exp(tops[k] - top)
            mass += sall[k, 2 + question : 3 + question, :] * scale
            flow += sall[k, 4 + question : 5 + question, :] * scale
        totals.append((top, 1.0 / mass, flow / mass))
    for r in range(PASSAGES_HERE):
        top, inverse, shift = (
            totals[0][k] * picks[r][0] + totals[1][k] * picks[r][1] for k in range(3)
        )
        stat[r, 3:4, :] = jnp.exp(stat[r, 0:1, :] - top) * inverse
        stat[r, 4:5, :] = shift

    def gradients(k, carry):
        r = passage(k)
        question = own_ref[r]
        probs = e_ref[r] * stat[r, 3:4, :]
        grad = (probs * (gp_ref[r] - stat[r, 4:5, :])).astype(BF16)
        probs = probs.astype(BF16)
        gs[r] = grad
        g[rows_of(r), 0:B] = nn(grad, qa[question]).astype(BF16)
        g[rows_of(r), B : 2 * B] = nn(probs, ca[question]).astype(BF16)
        gt[0:B, rows_of(r)] = nt(qat[question], grad).astype(BF16)
        gt[B : 2 * B, rows_of(r)] = nt(cat[question], probs).astype(BF16)
        return carry

    lax.fori_loop(0, 2, gradients, 0)

    over_head = Scatter(
        False, m_send, m_recv, my_send, my_recv, m_ssem, m_rsem, my_ssem, my_rsem, up, down, across
    )
    over_psg = Scatter(
        True, w_send, w_recv, wy_send, wy_recv, w_ssem, w_rsem, wy_ssem, wy_rsem,
        on_psg(0, 1), on_psg(0, 3), on_psg(1, 0),
    )

    def out_copy(source, target, number):
        return pltpu.make_async_copy(source, target, out_sem.at[number])

    def part(slot, dc, r):
        at = (slot * 2 + dc) * B
        return nt(g[r * B : (r + 1) * B, :], w[at : at + B, :]).astype(BF16)

    def sibling_copy(number):
        return pltpu.make_async_remote_copy(
            src_ref=sib_send.at[number],
            dst_ref=sib_recv.at[number],
            send_sem=sib_ssem.at[number],
            recv_sem=sib_rsem.at[number],
            device_id=sibling,
            device_id_type=MESH,
        )

    def sibling_item(number):
        kind, dy, u = ITEMS[number]
        for way in (0, 1):
            dz, r = chunk_of(kind, u, way)
            sib_send[number, way * B : (way + 1) * B, :] = part(SLOT[dy, dz], 1, r)
        sibling_copy(number).start()

    def head_item(number):
        kind, dy, u = ITEMS[number]
        sibling_copy(number).wait_recv()

        def own(dz, r, way):
            other = sib_recv[number, way * B : (way + 1) * B, :].astype(F32)
            return part(SLOT[dy, dz], 0, r).astype(F32) + other

        def store(r, value):
            gm_own[r * B : (r + 1) * B, :] = value.astype(BF16)
            out_copy(gm_own.at[pl.ds(r * B, B)], gm_out.at[pl.ds(r * B, B)], r).start()

        over_head.item(kind, dy, u, own, store)

    def psg_item(number):
        kind, dy, u = ITEMS[number]

        def own(dx, r, way):
            kv, half = r // 2, r % 2
            slot = slot_of((yl + dy + 2 - yh) % 2, (x + dx + 4 - z) % 4)
            column = (slot * 2 + (half + 2 - core) % 2) * B
            return nn(gt[kv * B : (kv + 1) * B, :], fm[:, pl.ds(pl.multiple_of(column, B), B)])

        def store(r, value):
            gw_own[r] = value
            out_copy(gw_own.at[r], gw_out.at[r], 4 + r).start()

        over_psg.item(kind, dy, u, own, store)

    piece = 2 * B // 8

    def q1_copy(dy, dx):
        there = seen_by(dy, dx)
        start = pl.multiple_of(psg_at(dy, dx) * piece, piece)
        return pltpu.make_async_remote_copy(
            src_ref=gq_send.at[pl.ds(start, piece)],
            dst_ref=gq_recv.at[there],
            send_sem=q1_ssem.at[dy * 4 + dx],
            recv_sem=q1_rsem.at[there],
            device_id=on_psg(dy, dx),
            device_id_type=MESH,
        )

    def q2_copy(dy, dx):
        return pltpu.make_async_remote_copy(
            src_ref=gq_own,
            dst_ref=gq_full.at[p],
            send_sem=q2_ssem.at[dy * 4 + dx],
            recv_sem=q2_rsem.at[seen_by(dy, dx)],
            device_id=on_psg(dy, dx),
            device_id_type=MESH,
        )

    def q2_wait(dy, dx):
        pltpu.make_async_remote_copy(
            src_ref=gq_own,
            dst_ref=gq_full.at[psg_at(dy, dx)],
            send_sem=q2_ssem.at[dy * 4 + dx],
            recv_sem=q2_rsem.at[dy * 4 + dx],
            device_id=on_psg(dy, dx),
            device_id_type=MESH,
        ).wait_recv()

    def query_terms():
        gq_acc[...] = jnp.zeros((2 * B, TQ), F32)
        for r in range(PASSAGES_HERE):
            term = nn(kt[r], gs[r])
            for head in range(HEADS_HERE):
                at = slice(head * HEAD_DIM, (head + 1) * HEAD_DIM)
                mine = term[at, head * TQ : (head + 1) * TQ]
                gq_acc[at, :] += mine * picks[r][0]
                after = slice(B + head * HEAD_DIM, B + (head + 1) * HEAD_DIM)
                gq_acc[after, :] += mine * picks[r][1]
        gq_send[...] = gq_acc[...].astype(BF16)
        for peer in peers:
            q1_copy(*peer).start()

    def query_sums():
        total = gq_acc[pl.ds(pl.multiple_of(p * piece, piece), piece), :]
        for dy, dx in peers:
            there = dy * 4 + dx
            pltpu.make_async_remote_copy(
                src_ref=gq_recv.at[there],
                dst_ref=gq_recv.at[there],
                send_sem=q1_ssem.at[there],
                recv_sem=q1_rsem.at[there],
                device_id=on_psg(dy, dx),
                device_id_type=MESH,
            ).wait_recv()
            total = total + gq_recv[there].astype(F32)
        gq_own[...] = total.astype(BF16)
        for peer in peers:
            q2_copy(*peer).start()
        gq_full[p] = gq_own[...]

    def query_end():
        for peer in peers:
            q2_wait(*peer)
        out_copy(gq_full, gq_out, 8).start()

    def gather_sent(r, carry):
        for number in range(15):
            gather_copy((0, 0), (0, 0), r, number, sibling).wait_send()
        return carry

    def sent():
        lax.fori_loop(0, PASSAGES_HERE, gather_sent, 0)
        for peer in peers:
            stat_copy(*peer).wait_send()
            q1_copy(*peer).wait_send()
            q2_copy(*peer).wait_send()
        for number in range(len(ITEMS) - 1):
            sibling_copy(number).wait_send()

    sibling_item(0)
    lax.fori_loop(2, 4, gradients, 0)
    for number in range(len(ITEMS)):
        if number == 14:
            query_end()
            sent()
            over_head.finish(EARLIER)
            over_psg.finish(EARLIER)
        psg_item(number)
        if number + 1 < len(ITEMS):
            sibling_item(number + 1)
        head_item(number)
        if number == 2:
            query_terms()
        if number == 8:
            query_sums()

    sibling_copy(len(ITEMS) - 1).wait_send()
    over_head.finish(LAST)
    over_psg.finish(LAST)
    over_head.finish_y()
    over_psg.finish_y()
    for r in range(PASSAGES_HERE):
        out_copy(gm_own.at[pl.ds(r * B, B)], gm_out.at[pl.ds(r * B, B)], r).wait()
        out_copy(gw_own.at[r], gw_out.at[r], 4 + r).wait()
    out_copy(gq_full, gq_out, 8).wait()


def epilogue(gq_in, gm_in, gw_in, gq_out, gm_out, gwk_out, gwv_out, gq, gm, gw, gq_t, gw_t, sem):
    def copy(source, target, number):
        return pltpu.make_async_copy(source, target, sem.at[number])

    def gw_write(r):
        out = gwk_out if r < 2 else gwv_out
        return copy(gw_t.at[r], out.at[pl.ds(r % 2 * B, B)], 6 + r)

    reads = [copy(gw_in.at[r], gw.at[r], r) for r in range(4)]
    reads += [copy(gm_in, gm, 4), copy(gq_in, gq, 5)]
    writes = [gw_write(r) for r in range(4)]
    writes += [copy(gm, gm_out, 10), copy(gq_t, gq_out, 11)]
    for read in reads:
        read.start()
    for r in range(4):
        reads[r].wait()
        gw_t[r] = gw[r].T
        writes[r].start()
    reads[4].wait()
    writes[4].start()
    reads[5].wait()
    for question in range(2):
        turned = jnp.concatenate([gq[question * 4 + k] for k in range(4)], axis=0)
        gq_t[question * TQ : (question + 1) * TQ, :] = turned.astype(F32).T.astype(BF16)
    writes[5].start()
    for write in writes:
        write.wait()


def on_device(queries, memory, lengths, owner, w_key, w_value, grad_context):
    rows, width = memory.shape[0], w_key.shape[0]
    anywhere = pl.BlockSpec(memory_space=pl.ANY)
    dma = pltpu.SemaphoreType.DMA
    half = 2 * B
    outs = pl.pallas_call(
        kernel,
        out_shape=(
            jax.ShapeDtypeStruct((8, 2 * B // 8, TQ), BF16),
            jax.ShapeDtypeStruct((rows, B), BF16),
            jax.ShapeDtypeStruct((4, B, B), F32),
        ),
        in_specs=[anywhere] * 7,
        out_specs=[anywhere] * 3,
        scratch_shapes=[
            pltpu.SMEM((PASSAGES_HERE,), jnp.int32),
            pltpu.SMEM((PASSAGES_HERE,), jnp.int32),
            pltpu.VMEM((2 * TQ, B), BF16),
            pltpu.VMEM((2 * TQ, B), BF16),
            pltpu.VMEM((rows, B), BF16),
            pltpu.VMEM((4, B, B), F32),
            pltpu.VMEM((rows, width), BF16),
            pltpu.VMEM((width, 2 * B), BF16),
            pltpu.VMEM((2, PAIRS, B), BF16),
            pltpu.VMEM((2, PAIRS, B), BF16),
            pltpu.VMEM((2, B, PAIRS), BF16),
            pltpu.VMEM((2, B, PAIRS), BF16),
            pltpu.VMEM((rows, 2 * B), F32),
            pltpu.VMEM((PASSAGES_HERE, B, B), BF16),
            pltpu.VMEM((PASSAGES_HERE, LEN, PAIRS), F32),
            pltpu.VMEM((PASSAGES_HERE, LEN, PAIRS), F32),
            pltpu.VMEM((PASSAGES_HERE, 8, PAIRS), F32),
            pltpu.VMEM((8, PAIRS), F32),
            pltpu.VMEM((8, 8, PAIRS), F32),
            pltpu.VMEM((rows, 2 * B), BF16),
            pltpu.VMEM((2 * B, rows), BF16),
            pltpu.VMEM((PASSAGES_HERE, LEN, PAIRS), BF16),
            pltpu.VMEM((16, half, B), BF16),
            pltpu.VMEM((16, half, B), BF16),
            pltpu.VMEM((12, half, B), BF16),
            pltpu.VMEM((12, half, B), BF16),
            pltpu.VMEM((2, half, B), BF16),
            pltpu.VMEM((2, half, B), BF16),
            pltpu.VMEM((12, half, B), BF16),
            pltpu.VMEM((12, half, B), BF16),
            pltpu.VMEM((2, half, B), BF16),
            pltpu.VMEM((2, half, B), BF16),
            pltpu.VMEM((2 * B, TQ), F32),
            pltpu.VMEM((2 * B, TQ), BF16),
            pltpu.VMEM((8, 2 * B // 8, TQ), BF16),
            pltpu.VMEM((2 * B // 8, TQ), BF16),
            pltpu.VMEM((8, 2 * B // 8, TQ), BF16),
            dma, dma((32,)), dma((4,)), dma((9,)),
            dma((15, 4)), dma((16, 4)),
            dma((8,)), dma((8,)),
            dma((16,)), dma((16,)),
            dma((12, 2)), dma((12, 2)), dma((2,)), dma((2,)),
            dma((12, 2)), dma((12, 2)), dma((2,)), dma((2,)),
            dma((8,)), dma((8,)), dma((8,)), dma((8,)),
        ],
        compiler_params=pltpu.CompilerParams(
            collective_id=0, has_side_effects=True, vmem_limit_bytes=60 * 2**20
        ),
        name="whole",
    )(lengths, owner, queries, grad_context, memory, w_key, w_value)
    gq, gm, gwk, gwv = pl.pallas_call(
        epilogue,
        out_shape=(
            jax.ShapeDtypeStruct((2 * TQ, B), BF16),
            jax.ShapeDtypeStruct((rows, B), BF16),
            jax.ShapeDtypeStruct((half, B), F32),
            jax.ShapeDtypeStruct((half, B), F32),
        ),
        in_specs=[anywhere] * 3,
        out_specs=[anywhere] * 4,
        scratch_shapes=[
            pltpu.VMEM((8, 2 * B // 8, TQ), BF16),
            pltpu.VMEM((rows, B), BF16),
            pltpu.VMEM((4, B, B), F32),
            pltpu.VMEM((2 * TQ, B), BF16),
            pltpu.VMEM((4, B, B), F32),
            dma((12,)),
        ],
        name="turn",
    )(*outs)
    return gq, gm, gwk, gwv


def solution(mesh):
    in_specs = (
        P(None, "head"),
        P("psg", "head"),
        P("psg"),
        P("psg"),
        P(None, "head"),
        P(None, "head"),
        P(None, "head"),
    )
    out_specs = (P(None, "head"), P("psg", "head"), P("psg", "head"), P("psg", "head"))
    return jax.shard_map(
        on_device, mesh=mesh, in_specs=in_specs, out_specs=out_specs, check_vma=False
    )
```

```python
import jax
import jax.numpy as jnp
from jax import lax
from jax.experimental import pallas as pl
from jax.experimental.pallas import tpu as pltpu
from jax.sharding import PartitionSpec as P

HEAD_DIM = 64
LEN = 256
TQ = 128
HEADS_HERE = 4
PASSAGES_HERE = 4
B = 256
PAIRS = HEADS_HERE * TQ
MESH = pl.DeviceIdType.MESH
FILL = -1e30
F32 = jnp.float32
BF16 = jnp.bfloat16

PLACES = ((0, 0), (0, 1), (0, 3), (1, 0), (0, 2), (1, 2), (1, 1), (1, 3))
SLOT = {place: slot for slot, place in enumerate(PLACES)}


def is_equal(a, k):
    return 1 - ((a - k) * (a - k) + 48) // 49


def slot_of(dy, dz):
    code = dy * 4 + dz
    total = 0
    for (py, pz), slot in SLOT.items():
        total = total + slot * is_equal(code, py * 4 + pz)
    return total


def nt(a, b):
    return lax.dot_general(a, b, (((1,), (1,)), ((), ())), preferred_element_type=F32)


def nn(a, b):
    return jnp.dot(a, b, preferred_element_type=F32)


class Scatter:
    def __init__(self, pair_first, send, recv, ysend, yrecv, ssem, rsem, yssem, yrsem, following, before, partner):
        self.pair_first = pair_first
        self.send, self.recv, self.ysend, self.yrecv = send, recv, ysend, yrecv
        self.ssem, self.rsem, self.yssem, self.yrsem = ssem, rsem, yssem, yrsem
        self.following, self.before, self.partner = following, before, partner

    def half(self, ref, index, way):
        return ref.at[index, pl.ds(way * B, B)]

    def copy(self, index, way):
        return pltpu.make_async_remote_copy(
            src_ref=self.half(self.send, index, way),
            dst_ref=self.half(self.recv, index, way),
            send_sem=self.ssem.at[index, way],
            recv_sem=self.rsem.at[index, way],
            device_id=self.before if way else self.following,
            device_id_type=MESH,
        )

    def first_copy(self):
        return pltpu.make_async_remote_copy(
            src_ref=self.send.at[FIRST],
            dst_ref=self.recv.at[FIRST],
            send_sem=self.ssem.at[FIRST, 0],
            recv_sem=self.rsem.at[FIRST, 0],
            device_id=self.partner,
            device_id_type=MESH,
        )

    def ycopy(self, u):
        return pltpu.make_async_remote_copy(
            src_ref=self.ysend.at[u],
            dst_ref=self.yrecv.at[u],
            send_sem=self.yssem.at[u],
            recv_sem=self.yrsem.at[u],
            device_id=self.partner,
            device_id_type=MESH,
        )

    def arrived(self, index, way):
        return self.recv[index, way * B : (way + 1) * B, :].astype(F32)

    def item(self, kind, dy, u, own, store):
        first = (dy * 2 + u) * 3
        if kind == "D":
            mine = [own(0, way * 2 + u, way) for way in (0, 1)]
            for way in (0, 1):
                self.copy(first + 1, way).wait_recv()
                self.copy(first + 2, way).wait_recv()
            if dy == 0:
                self.ycopy(u).wait_recv()
            for way in (0, 1):
                value = mine[way] + self.arrived(first + 2, way) + self.arrived(first + 1, 1 - way)
                if dy == 1:
                    self.ysend[u, way * B : (way + 1) * B, :] = value.astype(BF16)
                else:
                    value = value + self.yrecv[u, way * B : (way + 1) * B, :].astype(F32)
                    store(way * 2 + u, value)
            if dy == 1:
                self.ycopy(u).start()
            return
        index = first + "ABC".index(kind)
        if self.pair_first and index == FIRST:
            for way in (0, 1):
                dz, r = chunk_of(kind, u, way)
                self.send[index, way * B : (way + 1) * B, :] = own(dz, r, way).astype(BF16)
            self.first_copy().start()
            return
        if self.pair_first and index == 0:
            self.first_copy().wait_recv()
        for way in (0, 1):
            dz, r = chunk_of(kind, u, way)
            value = own(dz, r, way)
            if self.pair_first and index == 0:
                value = value + self.arrived(FIRST, way)
            if kind == "C" and not (self.pair_first and first == FIRST):
                self.copy(first, way).wait_recv()
                value = value + self.arrived(first, way)
            self.send[index, way * B : (way + 1) * B, :] = value.astype(BF16)
            self.copy(index, way).start()

    def finish(self, indices):
        for index in indices:
            if self.pair_first and index == FIRST:
                self.first_copy().wait_send()
                continue
            for way in (0, 1):
                self.copy(index, way).wait_send()

    def finish_y(self):
        for u in (0, 1):
            self.ycopy(u).wait_send()


def chunk_of(kind, u, way):
    if kind == "A":
        return 2, way * 2 + u
    if kind == "B":
        return (3, u) if way else (1, 2 + u)
    if kind == "C":
        return (3, 2 + u) if way else (1, u)
    return 0, way * 2 + u


ITEMS = (
    ("A", 1, 0), ("B", 1, 0), ("C", 1, 0), ("A", 1, 1), ("B", 1, 1), ("D", 1, 0),
    ("C", 1, 1), ("A", 0, 0), ("B", 0, 0), ("D", 1, 1), ("C", 0, 0), ("A", 0, 1),
    ("B", 0, 1), ("C", 0, 1), ("D", 0, 0), ("D", 0, 1),
)
FIRST = 6
LAST = (4, 5)
EARLIER = tuple(index for index in range(12) if index not in LAST)


def kernel(
    len_in, own_in, q_in, c_in, mem_ref, wk_ref, wv_ref,
    gq_out, gm_out, gw_out,
    len_ref, own_ref, q_ref, c_ref, gm_own, gw_own, fm, w, qa, ca, qat, cat, acc, kt, e_ref, gp_ref, stat, sl, sall, g, gt, gs,
    sib_send, sib_recv, m_send, m_recv, my_send, my_recv, w_send, w_recv, wy_send, wy_recv,
    gq_acc, gq_send, gq_recv, gq_own, gq_full,
    mem_sem, w_sem, qc_sem, out_sem, ag_ssem, ag_rsem, st_ssem, st_rsem, sib_ssem, sib_rsem,
    m_ssem, m_rsem, my_ssem, my_rsem, w_ssem, w_rsem, wy_ssem, wy_rsem,
    q1_ssem, q1_rsem, q2_ssem, q2_rsem,
):
    p, h = lax.axis_index("psg"), lax.axis_index("head")
    yl, x = p // 4, p % 4
    yh, z, core = h // 8, (h // 2) % 4, h % 2

    def head_at(dy, dz, dc=0):
        return ((yh + dy) % 2) * 8 + ((z + dz) % 4) * 2 + (core + dc) % 2

    def psg_at(dy, dx):
        return ((yl + dy) % 2) * 4 + (x + dx) % 4

    def on_head(dy, dz, dc=0):
        return (p, head_at(dy, dz, dc))

    def on_psg(dy, dx):
        return (psg_at(dy, dx), h)

    up, down, across, sibling = on_head(0, 1), on_head(0, 3), on_head(1, 0), on_head(0, 0, 1)
    peers = [(k // 4, k % 4) for k in range(1, 8)]

    mem_copy = pltpu.make_async_copy(mem_ref, fm.at[:, pl.ds(0, B)], mem_sem)
    mem_copy.start()
    q_copies = [
        pltpu.make_async_copy(q_in, q_ref, qc_sem.at[0]),
        pltpu.make_async_copy(c_in, c_ref, qc_sem.at[1]),
        pltpu.make_async_copy(len_in, len_ref, qc_sem.at[2]),
        pltpu.make_async_copy(own_in, own_ref, qc_sem.at[3]),
    ]
    for copy in q_copies:
        copy.start()
    barrier = pltpu.get_barrier_semaphore()
    partners = [on_psg(*peer) for peer in reversed(peers)] + [across, up, down, sibling]
    for device in partners:
        pl.semaphore_signal(barrier, inc=1, device_id=device, device_id_type=MESH)
    pl.semaphore_wait(barrier, len(partners))

    def block(slot, dc, r):
        return fm.at[pl.ds(r * B, B), pl.ds((slot * 2 + dc) * B, B)]

    def gather_copy(source, target, r, number, device):
        return pltpu.make_async_remote_copy(
            src_ref=block(source[0], source[1], r),
            dst_ref=block(target[0], target[1], r),
            send_sem=ag_ssem.at[number, r],
            recv_sem=ag_rsem.at[target[0] * 2 + target[1], r],
            device_id=device,
            device_id_type=MESH,
        )

    def gathered(slot, dc, r):
        gather_copy((slot, dc), (slot, dc), r, 0, sibling).wait_recv()

    def to_sibling(slot, r):
        gather_copy((slot, 0), (slot, 1), r, 4 + slot, sibling).start()

    def own_copy(target, r, number, device):
        return pltpu.make_async_remote_copy(
            src_ref=mem_ref.at[pl.ds(r * B, B)],
            dst_ref=block(target, 0, r),
            send_sem=ag_ssem.at[number, r],
            recv_sem=ag_rsem.at[target * 2, r],
            device_id=device,
            device_id_type=MESH,
        )

    def own_along(k):
        own_copy(SLOT[0, 3], k, 0, up).start()
        own_copy(SLOT[0, 1], (k + 2) % 4, 1, down).start()

    own_along(0)
    own_along(1)
    for k in range(PASSAGES_HERE):
        own_copy(SLOT[1, 0], k % 2 * 2 + k // 2, 2, across).start()
    mem_copy.wait()
    for r in range(PASSAGES_HERE):
        to_sibling(0, r)
    w_copies = []
    for slot, (dy, dz) in enumerate(PLACES):
        for dc in (0, 1):
            rows = pl.ds(pl.multiple_of(head_at(dy, dz, dc) * B, B), B)
            into = pl.ds((slot * 2 + dc) * B, B)
            for part, ref in enumerate((wk_ref, wv_ref)):
                w_copies.append(
                    pltpu.make_async_copy(
                        ref.at[rows, :],
                        w.at[into, pl.ds(part * B, B)],
                        w_sem.at[(slot * 2 + dc) * 2 + part],
                    )
                )
                w_copies[-1].start()

    def opposite(r):
        gathered(SLOT[0, 2], 0, r)
        gather_copy((SLOT[0, 2], 0), (SLOT[1, 2], 0), r, 14, across).start()
        to_sibling(SLOT[0, 2], r)

    def partner(r):
        gathered(SLOT[1, 0], 0, r)
        gather_copy((SLOT[1, 0], 0), (SLOT[1, 3], 0), r, 12, up).start()
        gather_copy((SLOT[1, 0], 0), (SLOT[1, 1], 0), r, 13, down).start()
        to_sibling(SLOT[1, 0], r)

    for r in (0, 1):
        gathered(SLOT[0, 3], 0, r)
        gather_copy((SLOT[0, 3], 0), (SLOT[0, 2], 0), r, 3, up).start()
        gathered(SLOT[0, 1], 0, 2 + r)
        gather_copy((SLOT[0, 1], 0), (SLOT[0, 2], 0), 2 + r, 3, down).start()
        own_along(2 + r)
        to_sibling(SLOT[0, 3], r)
        to_sibling(SLOT[0, 1], 2 + r)
    for r in (0, 1):
        partner(r)
        partner(2 + r)
        opposite(r)
        opposite(2 + r)

    lane = lax.broadcasted_iota(jnp.int32, (TQ, B), 1) // HEAD_DIM
    row = lax.broadcasted_iota(jnp.int32, (B, TQ), 0) // HEAD_DIM
    for copy in q_copies:
        copy.wait()
    for source, plain, turned in ((q_ref, qa, qat), (c_ref, ca, cat)):
        for question in range(2):
            mine = source[question * TQ : (question + 1) * TQ, :].astype(F32)
            mine_t = mine.T
            for head in range(HEADS_HERE):
                at = slice(head * TQ, (head + 1) * TQ)
                plain[question, at, :] = jnp.where(lane == head, mine, 0.0).astype(BF16)
                turned[question, :, at] = jnp.where(row == head, mine_t, 0.0).astype(BF16)

    def rows_of(r):
        return pl.ds(pl.multiple_of(r * B, B), B)

    def passage(k):
        return k % 2 * 2 + k // 2

    for r in (0, 1):
        gathered(SLOT[0, 1], 0, r)
        to_sibling(SLOT[0, 1], r)
        gathered(SLOT[0, 3], 0, 2 + r)
        to_sibling(SLOT[0, 3], 2 + r)

    for copy in w_copies[:16]:
        copy.wait()

    def first_part(k, carry):
        r = passage(k)
        for slot in range(4):
            gathered(slot, 1, r)
        acc[rows_of(r), :] = nn(fm[rows_of(r), 0 : 8 * B], w[0 : 8 * B, :])
        return carry

    lax.fori_loop(0, PASSAGES_HERE, first_part, 0)

    for copy in w_copies[16:]:
        copy.wait()

    def second_part(k, carry):
        @pl.when(k < PASSAGES_HERE)
        def _():
            r = passage(k)
            for slot in (SLOT[1, 2], SLOT[1, 1], SLOT[1, 3]):
                gathered(slot, 0, r)
                to_sibling(slot, r)
            gathered(SLOT[0, 2], 1, r)
            gathered(SLOT[1, 2], 1, r)
            acc[rows_of(r), :] += nn(fm[rows_of(r), 8 * B : 12 * B], w[8 * B : 12 * B, :])

        @pl.when(k > 0)
        def _():
            attend(passage(k - 1))

        return carry

    def attend(r):
        for slot in (SLOT[1, 1], SLOT[1, 3]):
            gathered(slot, 1, r)
        both = acc[rows_of(r), :] + nn(fm[rows_of(r), 12 * B :], w[12 * B :, :])
        keys, values = both[:, :B], both[:, B:].astype(BF16)
        kt[r] = keys.T.astype(BF16)
        keys = keys.astype(BF16)
        question = own_ref[r]
        scores = nt(keys, qa[question])
        flows = nt(values, ca[question])
        alive = lax.broadcasted_iota(jnp.int32, (LEN, PAIRS), 0) < len_ref[r]
        masked = jnp.where(alive, scores, FILL)
        top = jnp.max(masked, axis=0, keepdims=True)
        shifted = jnp.where(alive, jnp.exp(masked - top), 0.0)
        e_ref[r] = shifted
        gp_ref[r] = flows
        stat[r, 0:1, :] = top
        stat[r, 1:2, :] = jnp.sum(shifted, axis=0, keepdims=True)
        stat[r, 2:3, :] = jnp.sum(shifted * flows, axis=0, keepdims=True)

    lax.fori_loop(0, PASSAGES_HERE + 1, second_part, 0)

    picks = []
    for r in range(PASSAGES_HERE):
        second = own_ref[r].astype(F32)
        picks.append((1.0 - second, second))
    for question in range(2):
        tops = [
            stat[r, 0:1, :] * picks[r][question] + FILL * (1.0 - picks[r][question])
            for r in range(PASSAGES_HERE)
        ]
        top = jnp.maximum(jnp.maximum(tops[0], tops[1]), jnp.maximum(tops[2], tops[3]))
        mass = jnp.zeros((1, PAIRS), F32)
        flow = jnp.zeros((1, PAIRS), F32)
        for r in range(PASSAGES_HERE):
            scale = jnp.exp(tops[r] - top) * picks[r][question]
            mass += stat[r, 1:2, :] * scale
            flow += stat[r, 2:3, :] * scale
        sl[question : question + 1, :] = top
        sl[2 + question : 3 + question, :] = mass
        sl[4 + question : 5 + question, :] = flow
    sl[6:8, :] = jnp.zeros((2, PAIRS), F32)

    def seen_by(dy, dx):
        return dy * 4 + (4 - dx) % 4

    def stat_copy(dy, dx):
        there = seen_by(dy, dx)
        return pltpu.make_async_remote_copy(
            src_ref=sl,
            dst_ref=sall.at[there],
            send_sem=st_ssem.at[dy * 4 + dx],
            recv_sem=st_rsem.at[there],
            device_id=on_psg(dy, dx),
            device_id_type=MESH,
        )

    for peer in peers:
        stat_copy(*peer).start()
    for peer in peers:
        stat_copy(*peer).wait_recv()
    sall[0] = sl[...]
    totals = []
    for question in range(2):
        tops = [sall[k, question : question + 1, :] for k in range(8)]
        top = tops[0]
        for other in tops[1:]:
            top = jnp.maximum(top, other)
        mass = jnp.zeros((1, PAIRS), F32)
        flow = jnp.zeros((1, PAIRS), F32)
        for k in range(8):
            scale = jnp.exp(tops[k] - top)
            mass += sall[k, 2 + question : 3 + question, :] * scale
            flow += sall[k, 4 + question : 5 + question, :] * scale
        totals.append((top, 1.0 / mass, flow / mass))
    for r in range(PASSAGES_HERE):
        top, inverse, shift = (
            totals[0][k] * picks[r][0] + totals[1][k] * picks[r][1] for k in range(3)
        )
        stat[r, 3:4, :] = jnp.exp(stat[r, 0:1, :] - top) * inverse
        stat[r, 4:5, :] = shift

    def gradients(k, carry):
        r = passage(k)
        question = own_ref[r]
        probs = e_ref[r] * stat[r, 3:4, :]
        grad = (probs * (gp_ref[r] - stat[r, 4:5, :])).astype(BF16)
        probs = probs.astype(BF16)
        gs[r] = grad
        g[rows_of(r), 0:B] = nn(grad, qa[question]).astype(BF16)
        g[rows_of(r), B : 2 * B] = nn(probs, ca[question]).astype(BF16)
        gt[0:B, rows_of(r)] = nt(qat[question], grad).astype(BF16)
        gt[B : 2 * B, rows_of(r)] = nt(cat[question], probs).astype(BF16)
        return carry

    lax.fori_loop(0, 2, gradients, 0)

    over_head = Scatter(
        False, m_send, m_recv, my_send, my_recv, m_ssem, m_rsem, my_ssem, my_rsem, up, down, across
    )
    over_psg = Scatter(
        True, w_send, w_recv, wy_send, wy_recv, w_ssem, w_rsem, wy_ssem, wy_rsem,
        on_psg(0, 1), on_psg(0, 3), on_psg(1, 0),
    )

    def out_copy(source, target, number):
        return pltpu.make_async_copy(source, target, out_sem.at[number])

    def part(slot, dc, r):
        at = (slot * 2 + dc) * B
        return nt(g[r * B : (r + 1) * B, :], w[at : at + B, :]).astype(BF16)

    def sibling_copy(number):
        return pltpu.make_async_remote_copy(
            src_ref=sib_send.at[number],
            dst_ref=sib_recv.at[number],
            send_sem=sib_ssem.at[number],
            recv_sem=sib_rsem.at[number],
            device_id=sibling,
            device_id_type=MESH,
        )

    def sibling_item(number):
        kind, dy, u = ITEMS[number]
        for way in (0, 1):
            dz, r = chunk_of(kind, u, way)
            sib_send[number, way * B : (way + 1) * B, :] = part(SLOT[dy, dz], 1, r)
        sibling_copy(number).start()

    def head_item(number):
        kind, dy, u = ITEMS[number]
        sibling_copy(number).wait_recv()

        def own(dz, r, way):
            other = sib_recv[number, way * B : (way + 1) * B, :].astype(F32)
            return part(SLOT[dy, dz], 0, r).astype(F32) + other

        def store(r, value):
            gm_own[r * B : (r + 1) * B, :] = value.astype(BF16)
            out_copy(gm_own.at[pl.ds(r * B, B)], gm_out.at[pl.ds(r * B, B)], r).start()

        over_head.item(kind, dy, u, own, store)

    def psg_item(number):
        kind, dy, u = ITEMS[number]

        def own(dx, r, way):
            kv, half = r // 2, r % 2
            slot = slot_of((yl + dy + 2 - yh) % 2, (x + dx + 4 - z) % 4)
            column = (slot * 2 + (half + 2 - core) % 2) * B
            return nn(gt[kv * B : (kv + 1) * B, :], fm[:, pl.ds(pl.multiple_of(column, B), B)])

        def store(r, value):
            gw_own[r] = value
            out_copy(gw_own.at[r], gw_out.at[r], 4 + r).start()

        over_psg.item(kind, dy, u, own, store)

    piece = 2 * B // 8

    def q1_copy(dy, dx):
        there = seen_by(dy, dx)
        start = pl.multiple_of(psg_at(dy, dx) * piece, piece)
        return pltpu.make_async_remote_copy(
            src_ref=gq_send.at[pl.ds(start, piece)],
            dst_ref=gq_recv.at[there],
            send_sem=q1_ssem.at[dy * 4 + dx],
            recv_sem=q1_rsem.at[there],
            device_id=on_psg(dy, dx),
            device_id_type=MESH,
        )

    def q2_copy(dy, dx):
        return pltpu.make_async_remote_copy(
            src_ref=gq_own,
            dst_ref=gq_full.at[p],
            send_sem=q2_ssem.at[dy * 4 + dx],
            recv_sem=q2_rsem.at[seen_by(dy, dx)],
            device_id=on_psg(dy, dx),
            device_id_type=MESH,
        )

    def q2_wait(dy, dx):
        pltpu.make_async_remote_copy(
            src_ref=gq_own,
            dst_ref=gq_full.at[psg_at(dy, dx)],
            send_sem=q2_ssem.at[dy * 4 + dx],
            recv_sem=q2_rsem.at[dy * 4 + dx],
            device_id=on_psg(dy, dx),
            device_id_type=MESH,
        ).wait_recv()

    def query_terms():
        gq_acc[...] = jnp.zeros((2 * B, TQ), F32)
        for r in range(PASSAGES_HERE):
            term = nn(kt[r], gs[r])
            for head in range(HEADS_HERE):
                at = slice(head * HEAD_DIM, (head + 1) * HEAD_DIM)
                mine = term[at, head * TQ : (head + 1) * TQ]
                gq_acc[at, :] += mine * picks[r][0]
                after = slice(B + head * HEAD_DIM, B + (head + 1) * HEAD_DIM)
                gq_acc[after, :] += mine * picks[r][1]
        gq_send[...] = gq_acc[...].astype(BF16)
        for peer in peers:
            q1_copy(*peer).start()

    def query_sums():
        total = gq_acc[pl.ds(pl.multiple_of(p * piece, piece), piece), :]
        for dy, dx in peers:
            there = dy * 4 + dx
            pltpu.make_async_remote_copy(
                src_ref=gq_recv.at[there],
                dst_ref=gq_recv.at[there],
                send_sem=q1_ssem.at[there],
                recv_sem=q1_rsem.at[there],
                device_id=on_psg(dy, dx),
                device_id_type=MESH,
            ).wait_recv()
            total = total + gq_recv[there].astype(F32)
        gq_own[...] = total.astype(BF16)
        for peer in peers:
            q2_copy(*peer).start()
        gq_full[p] = gq_own[...]

    def query_end():
        for peer in peers:
            q2_wait(*peer)
        out_copy(gq_full, gq_out, 8).start()

    def gather_sent(r, carry):
        for number in range(15):
            gather_copy((0, 0), (0, 0), r, number, sibling).wait_send()
        return carry

    def sent():
        lax.fori_loop(0, PASSAGES_HERE, gather_sent, 0)
        for peer in peers:
            stat_copy(*peer).wait_send()
            q1_copy(*peer).wait_send()
            q2_copy(*peer).wait_send()
        for number in range(len(ITEMS) - 1):
            sibling_copy(number).wait_send()

    sibling_item(0)
    lax.fori_loop(2, 4, gradients, 0)
    for number in range(len(ITEMS)):
        if number == 14:
            query_end()
            sent()
            over_head.finish(EARLIER)
            over_psg.finish(EARLIER)
        psg_item(number)
        if number == 0:
            sibling_item(1)
        elif number + 2 < len(ITEMS):
            sibling_item(number + 2)
        head_item(number)
        if number == 0:
            sibling_item(2)
        if number == 2:
            query_terms()
        if number == 8:
            query_sums()

    sibling_copy(len(ITEMS) - 1).wait_send()
    over_head.finish(LAST)
    over_psg.finish(LAST)
    over_head.finish_y()
    over_psg.finish_y()
    for r in range(PASSAGES_HERE):
        out_copy(gm_own.at[pl.ds(r * B, B)], gm_out.at[pl.ds(r * B, B)], r).wait()
        out_copy(gw_own.at[r], gw_out.at[r], 4 + r).wait()
    out_copy(gq_full, gq_out, 8).wait()


def epilogue(gq_in, gm_in, gw_in, gq_out, gm_out, gwk_out, gwv_out, gq, gm, gw, gq_t, gw_t, sem):
    def copy(source, target, number):
        return pltpu.make_async_copy(source, target, sem.at[number])

    def gw_write(r):
        out = gwk_out if r < 2 else gwv_out
        return copy(gw_t.at[r], out.at[pl.ds(r % 2 * B, B)], 6 + r)

    reads = [copy(gw_in.at[r], gw.at[r], r) for r in range(4)]
    reads += [copy(gm_in, gm, 4), copy(gq_in, gq, 5)]
    writes = [gw_write(r) for r in range(4)]
    writes += [copy(gm, gm_out, 10), copy(gq_t, gq_out, 11)]
    for read in reads:
        read.start()
    for r in range(4):
        reads[r].wait()
        gw_t[r] = gw[r].T
        writes[r].start()
    reads[4].wait()
    writes[4].start()
    reads[5].wait()
    for question in range(2):
        turned = jnp.concatenate([gq[question * 4 + k] for k in range(4)], axis=0)
        gq_t[question * TQ : (question + 1) * TQ, :] = turned.astype(F32).T.astype(BF16)
    writes[5].start()
    for write in writes:
        write.wait()


def on_device(queries, memory, lengths, owner, w_key, w_value, grad_context):
    rows, width = memory.shape[0], w_key.shape[0]
    anywhere = pl.BlockSpec(memory_space=pl.ANY)
    dma = pltpu.SemaphoreType.DMA
    half = 2 * B
    outs = pl.pallas_call(
        kernel,
        out_shape=(
            jax.ShapeDtypeStruct((8, 2 * B // 8, TQ), BF16),
            jax.ShapeDtypeStruct((rows, B), BF16),
            jax.ShapeDtypeStruct((4, B, B), F32),
        ),
        in_specs=[anywhere] * 7,
        out_specs=[anywhere] * 3,
        scratch_shapes=[
            pltpu.SMEM((PASSAGES_HERE,), jnp.int32),
            pltpu.SMEM((PASSAGES_HERE,), jnp.int32),
            pltpu.VMEM((2 * TQ, B), BF16),
            pltpu.VMEM((2 * TQ, B), BF16),
            pltpu.VMEM((rows, B), BF16),
            pltpu.VMEM((4, B, B), F32),
            pltpu.VMEM((rows, width), BF16),
            pltpu.VMEM((width, 2 * B), BF16),
            pltpu.VMEM((2, PAIRS, B), BF16),
            pltpu.VMEM((2, PAIRS, B), BF16),
            pltpu.VMEM((2, B, PAIRS), BF16),
            pltpu.VMEM((2, B, PAIRS), BF16),
            pltpu.VMEM((rows, 2 * B), F32),
            pltpu.VMEM((PASSAGES_HERE, B, B), BF16),
            pltpu.VMEM((PASSAGES_HERE, LEN, PAIRS), F32),
            pltpu.VMEM((PASSAGES_HERE, LEN, PAIRS), F32),
            pltpu.VMEM((PASSAGES_HERE, 8, PAIRS), F32),
            pltpu.VMEM((8, PAIRS), F32),
            pltpu.VMEM((8, 8, PAIRS), F32),
            pltpu.VMEM((rows, 2 * B), BF16),
            pltpu.VMEM((2 * B, rows), BF16),
            pltpu.VMEM((PASSAGES_HERE, LEN, PAIRS), BF16),
            pltpu.VMEM((16, half, B), BF16),
            pltpu.VMEM((16, half, B), BF16),
            pltpu.VMEM((12, half, B), BF16),
            pltpu.VMEM((12, half, B), BF16),
            pltpu.VMEM((2, half, B), BF16),
            pltpu.VMEM((2, half, B), BF16),
            pltpu.VMEM((12, half, B), BF16),
            pltpu.VMEM((12, half, B), BF16),
            pltpu.VMEM((2, half, B), BF16),
            pltpu.VMEM((2, half, B), BF16),
            pltpu.VMEM((2 * B, TQ), F32),
            pltpu.VMEM((2 * B, TQ), BF16),
            pltpu.VMEM((8, 2 * B // 8, TQ), BF16),
            pltpu.VMEM((2 * B // 8, TQ), BF16),
            pltpu.VMEM((8, 2 * B // 8, TQ), BF16),
            dma, dma((32,)), dma((4,)), dma((9,)),
            dma((15, 4)), dma((16, 4)),
            dma((8,)), dma((8,)),
            dma((16,)), dma((16,)),
            dma((12, 2)), dma((12, 2)), dma((2,)), dma((2,)),
            dma((12, 2)), dma((12, 2)), dma((2,)), dma((2,)),
            dma((8,)), dma((8,)), dma((8,)), dma((8,)),
        ],
        compiler_params=pltpu.CompilerParams(
            collective_id=0, has_side_effects=True, vmem_limit_bytes=60 * 2**20
        ),
        name="whole",
    )(lengths, owner, queries, grad_context, memory, w_key, w_value)
    gq, gm, gwk, gwv = pl.pallas_call(
        epilogue,
        out_shape=(
            jax.ShapeDtypeStruct((2 * TQ, B), BF16),
            jax.ShapeDtypeStruct((rows, B), BF16),
            jax.ShapeDtypeStruct((half, B), F32),
            jax.ShapeDtypeStruct((half, B), F32),
        ),
        in_specs=[anywhere] * 3,
        out_specs=[anywhere] * 4,
        scratch_shapes=[
            pltpu.VMEM((8, 2 * B // 8, TQ), BF16),
            pltpu.VMEM((rows, B), BF16),
            pltpu.VMEM((4, B, B), F32),
            pltpu.VMEM((2 * TQ, B), BF16),
            pltpu.VMEM((4, B, B), F32),
            dma((12,)),
        ],
        name="turn",
    )(*outs)
    return gq, gm, gwk, gwv


def solution(mesh):
    in_specs = (
        P(None, "head"),
        P("psg", "head"),
        P("psg"),
        P("psg"),
        P(None, "head"),
        P(None, "head"),
        P(None, "head"),
    )
    out_specs = (P(None, "head"), P("psg", "head"), P("psg", "head"), P("psg", "head"))
    return jax.shard_map(
        on_device, mesh=mesh, in_specs=in_specs, out_specs=out_specs, check_vma=False
    )
```

```python
import jax
import jax.numpy as jnp
from jax import lax
from jax.experimental import pallas as pl
from jax.experimental.pallas import tpu as pltpu
from jax.sharding import PartitionSpec as P

HEAD_DIM = 64
LEN = 256
TQ = 128
HEADS_HERE = 4
PASSAGES_HERE = 4
B = 256
PAIRS = HEADS_HERE * TQ
MESH = pl.DeviceIdType.MESH
FILL = -1e30
F32 = jnp.float32
BF16 = jnp.bfloat16

PLACES = ((0, 0), (0, 1), (0, 3), (1, 0), (0, 2), (1, 2), (1, 1), (1, 3))
SLOT = {place: slot for slot, place in enumerate(PLACES)}


def is_equal(a, k):
    return 1 - ((a - k) * (a - k) + 48) // 49


def slot_of(dy, dz):
    code = dy * 4 + dz
    total = 0
    for (py, pz), slot in SLOT.items():
        total = total + slot * is_equal(code, py * 4 + pz)
    return total


def nt(a, b):
    return lax.dot_general(a, b, (((1,), (1,)), ((), ())), preferred_element_type=F32)


def nn(a, b):
    return jnp.dot(a, b, preferred_element_type=F32)


class Scatter:
    def __init__(self, pair_first, send, recv, ysend, yrecv, ssem, rsem, yssem, yrsem, following, before, partner):
        self.pair_first = pair_first
        self.send, self.recv, self.ysend, self.yrecv = send, recv, ysend, yrecv
        self.ssem, self.rsem, self.yssem, self.yrsem = ssem, rsem, yssem, yrsem
        self.following, self.before, self.partner = following, before, partner

    def half(self, ref, index, way):
        return ref.at[index, pl.ds(way * B, B)]

    def copy(self, index, way):
        return pltpu.make_async_remote_copy(
            src_ref=self.half(self.send, index, way),
            dst_ref=self.half(self.recv, index, way),
            send_sem=self.ssem.at[index, way],
            recv_sem=self.rsem.at[index, way],
            device_id=self.before if way else self.following,
            device_id_type=MESH,
        )

    def first_copy(self):
        return pltpu.make_async_remote_copy(
            src_ref=self.send.at[FIRST],
            dst_ref=self.recv.at[FIRST],
            send_sem=self.ssem.at[FIRST, 0],
            recv_sem=self.rsem.at[FIRST, 0],
            device_id=self.partner,
            device_id_type=MESH,
        )

    def ycopy(self, u):
        return pltpu.make_async_remote_copy(
            src_ref=self.ysend.at[u],
            dst_ref=self.yrecv.at[u],
            send_sem=self.yssem.at[u],
            recv_sem=self.yrsem.at[u],
            device_id=self.partner,
            device_id_type=MESH,
        )

    def arrived(self, index, way):
        return self.recv[index, way * B : (way + 1) * B, :].astype(F32)

    def item(self, kind, dy, u, own, store):
        first = (dy * 2 + u) * 3
        if kind == "D":
            mine = [own(0, way * 2 + u, way) for way in (0, 1)]
            for way in (0, 1):
                self.copy(first + 1, way).wait_recv()
                self.copy(first + 2, way).wait_recv()
            if dy == 0:
                self.ycopy(u).wait_recv()
            for way in (0, 1):
                value = mine[way] + self.arrived(first + 2, way) + self.arrived(first + 1, 1 - way)
                if dy == 1:
                    self.ysend[u, way * B : (way + 1) * B, :] = value.astype(BF16)
                else:
                    value = value + self.yrecv[u, way * B : (way + 1) * B, :].astype(F32)
                    store(way * 2 + u, value)
            if dy == 1:
                self.ycopy(u).start()
            return
        index = first + "ABC".index(kind)
        if self.pair_first and index == FIRST:
            for way in (0, 1):
                dz, r = chunk_of(kind, u, way)
                self.send[index, way * B : (way + 1) * B, :] = own(dz, r, way).astype(BF16)
            self.first_copy().start()
            return
        if self.pair_first and index == 0:
            self.first_copy().wait_recv()
        for way in (0, 1):
            dz, r = chunk_of(kind, u, way)
            value = own(dz, r, way)
            if self.pair_first and index == 0:
                value = value + self.arrived(FIRST, way)
            if kind == "C" and not (self.pair_first and first == FIRST):
                self.copy(first, way).wait_recv()
                value = value + self.arrived(first, way)
            self.send[index, way * B : (way + 1) * B, :] = value.astype(BF16)
            self.copy(index, way).start()

    def finish(self, indices):
        for index in indices:
            if self.pair_first and index == FIRST:
                self.first_copy().wait_send()
                continue
            for way in (0, 1):
                self.copy(index, way).wait_send()

    def finish_y(self):
        for u in (0, 1):
            self.ycopy(u).wait_send()


def chunk_of(kind, u, way):
    if kind == "A":
        return 2, way * 2 + u
    if kind == "B":
        return (3, u) if way else (1, 2 + u)
    if kind == "C":
        return (3, 2 + u) if way else (1, u)
    return 0, way * 2 + u


ITEMS = (
    ("A", 1, 0), ("B", 1, 0), ("C", 1, 0), ("A", 1, 1), ("B", 1, 1), ("D", 1, 0),
    ("C", 1, 1), ("A", 0, 0), ("B", 0, 0), ("D", 1, 1), ("C", 0, 0), ("A", 0, 1),
    ("B", 0, 1), ("C", 0, 1), ("D", 0, 0), ("D", 0, 1),
)
FIRST = 6
LAST = (4, 5)
EARLIER = tuple(index for index in range(12) if index not in LAST)


def kernel(
    len_in, own_in, q_in, c_in, mem_ref, wk_ref, wv_ref,
    gq_out, gm_out, gw_out,
    len_ref, own_ref, q_ref, c_ref, gm_own, gw_own, fm, w, qa, ca, qat, cat, acc, kt, e_ref, gp_ref, stat, sl, sall, g, gt, gs,
    sib_send, sib_recv, m_send, m_recv, my_send, my_recv, w_send, w_recv, wy_send, wy_recv,
    gq_acc, gq_send, gq_recv, gq_own, gq_full,
    mem_sem, w_sem, qc_sem, out_sem, ag_ssem, ag_rsem, st_ssem, st_rsem, sib_ssem, sib_rsem,
    m_ssem, m_rsem, my_ssem, my_rsem, w_ssem, w_rsem, wy_ssem, wy_rsem,
    q1_ssem, q1_rsem, q2_ssem, q2_rsem,
):
    p, h = lax.axis_index("psg"), lax.axis_index("head")
    yl, x = p // 4, p % 4
    yh, z, core = h // 8, (h // 2) % 4, h % 2

    def head_at(dy, dz, dc=0):
        return ((yh + dy) % 2) * 8 + ((z + dz) % 4) * 2 + (core + dc) % 2

    def psg_at(dy, dx):
        return ((yl + dy) % 2) * 4 + (x + dx) % 4

    def on_head(dy, dz, dc=0):
        return (p, head_at(dy, dz, dc))

    def on_psg(dy, dx):
        return (psg_at(dy, dx), h)

    up, down, across, sibling = on_head(0, 1), on_head(0, 3), on_head(1, 0), on_head(0, 0, 1)
    peers = [(k // 4, k % 4) for k in range(1, 8)]

    mem_copy = pltpu.make_async_copy(mem_ref, fm.at[:, pl.ds(0, B)], mem_sem)
    mem_copy.start()
    q_copies = [
        pltpu.make_async_copy(q_in, q_ref, qc_sem.at[0]),
        pltpu.make_async_copy(c_in, c_ref, qc_sem.at[1]),
        pltpu.make_async_copy(len_in, len_ref, qc_sem.at[2]),
        pltpu.make_async_copy(own_in, own_ref, qc_sem.at[3]),
    ]
    for copy in q_copies:
        copy.start()
    barrier = pltpu.get_barrier_semaphore()
    partners = [on_psg(*peer) for peer in reversed(peers)] + [across, up, down, sibling]
    for device in partners:
        pl.semaphore_signal(barrier, inc=1, device_id=device, device_id_type=MESH)
    pl.semaphore_wait(barrier, len(partners))

    def block(slot, dc, r):
        return fm.at[pl.ds(r * B, B), pl.ds((slot * 2 + dc) * B, B)]

    def gather_copy(source, target, r, number, device):
        return pltpu.make_async_remote_copy(
            src_ref=block(source[0], source[1], r),
            dst_ref=block(target[0], target[1], r),
            send_sem=ag_ssem.at[number, r],
            recv_sem=ag_rsem.at[target[0] * 2 + target[1], r],
            device_id=device,
            device_id_type=MESH,
        )

    def gathered(slot, dc, r):
        gather_copy((slot, dc), (slot, dc), r, 0, sibling).wait_recv()

    def to_sibling(slot, r):
        gather_copy((slot, 0), (slot, 1), r, 4 + slot, sibling).start()

    def own_copy(target, r, number, device):
        return pltpu.make_async_remote_copy(
            src_ref=mem_ref.at[pl.ds(r * B, B)],
            dst_ref=block(target, 0, r),
            send_sem=ag_ssem.at[number, r],
            recv_sem=ag_rsem.at[target * 2, r],
            device_id=device,
            device_id_type=MESH,
        )

    def own_along(k):
        own_copy(SLOT[0, 3], k, 0, up).start()
        own_copy(SLOT[0, 1], (k + 2) % 4, 1, down).start()

    own_along(0)
    own_along(1)
    for k in range(PASSAGES_HERE):
        own_copy(SLOT[1, 0], k % 2 * 2 + k // 2, 2, across).start()
    mem_copy.wait()
    for r in range(PASSAGES_HERE):
        to_sibling(0, r)
    w_copies = []
    for slot, (dy, dz) in enumerate(PLACES):
        for dc in (0, 1):
            rows = pl.ds(pl.multiple_of(head_at(dy, dz, dc) * B, B), B)
            into = pl.ds((slot * 2 + dc) * B, B)
            for part, ref in enumerate((wk_ref, wv_ref)):
                w_copies.append(
                    pltpu.make_async_copy(
                        ref.at[rows, :],
                        w.at[into, pl.ds(part * B, B)],
                        w_sem.at[(slot * 2 + dc) * 2 + part],
                    )
                )
                w_copies[-1].start()

    def opposite(r):
        gathered(SLOT[0, 2], 0, r)
        gather_copy((SLOT[0, 2], 0), (SLOT[1, 2], 0), r, 14, across).start()
        to_sibling(SLOT[0, 2], r)

    def partner(r):
        gathered(SLOT[1, 0], 0, r)
        gather_copy((SLOT[1, 0], 0), (SLOT[1, 3], 0), r, 12, up).start()
        gather_copy((SLOT[1, 0], 0), (SLOT[1, 1], 0), r, 13, down).start()
        to_sibling(SLOT[1, 0], r)

    for r in (0, 1):
        gathered(SLOT[0, 3], 0, r)
        gather_copy((SLOT[0, 3], 0), (SLOT[0, 2], 0), r, 3, up).start()
        gathered(SLOT[0, 1], 0, 2 + r)
        gather_copy((SLOT[0, 1], 0), (SLOT[0, 2], 0), 2 + r, 3, down).start()
        own_along(2 + r)
        to_sibling(SLOT[0, 3], r)
        to_sibling(SLOT[0, 1], 2 + r)
    for r in (0, 1):
        partner(r)
        partner(2 + r)
        opposite(r)
        opposite(2 + r)

    lane = lax.broadcasted_iota(jnp.int32, (TQ, B), 1) // HEAD_DIM
    row = lax.broadcasted_iota(jnp.int32, (B, TQ), 0) // HEAD_DIM
    for copy in q_copies:
        copy.wait()
    for source, plain, turned in ((q_ref, qa, qat), (c_ref, ca, cat)):
        for question in range(2):
            mine = source[question * TQ : (question + 1) * TQ, :].astype(F32)
            mine_t = mine.T
            for head in range(HEADS_HERE):
                at = slice(head * TQ, (head + 1) * TQ)
                plain[question, at, :] = jnp.where(lane == head, mine, 0.0).astype(BF16)
                turned[question, :, at] = jnp.where(row == head, mine_t, 0.0).astype(BF16)

    def rows_of(r):
        return pl.ds(pl.multiple_of(r * B, B), B)

    def passage(k):
        return k % 2 * 2 + k // 2

    for r in (0, 1):
        gathered(SLOT[0, 1], 0, r)
        to_sibling(SLOT[0, 1], r)
        gathered(SLOT[0, 3], 0, 2 + r)
        to_sibling(SLOT[0, 3], 2 + r)

    for copy in w_copies[:16]:
        copy.wait()

    def first_part(k, carry):
        r = passage(k)
        for slot in range(4):
            gathered(slot, 1, r)
        acc[rows_of(r), :] = nn(fm[rows_of(r), 0 : 8 * B], w[0 : 8 * B, :])
        return carry

    lax.fori_loop(0, PASSAGES_HERE, first_part, 0)

    for copy in w_copies[16:]:
        copy.wait()

    def second_part(k, carry):
        @pl.when(k < PASSAGES_HERE)
        def _():
            r = passage(k)
            for slot in (SLOT[1, 2], SLOT[1, 1], SLOT[1, 3]):
                gathered(slot, 0, r)
                to_sibling(slot, r)
            gathered(SLOT[0, 2], 1, r)
            gathered(SLOT[1, 2], 1, r)
            acc[rows_of(r), :] += nn(fm[rows_of(r), 8 * B : 12 * B], w[8 * B : 12 * B, :])

        @pl.when(k > 0)
        def _():
            attend(passage(k - 1))

        return carry

    def attend(r):
        for slot in (SLOT[1, 1], SLOT[1, 3]):
            gathered(slot, 1, r)
        both = acc[rows_of(r), :] + nn(fm[rows_of(r), 12 * B :], w[12 * B :, :])
        keys, values = both[:, :B], both[:, B:].astype(BF16)
        kt[r] = keys.T.astype(BF16)
        keys = keys.astype(BF16)
        question = own_ref[r]
        scores = nt(keys, qa[question])
        flows = nt(values, ca[question])
        alive = lax.broadcasted_iota(jnp.int32, (LEN, PAIRS), 0) < len_ref[r]
        masked = jnp.where(alive, scores, FILL)
        top = jnp.max(masked, axis=0, keepdims=True)
        shifted = jnp.where(alive, jnp.exp(masked - top), 0.0)
        e_ref[r] = shifted
        gp_ref[r] = flows
        stat[r, 0:1, :] = top
        stat[r, 1:2, :] = jnp.sum(shifted, axis=0, keepdims=True)
        stat[r, 2:3, :] = jnp.sum(shifted * flows, axis=0, keepdims=True)

    lax.fori_loop(0, PASSAGES_HERE + 1, second_part, 0)

    picks = []
    for r in range(PASSAGES_HERE):
        second = own_ref[r].astype(F32)
        picks.append((1.0 - second, second))
    for question in range(2):
        tops = [
            stat[r, 0:1, :] * picks[r][question] + FILL * (1.0 - picks[r][question])
            for r in range(PASSAGES_HERE)
        ]
        top = jnp.maximum(jnp.maximum(tops[0], tops[1]), jnp.maximum(tops[2], tops[3]))
        mass = jnp.zeros((1, PAIRS), F32)
        flow = jnp.zeros((1, PAIRS), F32)
        for r in range(PASSAGES_HERE):
            scale = jnp.exp(tops[r] - top) * picks[r][question]
            mass += stat[r, 1:2, :] * scale
            flow += stat[r, 2:3, :] * scale
        sl[question : question + 1, :] = top
        sl[2 + question : 3 + question, :] = mass
        sl[4 + question : 5 + question, :] = flow
    sl[6:8, :] = jnp.zeros((2, PAIRS), F32)

    def seen_by(dy, dx):
        return dy * 4 + (4 - dx) % 4

    def stat_copy(dy, dx):
        there = seen_by(dy, dx)
        return pltpu.make_async_remote_copy(
            src_ref=sl,
            dst_ref=sall.at[there],
            send_sem=st_ssem.at[dy * 4 + dx],
            recv_sem=st_rsem.at[there],
            device_id=on_psg(dy, dx),
            device_id_type=MESH,
        )

    for peer in peers:
        stat_copy(*peer).start()
    for peer in peers:
        stat_copy(*peer).wait_recv()
    sall[0] = sl[...]
    totals = []
    for question in range(2):
        tops = [sall[k, question : question + 1, :] for k in range(8)]
        top = tops[0]
        for other in tops[1:]:
            top = jnp.maximum(top, other)
        mass = jnp.zeros((1, PAIRS), F32)
        flow = jnp.zeros((1, PAIRS), F32)
        for k in range(8):
            scale = jnp.exp(tops[k] - top)
            mass += sall[k, 2 + question : 3 + question, :] * scale
            flow += sall[k, 4 + question : 5 + question, :] * scale
        totals.append((top, 1.0 / mass, flow / mass))
    for r in range(PASSAGES_HERE):
        top, inverse, shift = (
            totals[0][k] * picks[r][0] + totals[1][k] * picks[r][1] for k in range(3)
        )
        stat[r, 3:4, :] = jnp.exp(stat[r, 0:1, :] - top) * inverse
        stat[r, 4:5, :] = shift

    def gradients(k, carry):
        r = passage(k)
        question = own_ref[r]
        probs = e_ref[r] * stat[r, 3:4, :]
        grad = (probs * (gp_ref[r] - stat[r, 4:5, :])).astype(BF16)
        probs = probs.astype(BF16)
        gs[r] = grad
        g[rows_of(r), 0:B] = nn(grad, qa[question]).astype(BF16)
        g[rows_of(r), B : 2 * B] = nn(probs, ca[question]).astype(BF16)
        gt[0:B, rows_of(r)] = nt(qat[question], grad).astype(BF16)
        gt[B : 2 * B, rows_of(r)] = nt(cat[question], probs).astype(BF16)
        return carry

    lax.fori_loop(0, 2, gradients, 0)

    over_head = Scatter(
        True, m_send, m_recv, my_send, my_recv, m_ssem, m_rsem, my_ssem, my_rsem, up, down, across
    )
    over_psg = Scatter(
        True, w_send, w_recv, wy_send, wy_recv, w_ssem, w_rsem, wy_ssem, wy_rsem,
        on_psg(0, 1), on_psg(0, 3), on_psg(1, 0),
    )

    def out_copy(source, target, number):
        return pltpu.make_async_copy(source, target, out_sem.at[number])

    def part(slot, dc, r):
        at = (slot * 2 + dc) * B
        return nt(g[r * B : (r + 1) * B, :], w[at : at + B, :]).astype(BF16)

    def sibling_copy(number):
        return pltpu.make_async_remote_copy(
            src_ref=sib_send.at[number],
            dst_ref=sib_recv.at[number],
            send_sem=sib_ssem.at[number],
            recv_sem=sib_rsem.at[number],
            device_id=sibling,
            device_id_type=MESH,
        )

    def sibling_item(number):
        kind, dy, u = ITEMS[number]
        for way in (0, 1):
            dz, r = chunk_of(kind, u, way)
            sib_send[number, way * B : (way + 1) * B, :] = part(SLOT[dy, dz], 1, r)
        sibling_copy(number).start()

    def head_item(number):
        kind, dy, u = ITEMS[number]
        sibling_copy(number).wait_recv()

        def own(dz, r, way):
            other = sib_recv[number, way * B : (way + 1) * B, :].astype(F32)
            return part(SLOT[dy, dz], 0, r).astype(F32) + other

        def store(r, value):
            gm_own[r * B : (r + 1) * B, :] = value.astype(BF16)
            out_copy(gm_own.at[pl.ds(r * B, B)], gm_out.at[pl.ds(r * B, B)], r).start()

        over_head.item(kind, dy, u, own, store)

    def psg_item(number):
        kind, dy, u = ITEMS[number]

        def own(dx, r, way):
            kv, half = r // 2, r % 2
            slot = slot_of((yl + dy + 2 - yh) % 2, (x + dx + 4 - z) % 4)
            column = (slot * 2 + (half + 2 - core) % 2) * B
            return nn(gt[kv * B : (kv + 1) * B, :], fm[:, pl.ds(pl.multiple_of(column, B), B)])

        def store(r, value):
            gw_own[r] = value
            out_copy(gw_own.at[r], gw_out.at[r], 4 + r).start()

        over_psg.item(kind, dy, u, own, store)

    piece = 2 * B // 8

    def q1_copy(dy, dx):
        there = seen_by(dy, dx)
        start = pl.multiple_of(psg_at(dy, dx) * piece, piece)
        return pltpu.make_async_remote_copy(
            src_ref=gq_send.at[pl.ds(start, piece)],
            dst_ref=gq_recv.at[there],
            send_sem=q1_ssem.at[dy * 4 + dx],
            recv_sem=q1_rsem.at[there],
            device_id=on_psg(dy, dx),
            device_id_type=MESH,
        )

    def q2_copy(dy, dx):
        return pltpu.make_async_remote_copy(
            src_ref=gq_own,
            dst_ref=gq_full.at[p],
            send_sem=q2_ssem.at[dy * 4 + dx],
            recv_sem=q2_rsem.at[seen_by(dy, dx)],
            device_id=on_psg(dy, dx),
            device_id_type=MESH,
        )

    def q2_wait(dy, dx):
        pltpu.make_async_remote_copy(
            src_ref=gq_own,
            dst_ref=gq_full.at[psg_at(dy, dx)],
            send_sem=q2_ssem.at[dy * 4 + dx],
            recv_sem=q2_rsem.at[dy * 4 + dx],
            device_id=on_psg(dy, dx),
            device_id_type=MESH,
        ).wait_recv()

    def query_terms():
        gq_acc[...] = jnp.zeros((2 * B, TQ), F32)
        for r in range(PASSAGES_HERE):
            term = nn(kt[r], gs[r])
            for head in range(HEADS_HERE):
                at = slice(head * HEAD_DIM, (head + 1) * HEAD_DIM)
                mine = term[at, head * TQ : (head + 1) * TQ]
                gq_acc[at, :] += mine * picks[r][0]
                after = slice(B + head * HEAD_DIM, B + (head + 1) * HEAD_DIM)
                gq_acc[after, :] += mine * picks[r][1]
        gq_send[...] = gq_acc[...].astype(BF16)
        for peer in peers:
            q1_copy(*peer).start()

    def query_sums():
        total = gq_acc[pl.ds(pl.multiple_of(p * piece, piece), piece), :]
        for dy, dx in peers:
            there = dy * 4 + dx
            pltpu.make_async_remote_copy(
                src_ref=gq_recv.at[there],
                dst_ref=gq_recv.at[there],
                send_sem=q1_ssem.at[there],
                recv_sem=q1_rsem.at[there],
                device_id=on_psg(dy, dx),
                device_id_type=MESH,
            ).wait_recv()
            total = total + gq_recv[there].astype(F32)
        gq_own[...] = total.astype(BF16)
        for peer in peers:
            q2_copy(*peer).start()
        gq_full[p] = gq_own[...]

    def query_end():
        for peer in peers:
            q2_wait(*peer)
        out_copy(gq_full, gq_out, 8).start()

    def gather_sent(r, carry):
        for number in range(15):
            gather_copy((0, 0), (0, 0), r, number, sibling).wait_send()
        return carry

    def sent():
        lax.fori_loop(0, PASSAGES_HERE, gather_sent, 0)
        for peer in peers:
            stat_copy(*peer).wait_send()
            q1_copy(*peer).wait_send()
            q2_copy(*peer).wait_send()
        for number in range(len(ITEMS) - 1):
            sibling_copy(number).wait_send()

    sibling_item(0)
    lax.fori_loop(2, 4, gradients, 0)
    for number in range(len(ITEMS)):
        if number == 14:
            query_end()
            sent()
            over_head.finish(EARLIER)
            over_psg.finish(EARLIER)
        psg_item(number)
        if number == 0:
            sibling_item(1)
        elif number + 2 < len(ITEMS):
            sibling_item(number + 2)
        head_item(number)
        if number == 0:
            sibling_item(2)
        if number == 2:
            query_terms()
        if number == 8:
            query_sums()

    sibling_copy(len(ITEMS) - 1).wait_send()
    over_head.finish(LAST)
    over_psg.finish(LAST)
    over_head.finish_y()
    over_psg.finish_y()
    for r in range(PASSAGES_HERE):
        out_copy(gm_own.at[pl.ds(r * B, B)], gm_out.at[pl.ds(r * B, B)], r).wait()
        out_copy(gw_own.at[r], gw_out.at[r], 4 + r).wait()
    out_copy(gq_full, gq_out, 8).wait()


def epilogue(gq_in, gm_in, gw_in, gq_out, gm_out, gwk_out, gwv_out, gq, gm, gw, gq_t, gw_t, sem):
    def copy(source, target, number):
        return pltpu.make_async_copy(source, target, sem.at[number])

    def gw_write(r):
        out = gwk_out if r < 2 else gwv_out
        return copy(gw_t.at[r], out.at[pl.ds(r % 2 * B, B)], 6 + r)

    reads = [copy(gw_in.at[r], gw.at[r], r) for r in range(4)]
    reads += [copy(gm_in, gm, 4), copy(gq_in, gq, 5)]
    writes = [gw_write(r) for r in range(4)]
    writes += [copy(gm, gm_out, 10), copy(gq_t, gq_out, 11)]
    for read in reads:
        read.start()
    for r in range(4):
        reads[r].wait()
        gw_t[r] = gw[r].T
        writes[r].start()
    reads[4].wait()
    writes[4].start()
    reads[5].wait()
    for question in range(2):
        turned = jnp.concatenate([gq[question * 4 + k] for k in range(4)], axis=0)
        gq_t[question * TQ : (question + 1) * TQ, :] = turned.astype(F32).T.astype(BF16)
    writes[5].start()
    for write in writes:
        write.wait()


def on_device(queries, memory, lengths, owner, w_key, w_value, grad_context):
    rows, width = memory.shape[0], w_key.shape[0]
    anywhere = pl.BlockSpec(memory_space=pl.ANY)
    dma = pltpu.SemaphoreType.DMA
    half = 2 * B
    outs = pl.pallas_call(
        kernel,
        out_shape=(
            jax.ShapeDtypeStruct((8, 2 * B // 8, TQ), BF16),
            jax.ShapeDtypeStruct((rows, B), BF16),
            jax.ShapeDtypeStruct((4, B, B), F32),
        ),
        in_specs=[anywhere] * 7,
        out_specs=[anywhere] * 3,
        scratch_shapes=[
            pltpu.SMEM((PASSAGES_HERE,), jnp.int32),
            pltpu.SMEM((PASSAGES_HERE,), jnp.int32),
            pltpu.VMEM((2 * TQ, B), BF16),
            pltpu.VMEM((2 * TQ, B), BF16),
            pltpu.VMEM((rows, B), BF16),
            pltpu.VMEM((4, B, B), F32),
            pltpu.VMEM((rows, width), BF16),
            pltpu.VMEM((width, 2 * B), BF16),
            pltpu.VMEM((2, PAIRS, B), BF16),
            pltpu.VMEM((2, PAIRS, B), BF16),
            pltpu.VMEM((2, B, PAIRS), BF16),
            pltpu.VMEM((2, B, PAIRS), BF16),
            pltpu.VMEM((rows, 2 * B), F32),
            pltpu.VMEM((PASSAGES_HERE, B, B), BF16),
            pltpu.VMEM((PASSAGES_HERE, LEN, PAIRS), F32),
            pltpu.VMEM((PASSAGES_HERE, LEN, PAIRS), F32),
            pltpu.VMEM((PASSAGES_HERE, 8, PAIRS), F32),
            pltpu.VMEM((8, PAIRS), F32),
            pltpu.VMEM((8, 8, PAIRS), F32),
            pltpu.VMEM((rows, 2 * B), BF16),
            pltpu.VMEM((2 * B, rows), BF16),
            pltpu.VMEM((PASSAGES_HERE, LEN, PAIRS), BF16),
            pltpu.VMEM((16, half, B), BF16),
            pltpu.VMEM((16, half, B), BF16),
            pltpu.VMEM((12, half, B), BF16),
            pltpu.VMEM((12, half, B), BF16),
            pltpu.VMEM((2, half, B), BF16),
            pltpu.VMEM((2, half, B), BF16),
            pltpu.VMEM((12, half, B), BF16),
            pltpu.VMEM((12, half, B), BF16),
            pltpu.VMEM((2, half, B), BF16),
            pltpu.VMEM((2, half, B), BF16),
            pltpu.VMEM((2 * B, TQ), F32),
            pltpu.VMEM((2 * B, TQ), BF16),
            pltpu.VMEM((8, 2 * B // 8, TQ), BF16),
            pltpu.VMEM((2 * B // 8, TQ), BF16),
            pltpu.VMEM((8, 2 * B // 8, TQ), BF16),
            dma, dma((32,)), dma((4,)), dma((9,)),
            dma((15, 4)), dma((16, 4)),
            dma((8,)), dma((8,)),
            dma((16,)), dma((16,)),
            dma((12, 2)), dma((12, 2)), dma((2,)), dma((2,)),
            dma((12, 2)), dma((12, 2)), dma((2,)), dma((2,)),
            dma((8,)), dma((8,)), dma((8,)), dma((8,)),
        ],
        compiler_params=pltpu.CompilerParams(
            collective_id=0, has_side_effects=True, vmem_limit_bytes=60 * 2**20
        ),
        name="whole",
    )(lengths, owner, queries, grad_context, memory, w_key, w_value)
    gq, gm, gwk, gwv = pl.pallas_call(
        epilogue,
        out_shape=(
            jax.ShapeDtypeStruct((2 * TQ, B), BF16),
            jax.ShapeDtypeStruct((rows, B), BF16),
            jax.ShapeDtypeStruct((half, B), F32),
            jax.ShapeDtypeStruct((half, B), F32),
        ),
        in_specs=[anywhere] * 3,
        out_specs=[anywhere] * 4,
        scratch_shapes=[
            pltpu.VMEM((8, 2 * B // 8, TQ), BF16),
            pltpu.VMEM((rows, B), BF16),
            pltpu.VMEM((4, B, B), F32),
            pltpu.VMEM((2 * TQ, B), BF16),
            pltpu.VMEM((4, B, B), F32),
            dma((12,)),
        ],
        name="turn",
    )(*outs)
    return gq, gm, gwk, gwv


def solution(mesh):
    in_specs = (
        P(None, "head"),
        P("psg", "head"),
        P("psg"),
        P("psg"),
        P(None, "head"),
        P(None, "head"),
        P(None, "head"),
    )
    out_specs = (P(None, "head"), P("psg", "head"), P("psg", "head"), P("psg", "head"))
    return jax.shard_map(
        on_device, mesh=mesh, in_specs=in_specs, out_specs=out_specs, check_vma=False
    )
```

```python
import jax
import jax.numpy as jnp
from jax import lax
from jax.experimental import pallas as pl
from jax.experimental.pallas import tpu as pltpu
from jax.sharding import PartitionSpec as P

HEAD_DIM = 64
LEN = 256
TQ = 128
HEADS_HERE = 4
PASSAGES_HERE = 4
B = 256
PAIRS = HEADS_HERE * TQ
MESH = pl.DeviceIdType.MESH
FILL = -1e30
F32 = jnp.float32
BF16 = jnp.bfloat16

PLACES = ((0, 0), (0, 1), (0, 3), (1, 0), (0, 2), (1, 2), (1, 1), (1, 3))
SLOT = {place: slot for slot, place in enumerate(PLACES)}


def is_equal(a, k):
    return 1 - ((a - k) * (a - k) + 48) // 49


def slot_of(dy, dz):
    code = dy * 4 + dz
    total = 0
    for (py, pz), slot in SLOT.items():
        total = total + slot * is_equal(code, py * 4 + pz)
    return total


def nt(a, b):
    return lax.dot_general(a, b, (((1,), (1,)), ((), ())), preferred_element_type=F32)


def nn(a, b):
    return jnp.dot(a, b, preferred_element_type=F32)


class Scatter:
    def __init__(self, pair_first, send, recv, ysend, yrecv, ssem, rsem, yssem, yrsem, following, before, partner):
        self.pair_first = pair_first
        self.send, self.recv, self.ysend, self.yrecv = send, recv, ysend, yrecv
        self.ssem, self.rsem, self.yssem, self.yrsem = ssem, rsem, yssem, yrsem
        self.following, self.before, self.partner = following, before, partner

    def half(self, ref, index, way):
        return ref.at[index, pl.ds(way * B, B)]

    def copy(self, index, way):
        return pltpu.make_async_remote_copy(
            src_ref=self.half(self.send, index, way),
            dst_ref=self.half(self.recv, index, way),
            send_sem=self.ssem.at[index, way],
            recv_sem=self.rsem.at[index, way],
            device_id=self.before if way else self.following,
            device_id_type=MESH,
        )

    def first_copy(self):
        return pltpu.make_async_remote_copy(
            src_ref=self.send.at[FIRST],
            dst_ref=self.recv.at[FIRST],
            send_sem=self.ssem.at[FIRST, 0],
            recv_sem=self.rsem.at[FIRST, 0],
            device_id=self.partner,
            device_id_type=MESH,
        )

    def ycopy(self, u, way):
        return pltpu.make_async_remote_copy(
            src_ref=self.half(self.ysend, u, way),
            dst_ref=self.half(self.yrecv, u, way),
            send_sem=self.yssem.at[u, way],
            recv_sem=self.yrsem.at[u, way],
            device_id=self.partner,
            device_id_type=MESH,
        )

    def arrived(self, index, way):
        return self.recv[index, way * B : (way + 1) * B, :].astype(F32)

    def item(self, kind, dy, u, own, store):
        first = (dy * 2 + u) * 3
        if kind == "D":
            mine = [own(0, way * 2 + u, way) for way in (0, 1)]
            for way in (0, 1):
                self.copy(first + 1, 1 - way).wait_recv()
                self.copy(first + 2, way).wait_recv()
                value = mine[way] + self.arrived(first + 2, way) + self.arrived(first + 1, 1 - way)
                if dy == 1:
                    self.ysend[u, way * B : (way + 1) * B, :] = value.astype(BF16)
                    self.ycopy(u, way).start()
                else:
                    self.ycopy(u, way).wait_recv()
                    value = value + self.yrecv[u, way * B : (way + 1) * B, :].astype(F32)
                    store(way * 2 + u, value)
            return
        index = first + "ABC".index(kind)
        if self.pair_first and index == FIRST:
            for way in (0, 1):
                dz, r = chunk_of(kind, u, way)
                self.send[index, way * B : (way + 1) * B, :] = own(dz, r, way).astype(BF16)
            self.first_copy().start()
            return
        if self.pair_first and index == 0:
            self.first_copy().wait_recv()
        for way in (0, 1):
            dz, r = chunk_of(kind, u, way)
            value = own(dz, r, way)
            if self.pair_first and index == 0:
                value = value + self.arrived(FIRST, way)
            if kind == "C" and not (self.pair_first and first == FIRST):
                self.copy(first, way).wait_recv()
                value = value + self.arrived(first, way)
            self.send[index, way * B : (way + 1) * B, :] = value.astype(BF16)
            self.copy(index, way).start()

    def finish(self, indices):
        for index in indices:
            if self.pair_first and index == FIRST:
                self.first_copy().wait_send()
                continue
            for way in (0, 1):
                self.copy(index, way).wait_send()

    def finish_y(self):
        for u in (0, 1):
            for way in (0, 1):
                self.ycopy(u, way).wait_send()


def chunk_of(kind, u, way):
    if kind == "A":
        return 2, way * 2 + u
    if kind == "B":
        return (3, u) if way else (1, 2 + u)
    if kind == "C":
        return (3, 2 + u) if way else (1, u)
    return 0, way * 2 + u


ITEMS = (
    ("A", 1, 0), ("B", 1, 0), ("C", 1, 0), ("A", 1, 1), ("B", 1, 1), ("D", 1, 0),
    ("C", 1, 1), ("A", 0, 0), ("B", 0, 0), ("D", 1, 1), ("C", 0, 0), ("A", 0, 1),
    ("B", 0, 1), ("C", 0, 1), ("D", 0, 0), ("D", 0, 1),
)
FIRST = 6
LAST = (4, 5)
EARLIER = tuple(index for index in range(12) if index not in LAST)


def kernel(
    len_in, own_in, q_in, c_in, mem_ref, wk_ref, wv_ref,
    gq_out, gm_out, gw_out,
    len_ref, own_ref, q_ref, c_ref, gm_own, gw_own, fm, w, qa, ca, qat, cat, acc, kt, e_ref, gp_ref, stat, sl, sall, g, gt, gs,
    sib_send, sib_recv, m_send, m_recv, my_send, my_recv, w_send, w_recv, wy_send, wy_recv,
    gq_acc, gq_send, gq_recv, gq_own, gq_full,
    mem_sem, w_sem, qc_sem, out_sem, ag_ssem, ag_rsem, st_ssem, st_rsem, sib_ssem, sib_rsem,
    m_ssem, m_rsem, my_ssem, my_rsem, w_ssem, w_rsem, wy_ssem, wy_rsem,
    q1_ssem, q1_rsem, q2_ssem, q2_rsem,
):
    p, h = lax.axis_index("psg"), lax.axis_index("head")
    yl, x = p // 4, p % 4
    yh, z, core = h // 8, (h // 2) % 4, h % 2

    def head_at(dy, dz, dc=0):
        return ((yh + dy) % 2) * 8 + ((z + dz) % 4) * 2 + (core + dc) % 2

    def psg_at(dy, dx):
        return ((yl + dy) % 2) * 4 + (x + dx) % 4

    def on_head(dy, dz, dc=0):
        return (p, head_at(dy, dz, dc))

    def on_psg(dy, dx):
        return (psg_at(dy, dx), h)

    up, down, across, sibling = on_head(0, 1), on_head(0, 3), on_head(1, 0), on_head(0, 0, 1)
    peers = [(k // 4, k % 4) for k in range(1, 8)]

    barrier = pltpu.get_barrier_semaphore()
    partners = [on_psg(*peer) for peer in reversed(peers)] + [across, up, down, sibling]
    for device in partners:
        pl.semaphore_signal(barrier, inc=1, device_id=device, device_id_type=MESH)

    mem_copy = pltpu.make_async_copy(mem_ref, fm.at[:, pl.ds(0, B)], mem_sem)
    mem_copy.start()
    q_copies = [
        pltpu.make_async_copy(q_in, q_ref, qc_sem.at[0]),
        pltpu.make_async_copy(c_in, c_ref, qc_sem.at[1]),
        pltpu.make_async_copy(len_in, len_ref, qc_sem.at[2]),
        pltpu.make_async_copy(own_in, own_ref, qc_sem.at[3]),
    ]
    for copy in q_copies:
        copy.start()
    pl.semaphore_wait(barrier, len(partners))

    def block(slot, dc, r):
        return fm.at[pl.ds(r * B, B), pl.ds((slot * 2 + dc) * B, B)]

    def gather_copy(source, target, r, number, device):
        return pltpu.make_async_remote_copy(
            src_ref=block(source[0], source[1], r),
            dst_ref=block(target[0], target[1], r),
            send_sem=ag_ssem.at[number, r],
            recv_sem=ag_rsem.at[target[0] * 2 + target[1], r],
            device_id=device,
            device_id_type=MESH,
        )

    def gathered(slot, dc, r):
        gather_copy((slot, dc), (slot, dc), r, 0, sibling).wait_recv()

    def to_sibling(slot, r):
        gather_copy((slot, 0), (slot, 1), r, 4 + slot, sibling).start()

    def own_copy(target, r, number, device):
        return pltpu.make_async_remote_copy(
            src_ref=mem_ref.at[pl.ds(r * B, B)],
            dst_ref=block(target, 0, r),
            send_sem=ag_ssem.at[number, r],
            recv_sem=ag_rsem.at[target * 2, r],
            device_id=device,
            device_id_type=MESH,
        )

    def own_along(k):
        own_copy(SLOT[0, 3], k, 0, up).start()
        own_copy(SLOT[0, 1], (k + 2) % 4, 1, down).start()

    own_along(0)
    own_along(1)
    for k in range(PASSAGES_HERE):
        own_copy(SLOT[1, 0], k % 2 * 2 + k // 2, 2, across).start()
    mem_copy.wait()
    for r in range(PASSAGES_HERE):
        to_sibling(0, r)
    w_copies = []
    for slot, (dy, dz) in enumerate(PLACES):
        for dc in (0, 1):
            rows = pl.ds(pl.multiple_of(head_at(dy, dz, dc) * B, B), B)
            into = pl.ds((slot * 2 + dc) * B, B)
            for part, ref in enumerate((wk_ref, wv_ref)):
                w_copies.append(
                    pltpu.make_async_copy(
                        ref.at[rows, :],
                        w.at[into, pl.ds(part * B, B)],
                        w_sem.at[(slot * 2 + dc) * 2 + part],
                    )
                )
                w_copies[-1].start()

    def opposite(r):
        gathered(SLOT[0, 2], 0, r)
        gather_copy((SLOT[0, 2], 0), (SLOT[1, 2], 0), r, 14, across).start()
        to_sibling(SLOT[0, 2], r)

    def partner(r):
        gathered(SLOT[1, 0], 0, r)
        gather_copy((SLOT[1, 0], 0), (SLOT[1, 3], 0), r, 12, up).start()
        gather_copy((SLOT[1, 0], 0), (SLOT[1, 1], 0), r, 13, down).start()
        to_sibling(SLOT[1, 0], r)

    for r in (0, 1):
        gathered(SLOT[0, 3], 0, r)
        gather_copy((SLOT[0, 3], 0), (SLOT[0, 2], 0), r, 3, up).start()
        gathered(SLOT[0, 1], 0, 2 + r)
        gather_copy((SLOT[0, 1], 0), (SLOT[0, 2], 0), 2 + r, 3, down).start()
        own_along(2 + r)
        to_sibling(SLOT[0, 3], r)
        to_sibling(SLOT[0, 1], 2 + r)
    for r in (0, 1):
        partner(r)
        partner(2 + r)
        opposite(r)
        opposite(2 + r)

    lane = lax.broadcasted_iota(jnp.int32, (TQ, B), 1) // HEAD_DIM
    row = lax.broadcasted_iota(jnp.int32, (B, TQ), 0) // HEAD_DIM
    for copy in q_copies:
        copy.wait()
    for source, plain, turned in ((q_ref, qa, qat), (c_ref, ca, cat)):
        for question in range(2):
            mine = source[question * TQ : (question + 1) * TQ, :].astype(F32)
            mine_t = mine.T
            for head in range(HEADS_HERE):
                at = slice(head * TQ, (head + 1) * TQ)
                plain[question, at, :] = jnp.where(lane == head, mine, 0.0).astype(BF16)
                turned[question, :, at] = jnp.where(row == head, mine_t, 0.0).astype(BF16)

    def rows_of(r):
        return pl.ds(pl.multiple_of(r * B, B), B)

    def passage(k):
        return k % 2 * 2 + k // 2

    for r in (0, 1):
        gathered(SLOT[0, 1], 0, r)
        to_sibling(SLOT[0, 1], r)
        gathered(SLOT[0, 3], 0, 2 + r)
        to_sibling(SLOT[0, 3], 2 + r)

    for copy in w_copies[:16]:
        copy.wait()

    def first_part(k, carry):
        r = passage(k)
        for slot in range(4):
            gathered(slot, 1, r)
        acc[rows_of(r), :] = nn(fm[rows_of(r), 0 : 8 * B], w[0 : 8 * B, :])
        return carry

    lax.fori_loop(0, PASSAGES_HERE, first_part, 0)

    for copy in w_copies[16:]:
        copy.wait()

    def second_part(k, carry):
        @pl.when(k < PASSAGES_HERE)
        def _():
            r = passage(k)
            for slot in (SLOT[1, 2], SLOT[1, 1], SLOT[1, 3]):
                gathered(slot, 0, r)
                to_sibling(slot, r)
            gathered(SLOT[0, 2], 1, r)
            gathered(SLOT[1, 2], 1, r)
            acc[rows_of(r), :] += nn(fm[rows_of(r), 8 * B : 12 * B], w[8 * B : 12 * B, :])

        @pl.when(k > 0)
        def _():
            attend(passage(k - 1))

        return carry

    def attend(r):
        for slot in (SLOT[1, 1], SLOT[1, 3]):
            gathered(slot, 1, r)
        both = acc[rows_of(r), :] + nn(fm[rows_of(r), 12 * B :], w[12 * B :, :])
        keys, values = both[:, :B], both[:, B:].astype(BF16)
        kt[r] = keys.T.astype(BF16)
        keys = keys.astype(BF16)
        question = own_ref[r]
        scores = nt(keys, qa[question])
        flows = nt(values, ca[question])
        alive = lax.broadcasted_iota(jnp.int32, (LEN, PAIRS), 0) < len_ref[r]
        masked = jnp.where(alive, scores, FILL)
        top = jnp.max(masked, axis=0, keepdims=True)
        shifted = jnp.where(alive, jnp.exp(masked - top), 0.0)
        e_ref[r] = shifted
        gp_ref[r] = flows
        stat[r, 0:1, :] = top
        stat[r, 1:2, :] = jnp.sum(shifted, axis=0, keepdims=True)
        stat[r, 2:3, :] = jnp.sum(shifted * flows, axis=0, keepdims=True)

    lax.fori_loop(0, PASSAGES_HERE + 1, second_part, 0)

    picks = []
    for r in range(PASSAGES_HERE):
        second = own_ref[r].astype(F32)
        picks.append((1.0 - second, second))
    for question in range(2):
        tops = [
            stat[r, 0:1, :] * picks[r][question] + FILL * (1.0 - picks[r][question])
            for r in range(PASSAGES_HERE)
        ]
        top = jnp.maximum(jnp.maximum(tops[0], tops[1]), jnp.maximum(tops[2], tops[3]))
        mass = jnp.zeros((1, PAIRS), F32)
        flow = jnp.zeros((1, PAIRS), F32)
        for r in range(PASSAGES_HERE):
            scale = jnp.exp(tops[r] - top) * picks[r][question]
            mass += stat[r, 1:2, :] * scale
            flow += stat[r, 2:3, :] * scale
        sl[question : question + 1, :] = top
        sl[2 + question : 3 + question, :] = mass
        sl[4 + question : 5 + question, :] = flow
    sl[6:8, :] = jnp.zeros((2, PAIRS), F32)

    def seen_by(dy, dx):
        return dy * 4 + (4 - dx) % 4

    def stat_copy(dy, dx):
        there = seen_by(dy, dx)
        return pltpu.make_async_remote_copy(
            src_ref=sl,
            dst_ref=sall.at[there],
            send_sem=st_ssem.at[dy * 4 + dx],
            recv_sem=st_rsem.at[there],
            device_id=on_psg(dy, dx),
            device_id_type=MESH,
        )

    for peer in reversed(peers):
        stat_copy(*peer).start()
    for peer in peers:
        stat_copy(*peer).wait_recv()
    sall[0] = sl[...]
    totals = []
    for question in range(2):
        tops = [sall[k, question : question + 1, :] for k in range(8)]
        top = tops[0]
        for other in tops[1:]:
            top = jnp.maximum(top, other)
        mass = jnp.zeros((1, PAIRS), F32)
        flow = jnp.zeros((1, PAIRS), F32)
        for k in range(8):
            scale = jnp.exp(tops[k] - top)
            mass += sall[k, 2 + question : 3 + question, :] * scale
            flow += sall[k, 4 + question : 5 + question, :] * scale
        totals.append((top, 1.0 / mass, flow / mass))
    for r in range(PASSAGES_HERE):
        top, inverse, shift = (
            totals[0][k] * picks[r][0] + totals[1][k] * picks[r][1] for k in range(3)
        )
        stat[r, 3:4, :] = jnp.exp(stat[r, 0:1, :] - top) * inverse
        stat[r, 4:5, :] = shift

    def gradients(k, carry):
        r = passage(k)
        question = own_ref[r]
        probs = e_ref[r] * stat[r, 3:4, :]
        grad = (probs * (gp_ref[r] - stat[r, 4:5, :])).astype(BF16)
        probs = probs.astype(BF16)
        gs[r] = grad
        g[rows_of(r), 0:B] = nn(grad, qa[question]).astype(BF16)
        g[rows_of(r), B : 2 * B] = nn(probs, ca[question]).astype(BF16)
        gt[0:B, rows_of(r)] = nt(qat[question], grad).astype(BF16)
        gt[B : 2 * B, rows_of(r)] = nt(cat[question], probs).astype(BF16)
        return carry

    lax.fori_loop(0, 2, gradients, 0)

    over_head = Scatter(
        False, m_send, m_recv, my_send, my_recv, m_ssem, m_rsem, my_ssem, my_rsem, up, down, across
    )
    over_psg = Scatter(
        True, w_send, w_recv, wy_send, wy_recv, w_ssem, w_rsem, wy_ssem, wy_rsem,
        on_psg(0, 1), on_psg(0, 3), on_psg(1, 0),
    )

    def out_copy(source, target, number):
        return pltpu.make_async_copy(source, target, out_sem.at[number])

    def part(slot, dc, r):
        at = (slot * 2 + dc) * B
        return nt(g[r * B : (r + 1) * B, :], w[at : at + B, :]).astype(BF16)

    def sibling_copy(number):
        return pltpu.make_async_remote_copy(
            src_ref=sib_send.at[number],
            dst_ref=sib_recv.at[number],
            send_sem=sib_ssem.at[number],
            recv_sem=sib_rsem.at[number],
            device_id=sibling,
            device_id_type=MESH,
        )

    def sibling_item(number):
        kind, dy, u = ITEMS[number]
        for way in (0, 1):
            dz, r = chunk_of(kind, u, way)
            sib_send[number, way * B : (way + 1) * B, :] = part(SLOT[dy, dz], 1, r)
        sibling_copy(number).start()

    def head_item(number):
        kind, dy, u = ITEMS[number]
        sibling_copy(number).wait_recv()

        def own(dz, r, way):
            other = sib_recv[number, way * B : (way + 1) * B, :].astype(F32)
            return part(SLOT[dy, dz], 0, r).astype(F32) + other

        def store(r, value):
            gm_own[r * B : (r + 1) * B, :] = value.astype(BF16)
            out_copy(gm_own.at[pl.ds(r * B, B)], gm_out.at[pl.ds(r * B, B)], r).start()

        over_head.item(kind, dy, u, own, store)

    def psg_item(number):
        kind, dy, u = ITEMS[number]

        def own(dx, r, way):
            kv, half = r // 2, r % 2
            slot = slot_of((yl + dy + 2 - yh) % 2, (x + dx + 4 - z) % 4)
            column = (slot * 2 + (half + 2 - core) % 2) * B
            return nn(gt[kv * B : (kv + 1) * B, :], fm[:, pl.ds(pl.multiple_of(column, B), B)])

        def store(r, value):
            gw_own[r] = value
            out_copy(gw_own.at[r], gw_out.at[r], 4 + r).start()

        over_psg.item(kind, dy, u, own, store)

    piece = 2 * B // 8

    def q1_copy(dy, dx):
        there = seen_by(dy, dx)
        start = pl.multiple_of(psg_at(dy, dx) * piece, piece)
        return pltpu.make_async_remote_copy(
            src_ref=gq_send.at[pl.ds(start, piece)],
            dst_ref=gq_recv.at[there],
            send_sem=q1_ssem.at[dy * 4 + dx],
            recv_sem=q1_rsem.at[there],
            device_id=on_psg(dy, dx),
            device_id_type=MESH,
        )

    def q2_copy(dy, dx):
        return pltpu.make_async_remote_copy(
            src_ref=gq_own,
            dst_ref=gq_full.at[p],
            send_sem=q2_ssem.at[dy * 4 + dx],
            recv_sem=q2_rsem.at[seen_by(dy, dx)],
            device_id=on_psg(dy, dx),
            device_id_type=MESH,
        )

    def q2_wait(dy, dx):
        pltpu.make_async_remote_copy(
            src_ref=gq_own,
            dst_ref=gq_full.at[psg_at(dy, dx)],
            send_sem=q2_ssem.at[dy * 4 + dx],
            recv_sem=q2_rsem.at[dy * 4 + dx],
            device_id=on_psg(dy, dx),
            device_id_type=MESH,
        ).wait_recv()

    def query_terms():
        gq_acc[...] = jnp.zeros((2 * B, TQ), F32)
        for r in range(PASSAGES_HERE):
            term = nn(kt[r], gs[r])
            for head in range(HEADS_HERE):
                at = slice(head * HEAD_DIM, (head + 1) * HEAD_DIM)
                mine = term[at, head * TQ : (head + 1) * TQ]
                gq_acc[at, :] += mine * picks[r][0]
                after = slice(B + head * HEAD_DIM, B + (head + 1) * HEAD_DIM)
                gq_acc[after, :] += mine * picks[r][1]
        gq_send[...] = gq_acc[...].astype(BF16)
        for peer in peers:
            q1_copy(*peer).start()

    def query_sums():
        total = gq_acc[pl.ds(pl.multiple_of(p * piece, piece), piece), :]
        for dy, dx in peers:
            there = dy * 4 + dx
            pltpu.make_async_remote_copy(
                src_ref=gq_recv.at[there],
                dst_ref=gq_recv.at[there],
                send_sem=q1_ssem.at[there],
                recv_sem=q1_rsem.at[there],
                device_id=on_psg(dy, dx),
                device_id_type=MESH,
            ).wait_recv()
            total = total + gq_recv[there].astype(F32)
        gq_own[...] = total.astype(BF16)
        for peer in peers:
            q2_copy(*peer).start()
        gq_full[p] = gq_own[...]

    def query_end():
        for peer in peers:
            q2_wait(*peer)
        out_copy(gq_full, gq_out, 8).start()

    def gather_sent(r, carry):
        for number in range(15):
            gather_copy((0, 0), (0, 0), r, number, sibling).wait_send()
        return carry

    def sent():
        lax.fori_loop(0, PASSAGES_HERE, gather_sent, 0)
        for peer in peers:
            stat_copy(*peer).wait_send()
            q1_copy(*peer).wait_send()
            q2_copy(*peer).wait_send()
        for number in range(len(ITEMS) - 1):
            sibling_copy(number).wait_send()

    sibling_item(0)
    lax.fori_loop(2, 4, gradients, 0)
    for number in range(len(ITEMS)):
        if number == 14:
            query_end()
            sent()
            over_head.finish(EARLIER)
            over_psg.finish(EARLIER)
        psg_item(number)
        if number == 0:
            sibling_item(1)
        elif number + 2 < len(ITEMS):
            sibling_item(number + 2)
        head_item(number)
        if number == 0:
            sibling_item(2)
        if number == 2:
            query_terms()
        if number == 8:
            query_sums()

    sibling_copy(len(ITEMS) - 1).wait_send()
    over_head.finish(LAST)
    over_psg.finish(LAST)
    over_head.finish_y()
    over_psg.finish_y()
    for r in range(PASSAGES_HERE):
        out_copy(gm_own.at[pl.ds(r * B, B)], gm_out.at[pl.ds(r * B, B)], r).wait()
        out_copy(gw_own.at[r], gw_out.at[r], 4 + r).wait()
    out_copy(gq_full, gq_out, 8).wait()


def epilogue(gq_in, gm_in, gw_in, gq_out, gm_out, gwk_out, gwv_out, gq, gm, gw, gq_t, gw_t, sem):
    def copy(source, target, number):
        return pltpu.make_async_copy(source, target, sem.at[number])

    def gw_write(r):
        out = gwk_out if r < 2 else gwv_out
        return copy(gw_t.at[r], out.at[pl.ds(r % 2 * B, B)], 6 + r)

    reads = [copy(gw_in.at[r], gw.at[r], r) for r in range(4)]
    reads += [copy(gm_in, gm, 4), copy(gq_in, gq, 5)]
    writes = [gw_write(r) for r in range(4)]
    writes += [copy(gm, gm_out, 10), copy(gq_t, gq_out, 11)]
    for read in reads:
        read.start()
    for r in range(4):
        reads[r].wait()
        gw_t[r] = gw[r].T
        writes[r].start()
    reads[4].wait()
    writes[4].start()
    reads[5].wait()
    for question in range(2):
        turned = jnp.concatenate([gq[question * 4 + k] for k in range(4)], axis=0)
        gq_t[question * TQ : (question + 1) * TQ, :] = turned.astype(F32).T.astype(BF16)
    writes[5].start()
    for write in writes:
        write.wait()


def on_device(queries, memory, lengths, owner, w_key, w_value, grad_context):
    rows, width = memory.shape[0], w_key.shape[0]
    anywhere = pl.BlockSpec(memory_space=pl.ANY)
    dma = pltpu.SemaphoreType.DMA
    half = 2 * B
    outs = pl.pallas_call(
        kernel,
        out_shape=(
            jax.ShapeDtypeStruct((8, 2 * B // 8, TQ), BF16),
            jax.ShapeDtypeStruct((rows, B), BF16),
            jax.ShapeDtypeStruct((4, B, B), F32),
        ),
        in_specs=[anywhere] * 7,
        out_specs=[anywhere] * 3,
        scratch_shapes=[
            pltpu.SMEM((PASSAGES_HERE,), jnp.int32),
            pltpu.SMEM((PASSAGES_HERE,), jnp.int32),
            pltpu.VMEM((2 * TQ, B), BF16),
            pltpu.VMEM((2 * TQ, B), BF16),
            pltpu.VMEM((rows, B), BF16),
            pltpu.VMEM((4, B, B), F32),
            pltpu.VMEM((rows, width), BF16),
            pltpu.VMEM((width, 2 * B), BF16),
            pltpu.VMEM((2, PAIRS, B), BF16),
            pltpu.VMEM((2, PAIRS, B), BF16),
            pltpu.VMEM((2, B, PAIRS), BF16),
            pltpu.VMEM((2, B, PAIRS), BF16),
            pltpu.VMEM((rows, 2 * B), F32),
            pltpu.VMEM((PASSAGES_HERE, B, B), BF16),
            pltpu.VMEM((PASSAGES_HERE, LEN, PAIRS), F32),
            pltpu.VMEM((PASSAGES_HERE, LEN, PAIRS), F32),
            pltpu.VMEM((PASSAGES_HERE, 8, PAIRS), F32),
            pltpu.VMEM((8, PAIRS), F32),
            pltpu.VMEM((8, 8, PAIRS), F32),
            pltpu.VMEM((rows, 2 * B), BF16),
            pltpu.VMEM((2 * B, rows), BF16),
            pltpu.VMEM((PASSAGES_HERE, LEN, PAIRS), BF16),
            pltpu.VMEM((16, half, B), BF16),
            pltpu.VMEM((16, half, B), BF16),
            pltpu.VMEM((12, half, B), BF16),
            pltpu.VMEM((12, half, B), BF16),
            pltpu.VMEM((2, half, B), BF16),
            pltpu.VMEM((2, half, B), BF16),
            pltpu.VMEM((12, half, B), BF16),
            pltpu.VMEM((12, half, B), BF16),
            pltpu.VMEM((2, half, B), BF16),
            pltpu.VMEM((2, half, B), BF16),
            pltpu.VMEM((2 * B, TQ), F32),
            pltpu.VMEM((2 * B, TQ), BF16),
            pltpu.VMEM((8, 2 * B // 8, TQ), BF16),
            pltpu.VMEM((2 * B // 8, TQ), BF16),
            pltpu.VMEM((8, 2 * B // 8, TQ), BF16),
            dma, dma((32,)), dma((4,)), dma((9,)),
            dma((15, 4)), dma((16, 4)),
            dma((8,)), dma((8,)),
            dma((16,)), dma((16,)),
            dma((12, 2)), dma((12, 2)), dma((2, 2)), dma((2, 2)),
            dma((12, 2)), dma((12, 2)), dma((2, 2)), dma((2, 2)),
            dma((8,)), dma((8,)), dma((8,)), dma((8,)),
        ],
        compiler_params=pltpu.CompilerParams(
            collective_id=0, has_side_effects=True, vmem_limit_bytes=60 * 2**20
        ),
        name="whole",
    )(lengths, owner, queries, grad_context, memory, w_key, w_value)
    gq, gm, gwk, gwv = pl.pallas_call(
        epilogue,
        out_shape=(
            jax.ShapeDtypeStruct((2 * TQ, B), BF16),
            jax.ShapeDtypeStruct((rows, B), BF16),
            jax.ShapeDtypeStruct((half, B), F32),
            jax.ShapeDtypeStruct((half, B), F32),
        ),
        in_specs=[anywhere] * 3,
        out_specs=[anywhere] * 4,
        scratch_shapes=[
            pltpu.VMEM((8, 2 * B // 8, TQ), BF16),
            pltpu.VMEM((rows, B), BF16),
            pltpu.VMEM((4, B, B), F32),
            pltpu.VMEM((2 * TQ, B), BF16),
            pltpu.VMEM((4, B, B), F32),
            dma((12,)),
        ],
        name="turn",
    )(*outs)
    return gq, gm, gwk, gwv


def solution(mesh):
    in_specs = (
        P(None, "head"),
        P("psg", "head"),
        P("psg"),
        P("psg"),
        P(None, "head"),
        P(None, "head"),
        P(None, "head"),
    )
    out_specs = (P(None, "head"), P("psg", "head"), P("psg", "head"), P("psg", "head"))
    return jax.shard_map(
        on_device, mesh=mesh, in_specs=in_specs, out_specs=out_specs, check_vma=False
    )
```
